256 devices in a mesh: trainer: 8 (over y_hi, x), table: 32 (over y_lo, z, core).
Axes of the slice: x: 4, y: 4 (y_hi: 2, y_lo: 2; y = y_hi * 2 + y_lo), z: 8, core: 2. Of those that a mesh axis runs over, the one named last changes fastest.
Arguments:
- slot_ids: int32 [65536, 32], P(('trainer', 'table')), may hold values from 0 to 1023, as said below
- labels: int32 [65536], P(('trainer', 'table')), may hold values 0 or 1
- cache_rows: float32 [262144, 256], P(('trainer', 'table')), may hold values from -3 to 3
- cache_accum: float32 [262144], P(('trainer', 'table')), may hold values from 0.01 to 1
- table_rows: float32 [262144, 256], P(('trainer', 'table')), may hold values from -3 to 3
- table_accum: float32 [262144], P(('trainer', 'table')), may hold values from 0.01 to 1
- miss_dest: int32 [16384, 2], P(('trainer', 'table')), may hold values from 0 to 1023, as said below
- evict_slot: int32 [16384], P(('trainer', 'table')), may hold values from 0 to 1023, as said below
- evict_dest: int32 [16384, 2], P(('trainer', 'table')), may hold values from 0 to 1023, as said below
- proj_u: bfloat16 [2048, 256], replicated, may hold values from -0.375 to 0.375
- proj_v: bfloat16 [2048, 256], replicated, may hold values from -0.125 to 0.125
- cross_bias: float32 [2048], replicated, may hold values from -3 to 3
- head: float32 [2048], replicated, may hold values from 0.002 to 0.05
Outputs:
- new_cache_rows: float32 [262144, 256], P(('trainer', 'table'))
- new_cache_accum: float32 [262144], P(('trainer', 'table'))
- new_table_rows: float32 [262144, 256], P(('trainer', 'table'))
- new_table_accum: float32 [262144], P(('trainer', 'table'))
- clipped_proj: float32 [2, 2048, 256], replicated
- clipped_vecs: float32 [2, 2048], replicated
- loss: float32 [], replicated
The draws below stay inside these ranges and needn't reach their ends.
Inputs may be any that keep to these rules, and one draw needn't show every extreme that they name: `slot_ids`: no sample names a slot that its device evicts. `evict_slot`: the 64 slots of one device are distinct. `evict_dest`: column 0 is an owner's index along table, column 1 a row of that owner. No owned row is named twice among the devices of one trainer index. One device names one owner at most 6 times; in every draw some owner is named 6 times by every device of its trainer index. `miss_dest`: column 0 is an owner's index along table, column 1 a row of that owner. One device names one owner at most 6 times; in every draw some owner is named 6 times by every device of its trainer index.
All inputs are finite; a program needn't handle non-finite values. No bound on the sum of `labels` on one device may be relied on, other than what follows from the above.
Results may differ from the reference program's by a relative error of at most 0.0024.
Values sent between devices are 32-bit elements; how exact they have to be, the bound alone decides.
No kernel may reach another device: no remote copies, remote signals or barrier semaphores. Data moves between devices by JAX's collectives and lax.ppermute only.
A program may use at most 64 MiB of HBM per device.

```python
import math
import jax
import jax.numpy as jnp
from jax import lax

E = 256
F = 8
P_SIZE = 4
R = 256
SAMP_DEV = 256
C = 1024
R_OWN = 1024
LIST = 64
D = 2048
CAP = 6
SAMPLES = 65536
N_TRAINER = 8
N_TABLE = 32


def slot_order(key):
    devices = N_TRAINER * N_TABLE
    keys = jax.random.split(key, devices)
    return jax.vmap(lambda single: jax.random.permutation(single, C))(keys).astype(jnp.int32)


def grouped_owners(key):
    devices = N_TRAINER * N_TABLE
    first_key, second_key, third_key = jax.random.split(key, 3)
    hottest = jax.random.randint(first_key, (N_TRAINER,), 0, N_TABLE).astype(jnp.int32)
    hot_owner = jnp.repeat(hottest, N_TABLE)
    spots = (N_TABLE - 1) * CAP
    chosen = jax.vmap(lambda single: jax.random.permutation(single, spots))(jax.random.split(second_key, devices))[:, :LIST - CAP].astype(jnp.int32)
    other = chosen // CAP
    owner_rest = other + (other >= hot_owner[:, None]).astype(jnp.int32)
    rank_rest = chosen % CAP
    owner_all = jnp.concatenate([jnp.broadcast_to(hot_owner[:, None], (devices, CAP)), owner_rest], axis=1)
    rank_all = jnp.concatenate([jnp.broadcast_to(jnp.arange(CAP, dtype=jnp.int32)[None, :], (devices, CAP)), rank_rest], axis=1)
    shuffle = jax.vmap(lambda single: jax.random.permutation(single, LIST))(jax.random.split(third_key, devices)).astype(jnp.int32)
    return (jnp.take_along_axis(owner_all, shuffle, axis=1), jnp.take_along_axis(rank_all, shuffle, axis=1))


def draw_evict_slot(key, part):
    orders = slot_order(key)
    return orders[:, :LIST].reshape(-1)


def draw_slot_ids(key, part):
    orders = slot_order(key)
    key = jax.random.fold_in(key, 17)
    devices = N_TRAINER * N_TABLE
    picks = jax.random.randint(key, (devices, SAMP_DEV * F * P_SIZE), LIST, C).astype(jnp.int32)
    slots = jnp.take_along_axis(orders, picks, axis=1)
    return slots.reshape(devices * SAMP_DEV, F * P_SIZE)


def draw_evict_dest(key, part):
    key = jax.random.fold_in(key, 11)
    devices = N_TRAINER * N_TABLE
    owner, rank = grouped_owners(key)
    device_ids = jnp.arange(devices, dtype=jnp.int32)
    sender = device_ids % N_TABLE
    group_base = device_ids // N_TABLE * N_TABLE
    row_orders = jax.vmap(lambda single: jax.random.permutation(single, R_OWN))(jax.random.split(jax.random.fold_in(key, 5), devices)).astype(jnp.int32)
    owner_device = group_base[:, None] + owner
    position = sender[:, None] * (R_OWN // N_TABLE) + rank
    local = row_orders[owner_device, position]
    return jnp.stack([owner, local], axis=-1).reshape(devices * LIST, 2)


def draw_miss_dest(key, part):
    key = jax.random.fold_in(key, 13)
    devices = N_TRAINER * N_TABLE
    owner, rank = grouped_owners(key)
    local = jax.random.randint(jax.random.fold_in(key, 6), (devices, LIST), 0, R_OWN).astype(jnp.int32)
    return jnp.stack([owner, local], axis=-1).reshape(devices * LIST, 2)


def plant(array, rng, smallest, high):
    extent = array.shape
    spot = [jax.random.randint(jax.random.fold_in(rng, axis), (), 0, extent[axis]) for axis in range(len(extent))]
    array = array.at[tuple(spot)].set(smallest)
    longest = extent.index(max(extent))
    spot[longest] = (spot[longest] + 1) % extent[longest]
    return array.at[tuple(spot)].set(high)


def level_of(key, dims, pieces, smallest, top_value):
    level, own = 1.0, jax.random.fold_in(key, 6)
    for axis_at, shards_of in pieces:
        heights = jnp.exp(jax.random.uniform(jax.random.fold_in(own, axis_at), (shards_of,), jnp.float32, smallest / len(pieces), top_value / len(pieces)))
        level = level * jnp.repeat(heights, dims[axis_at] // shards_of).reshape([-1 if axis == axis_at else 1 for axis in range(len(dims))])
    return level


def gaussian(stream_key, shape, deviation, reach, shards=(), kind=jnp.bfloat16):
    values = jax.random.normal(stream_key, shape, jnp.float32) * deviation
    if len(shards) > 0:
        values = level_of(stream_key, shape, shards, -0.22, 0.18) * values
    return jnp.clip(values, min=-reach, max=reach).astype(kind)


def setup_inputs(seed: int = 0) -> dict:
    seeds = jax.random.split(jax.random.key(seed), 14)
    return {
        "slot_ids": draw_slot_ids(jax.random.fold_in(seeds[13], 71), 0),
        "labels": plant((jax.random.randint(seeds[1], (SAMPLES,), 0, 4) < 1).astype(jnp.int32), jax.random.fold_in(seeds[1], 1), 0, 1),
        "cache_rows": gaussian(seeds[2], (N_TRAINER * N_TABLE * C, E), 0.5, 3.0, ((0, 256),), jnp.float32),
        "cache_accum": jnp.clip(jnp.exp(math.log(1.0) - 4.6051702 * jax.random.uniform(seeds[3], (N_TRAINER * N_TABLE * C,), jnp.float32) ** level_of(seeds[3], (N_TRAINER * N_TABLE * C,), ((0, 256),), -0.2, 0.2)), 0.01, 1.0),
        "table_rows": gaussian(seeds[4], (N_TRAINER * N_TABLE * R_OWN, E), 0.5, 3.0, ((0, 256),), jnp.float32),
        "table_accum": jnp.clip(jnp.exp(math.log(1.0) - 4.6051702 * jax.random.uniform(seeds[5], (N_TRAINER * N_TABLE * R_OWN,), jnp.float32) ** level_of(seeds[5], (N_TRAINER * N_TABLE * R_OWN,), ((0, 256),), -0.2, 0.2)), 0.01, 1.0),
        "miss_dest": draw_miss_dest(jax.random.fold_in(seeds[13], 71), 0),
        "evict_slot": draw_evict_slot(jax.random.fold_in(seeds[13], 71), 0),
        "evict_dest": draw_evict_dest(jax.random.fold_in(seeds[13], 71), 0),
        "proj_u": gaussian(seeds[9], (D, R), R ** -0.5, 0.375),
        "proj_v": gaussian(seeds[10], (D, R), D ** -0.5, 0.125),
        "cross_bias": gaussian(seeds[11], (D,), 0.5, 3.0, (), jnp.float32),
        "head": jnp.clip(jnp.exp(jax.random.uniform(seeds[12], (D,), jnp.float32, math.log(0.002), math.log(0.05))), 0.002, 0.05),
    }


EPS = 1e-06
ETA = 0.05

def normalize(grad, axes):
    return grad * lax.rsqrt(lax.optimization_barrier(jnp.mean(grad * grad, axis=axes, keepdims=True)) + EPS)

def dense_pass(slots, marks, cache, accum, fetched, fetched_acc, evicted, proj_u, proj_v, cross_bias, head):
    count = slots.shape[0]
    gathered = cache[slots].reshape(count, F, P_SIZE, E)
    pooled = lax.optimization_barrier(jnp.sum(gathered, axis=2)).reshape(count, F * E).astype(jnp.bfloat16)
    latent = jnp.dot(pooled, proj_v, preferred_element_type=jnp.float32).astype(jnp.bfloat16)
    shifted = jnp.dot(latent, proj_u.T, preferred_element_type=jnp.float32) + cross_bias
    pooled_f = pooled.astype(jnp.float32)
    crossed = pooled_f * shifted + pooled_f
    logit = jnp.dot(crossed, head, precision=lax.Precision.HIGHEST)
    target = marks.astype(jnp.float32)
    objective = jnp.sum(jax.nn.softplus(logit) - target * logit)
    dlogit = jax.nn.sigmoid(logit) - target
    dcross = dlogit[:, None] * head[None, :]
    dhead = jnp.dot(dlogit, crossed, precision=lax.Precision.HIGHEST)
    dlift_full = dcross * pooled_f
    dbias = lax.optimization_barrier(jnp.sum(dlift_full, axis=0))
    dlift = dlift_full.astype(jnp.bfloat16)
    grad_u = jnp.dot(dlift.T, latent, preferred_element_type=jnp.float32)
    dlatent = jnp.dot(dlift, proj_u, preferred_element_type=jnp.float32).astype(jnp.bfloat16)
    grad_v = jnp.dot(pooled.T, dlatent, preferred_element_type=jnp.float32)
    dpooled = (dcross * (shifted + 1.0) + jnp.dot(dlatent, proj_v.T, preferred_element_type=jnp.float32)).astype(jnp.bfloat16)
    spread = jnp.broadcast_to(dpooled.reshape(count, F, 1, E), (count, F, P_SIZE, E)).astype(jnp.float32).reshape(count * F * P_SIZE, E)
    row_grad = jnp.zeros((C, E), jnp.float32).at[slots.reshape(-1)].add(spread)
    accum_new = accum + lax.optimization_barrier(jnp.mean(row_grad * row_grad, axis=1))
    rows_new = cache - ETA * row_grad * lax.rsqrt(accum_new)[:, None]
    rows_new = rows_new.at[evicted].set(fetched)
    accum_new = accum_new.at[evicted].set(fetched_acc)
    return (jnp.stack([grad_u, grad_v]), jnp.stack([dbias, dhead]), objective, rows_new, accum_new)

def reference(slot_ids, labels, cache_rows, cache_accum, table_rows, table_accum, miss_dest, evict_slot, evict_dest, proj_u, proj_v, cross_bias, head):
    devices = N_TRAINER * N_TABLE
    entry = jnp.arange(devices * LIST, dtype=jnp.int32)
    device_of = entry // LIST
    group_base = device_of // N_TABLE * N_TABLE
    source = device_of * C + evict_slot
    target = (group_base + evict_dest[:, 0]) * R_OWN + evict_dest[:, 1]
    new_table_rows = table_rows.at[target].set(cache_rows[source])
    new_table_accum = table_accum.at[target].set(cache_accum[source])
    wanted = (group_base + miss_dest[:, 0]) * R_OWN + miss_dest[:, 1]
    got_rows = new_table_rows[wanted].reshape(devices, LIST, E)
    got_accum = new_table_accum[wanted].reshape(devices, LIST)

    def one_device(carry, blocks):
        slots, marks, cache, accum, fetched, fetched_acc, evicted = blocks
        grad_uv, grad_vecs, objective, rows_new, accum_new = dense_pass(slots, marks, cache, accum, fetched, fetched_acc, evicted, proj_u, proj_v, cross_bias, head)
        return ((carry[0] + grad_uv, carry[1] + grad_vecs, carry[2] + objective), (rows_new, accum_new))
    start = (jnp.zeros((2, D, R), jnp.float32), jnp.zeros((2, D), jnp.float32), jnp.zeros((), jnp.float32))
    blocks = (slot_ids.reshape(devices, SAMP_DEV, F * P_SIZE), labels.reshape(devices, SAMP_DEV), cache_rows.reshape(devices, C, E), cache_accum.reshape(devices, C), got_rows, got_accum, evict_slot.reshape(devices, LIST))
    totals, outputs = lax.scan(one_device, start, blocks)
    new_cache_rows = outputs[0].reshape(devices * C, E)
    new_cache_accum = outputs[1].reshape(devices * C)
    clipped_proj = normalize(totals[0], (1, 2))
    clipped_vecs = normalize(totals[1], (1,))
    loss = totals[2] / SAMPLES
    return (new_cache_rows, new_cache_accum, new_table_rows, new_table_accum, clipped_proj, clipped_vecs, loss)
```

```python
import jax
import jax.numpy as jnp
from jax import lax
from jax.sharding import PartitionSpec as P

EPS = 1e-06
ETA = 0.05
AXES = ("trainer", "table")


def device_at(y, x, z, core):
    return (((y // 2 * 4 + x) * 2 + y % 2) * 8 + z % 8) * 2 + core


def first_groups():
    groups = []
    for y in range(4):
        for pair in range(4):
            groups.append([device_at(y, x, 2 * pair + b, 0) for x in range(4) for b in range(2)])
    for x in range(4):
        for pair in range(4):
            groups.append([device_at(y, x, 2 * pair + 1 + b, 1) for y in range(4) for b in range(2)])
    return groups


def second_groups():
    groups = []
    for x in range(4):
        for b in range(2):
            groups.append([device_at(y, x, 2 * k + b, 0) for y in range(4) for k in range(4)])
    for y in range(4):
        for b in range(2):
            groups.append([device_at(y, x, 2 * k + b, 1) for x in range(4) for k in range(4)])
    return groups


def swap_cores(value):
    return lax.ppermute(value, AXES, [(i, i ^ 1) for i in range(256)])


def exchange(value, groups):
    return lax.all_to_all(
        value, AXES, split_axis=0, concat_axis=0, tiled=True, axis_index_groups=groups
    )


def ranks(owner):
    listed = owner.shape[0]
    order = jnp.arange(listed, dtype=jnp.int32)
    earlier = (owner[:, None] == owner[None, :]) & (order[None, :] < order[:, None])
    return jnp.sum(earlier.astype(jnp.int32), axis=1)


def placed_at(place, values, cells):
    hit = place[None, :] == jnp.arange(cells, dtype=jnp.int32)[:, None]
    return jnp.sum(jnp.where(hit, values[None, :], 0), axis=1)


def split3(value):
    high = lax.reduce_precision(value, 8, 7)
    rest = value - high
    mid = lax.reduce_precision(rest, 8, 7)
    return [part.astype(jnp.bfloat16) for part in (high, mid, rest - mid)]


def meta_row(columns, width):
    block = jnp.concatenate(columns, axis=1)
    return jnp.pad(block, ((0, 0), (0, width - block.shape[1])))[:, None, :]


def shards(
    slot_ids,
    labels,
    cache_rows,
    cache_accum,
    table_rows,
    table_accum,
    miss_dest,
    evict_slot,
    evict_dest,
    proj_u,
    proj_v,
    cross_bias,
    head,
):
    owners = 32
    per = 8
    cap = 6
    width = cache_rows.shape[1]
    owned = table_rows.shape[0]
    cells = cache_rows.shape[0]
    spots = owners * per
    core = lax.axis_index("table") % 2

    out_place = evict_dest[:, 0] * per + ranks(evict_dest[:, 0])
    in_place = miss_dest[:, 0] * per + ranks(miss_dest[:, 0])
    source = placed_at(out_place, evict_slot, spots)
    leave_id = placed_at(out_place, evict_dest[:, 1] + 1, spots) - 1
    ask_id = placed_at(in_place, miss_dest[:, 1], spots)
    rows_out = jnp.take(cache_rows, source, axis=0, mode="clip").reshape(owners, per, width)
    accum_out = jnp.take(cache_accum, source, mode="clip").reshape(owners, per)
    meta = meta_row(
        [
            accum_out,
            leave_id.reshape(owners, per).astype(jnp.float32),
            ask_id.reshape(owners, per).astype(jnp.float32),
        ],
        width,
    )
    is_meta = (jnp.arange(per) == per - 1)[None, :, None]
    sent = jnp.where(is_meta, meta, rows_out)
    got = lax.all_to_all(sent, "table", split_axis=0, concat_axis=0, tiled=True)
    got_meta = got[:, per - 1, :]
    got_id = got_meta[:, per : per + cap].astype(jnp.int32)
    got_ask = got_meta[:, 2 * per : 2 * per + cap].astype(jnp.int32)
    flat = jnp.where(got_id < 0, owned, got_id).reshape(-1)
    table_new = table_rows.at[flat].set(got[:, :cap, :].reshape(-1, width), mode="drop")
    accum_table = table_accum.at[flat].set(got_meta[:, :cap].reshape(-1), mode="drop")

    asked = jnp.pad(got_ask, ((0, 0), (0, per - cap)))
    reply_rows = jnp.take(table_new, asked, axis=0, mode="clip")
    reply_accum = jnp.take(accum_table, asked, mode="clip")
    reply = jnp.where(is_meta, meta_row([reply_accum], width), reply_rows)
    back = lax.all_to_all(reply, "table", split_axis=0, concat_axis=0, tiled=True)
    fetched_rows = jnp.take(back.reshape(spots, width), in_place, axis=0, mode="clip")
    fetched_accum = jnp.take(back[:, per - 1, :per].reshape(-1), in_place, mode="clip")

    count = slot_ids.shape[0]
    feats = proj_u.shape[0] // width
    looks = slot_ids.shape[1] // feats
    slot_range = jnp.arange(cells, dtype=jnp.int32)
    parts = jnp.concatenate(split3(cache_rows), axis=1)
    pieces = []
    counted = []
    for feature in range(feats):
        counts = jnp.zeros((count, cells), jnp.bfloat16)
        for lookup in range(looks):
            column = slot_ids[:, feature * looks + lookup]
            counts = counts + (column[:, None] == slot_range[None, :]).astype(jnp.bfloat16)
        counted.append(counts)
        summed = jnp.dot(counts, parts, preferred_element_type=jnp.float32)
        pieces.append(
            (summed[:, 2 * width :] + summed[:, width : 2 * width] + summed[:, :width]).astype(
                jnp.bfloat16
            )
        )
    pooled = jnp.concatenate(pieces, axis=1)
    latent = jnp.dot(pooled, proj_v, preferred_element_type=jnp.float32).astype(jnp.bfloat16)
    shifted = jnp.dot(latent, proj_u.T, preferred_element_type=jnp.float32) + cross_bias
    pooled_f = pooled.astype(jnp.float32)
    crossed = pooled_f * shifted + pooled_f
    logit = jnp.sum(crossed * head, axis=1)
    target = labels.astype(jnp.float32)
    objective = jnp.sum(jax.nn.softplus(logit) - target * logit)
    dlogit = jax.nn.sigmoid(logit) - target
    dcross = dlogit[:, None] * head[None, :]
    dhead = jnp.sum(dlogit[:, None] * crossed, axis=0)
    dlift_full = dcross * pooled_f
    dbias = jnp.sum(dlift_full, axis=0)
    dlift = dlift_full.astype(jnp.bfloat16)
    grad_u = lax.dot_general(
        dlift, latent, (((0,), (0,)), ((), ())), preferred_element_type=jnp.float32
    )
    dlatent = jnp.dot(dlift, proj_u, preferred_element_type=jnp.float32).astype(jnp.bfloat16)
    grad_v = lax.dot_general(
        pooled, dlatent, (((0,), (0,)), ((), ())), preferred_element_type=jnp.float32
    )
    dpooled = (
        dcross * (shifted + 1.0) + jnp.dot(dlatent, proj_v.T, preferred_element_type=jnp.float32)
    ).astype(jnp.bfloat16)

    blocks = 8
    depth = grad_u.shape[0] // blocks
    loss_row = jnp.pad(objective[None, None, None], ((0, 0), (0, 0), (0, width - 1)))
    loss_row = jnp.broadcast_to(loss_row, (blocks, 1, width))
    blank = jnp.zeros((blocks, 6, width), jnp.float32)

    def bundle(grad, vector):
        extra = jnp.concatenate([vector.reshape(blocks, 1, width), loss_row, blank], axis=1)
        return jnp.concatenate([grad.reshape(blocks, depth, width), extra], axis=1)

    with_u = bundle(grad_u, dbias)
    with_v = bundle(grad_v, dhead)
    mine = core == 0
    held = jnp.where(mine, with_u, with_v) + swap_cores(jnp.where(mine, with_v, with_u))
    held = jnp.sum(exchange(held, first_groups()), axis=0)
    fine = depth // 16
    pieces16 = jnp.concatenate(
        [
            held[:depth].reshape(16, fine, width),
            jnp.broadcast_to(held[None, depth:], (16, 8, width)),
        ],
        axis=1,
    )
    summed16 = jnp.sum(exchange(pieces16, second_groups()), axis=0)
    extras = summed16[fine:]
    spread = jnp.broadcast_to(summed16[None, :fine], (16, fine, width))
    whole = exchange(spread, second_groups()).reshape(depth, width)
    whole = jnp.concatenate([whole, extras], axis=0)
    whole = exchange(jnp.broadcast_to(whole[None], (blocks, depth + 8, width)), first_groups())
    other = swap_cores(whole)
    sum_u = jnp.where(mine, whole, other)
    sum_v = jnp.where(mine, other, whole)

    def main_part(value):
        return value[:, :depth].reshape(1, blocks * depth, width)

    def vector_part(value):
        return value[:, depth].reshape(1, blocks * width)

    proj_sums = jnp.concatenate([main_part(sum_u), main_part(sum_v)], axis=0)
    vec_sums = jnp.concatenate([vector_part(sum_u), vector_part(sum_v)], axis=0)
    clipped_proj = proj_sums * lax.rsqrt(
        jnp.mean(proj_sums * proj_sums, axis=(1, 2), keepdims=True) + EPS
    )
    clipped_vecs = vec_sums * lax.rsqrt(jnp.mean(vec_sums * vec_sums, axis=1, keepdims=True) + EPS)
    loss = sum_v[0, depth + 1, 0] / (count * 256)

    row_grad = jnp.zeros((cells, width), jnp.float32)
    for feature in range(feats):
        block = dpooled[:, feature * width : (feature + 1) * width]
        row_grad = row_grad + lax.dot_general(
            counted[feature], block, (((0,), (0,)), ((), ())), preferred_element_type=jnp.float32
        )
    accum_new = cache_accum + jnp.mean(row_grad * row_grad, axis=1)
    rows_new = cache_rows - ETA * row_grad * lax.rsqrt(accum_new)[:, None]
    rows_new = rows_new.at[evict_slot].set(fetched_rows)
    accum_new = accum_new.at[evict_slot].set(fetched_accum)
    return (rows_new, accum_new, table_new, accum_table, clipped_proj, clipped_vecs, loss)


def solution(mesh):
    split = P(AXES)
    rows = P(AXES, None)
    return jax.shard_map(
        shards,
        mesh=mesh,
        in_specs=(
            rows,
            split,
            rows,
            split,
            rows,
            split,
            rows,
            split,
            rows,
            P(),
            P(),
            P(),
            P(),
        ),
        out_specs=(rows, split, rows, split, P(), P(), P()),
        check_vma=False,
    )
```

```python
import jax
import jax.numpy as jnp
from jax import lax
from jax.sharding import PartitionSpec as P

EPS = 1e-06
ETA = 0.05
AXES = ("trainer", "table")


def device_at(y, x, z, core):
    return (((y // 2 * 4 + x) * 2 + y % 2) * 8 + z % 8) * 2 + core


def first_groups():
    groups = []
    for y in range(4):
        for pair in range(4):
            groups.append([device_at(y, x, 2 * pair + b, 0) for x in range(4) for b in range(2)])
    for x in range(4):
        for pair in range(4):
            groups.append([device_at(y, x, 2 * pair + 1 + b, 1) for y in range(4) for b in range(2)])
    return groups


def second_groups():
    groups = []
    for x in range(4):
        for b in range(2):
            groups.append([device_at(y, x, 2 * k + b, 0) for y in range(4) for k in range(4)])
    for y in range(4):
        for b in range(2):
            groups.append([device_at(y, x, 2 * k + b, 1) for x in range(4) for k in range(4)])
    return groups


def swap_cores(value):
    return lax.ppermute(value, AXES, [(i, i ^ 1) for i in range(256)])


def exchange(value, groups):
    return lax.all_to_all(
        value, AXES, split_axis=0, concat_axis=0, tiled=True, axis_index_groups=groups
    )


def ranks(owner):
    listed = owner.shape[0]
    order = jnp.arange(listed, dtype=jnp.int32)
    earlier = (owner[:, None] == owner[None, :]) & (order[None, :] < order[:, None])
    return jnp.sum(earlier.astype(jnp.int32), axis=1)


def placed_at(place, values, cells):
    hit = place[None, :] == jnp.arange(cells, dtype=jnp.int32)[:, None]
    return jnp.sum(jnp.where(hit, values[None, :], 0), axis=1)


def split3(value):
    high = lax.reduce_precision(value, 8, 7)
    rest = value - high
    mid = lax.reduce_precision(rest, 8, 7)
    return [part.astype(jnp.bfloat16) for part in (high, mid, rest - mid)]


def meta_row(columns, width):
    block = jnp.concatenate(columns, axis=1)
    return jnp.pad(block, ((0, 0), (0, width - block.shape[1])))[:, None, :]


def picked(values, index):
    hit = index[:, None] == jnp.arange(values.shape[0], dtype=jnp.int32)[None, :]
    return jnp.sum(jnp.where(hit, values[None, :], 0.0), axis=1)


def cross(value, bit):
    split = value.reshape(value.shape[0] // (2 * bit), 2, bit, *value.shape[1:])
    there = [(i, i ^ bit) for i in range(256)]
    came = lax.ppermute(split[:, 1], AXES, there)
    return jnp.stack([split[:, 0], came], axis=1).reshape(value.shape)


def shards(
    slot_ids,
    labels,
    cache_rows,
    cache_accum,
    table_rows,
    table_accum,
    miss_dest,
    evict_slot,
    evict_dest,
    proj_u,
    proj_v,
    cross_bias,
    head,
):
    owners = 32
    per = 8
    cap = 6
    width = cache_rows.shape[1]
    owned = table_rows.shape[0]
    cells = cache_rows.shape[0]
    spots = owners * per
    core = lax.axis_index("table") % 2

    me = lax.axis_index("table")
    out_place = (evict_dest[:, 0] ^ me) * per + ranks(evict_dest[:, 0])
    in_place = (miss_dest[:, 0] ^ me) * per + ranks(miss_dest[:, 0])
    source = placed_at(out_place, evict_slot, spots)
    leave_id = placed_at(out_place, evict_dest[:, 1] + 1, spots) - 1
    ask_id = placed_at(in_place, miss_dest[:, 1], spots)
    rows_out = jnp.take(cache_rows, source, axis=0, mode="clip").reshape(owners, per, width)
    accum_out = picked(cache_accum, source).reshape(owners, per)
    meta = meta_row(
        [
            accum_out,
            leave_id.reshape(owners, per).astype(jnp.float32),
            ask_id.reshape(owners, per).astype(jnp.float32),
        ],
        width,
    )
    is_meta = (jnp.arange(per) == per - 1)[None, :, None]
    sent = jnp.where(is_meta, meta, rows_out)

    count = slot_ids.shape[0]
    feats = proj_u.shape[0] // width
    looks = slot_ids.shape[1] // feats
    slot_range = jnp.arange(cells, dtype=jnp.int32)
    parts = jnp.concatenate(split3(cache_rows), axis=1)
    pieces = []
    counted = []
    for feature in range(feats):
        counts = jnp.zeros((count, cells), jnp.bfloat16)
        for lookup in range(looks):
            column = slot_ids[:, feature * looks + lookup]
            counts = counts + (column[:, None] == slot_range[None, :]).astype(jnp.bfloat16)
        counted.append(counts)
        summed = jnp.dot(counts, parts, preferred_element_type=jnp.float32)
        pieces.append(
            (summed[:, 2 * width :] + summed[:, width : 2 * width] + summed[:, :width]).astype(
                jnp.bfloat16
            )
        )
    pooled = jnp.concatenate(pieces, axis=1)
    latent = jnp.dot(pooled, proj_v, preferred_element_type=jnp.float32).astype(jnp.bfloat16)
    shifted = jnp.dot(latent, proj_u.T, preferred_element_type=jnp.float32) + cross_bias
    pooled_f = pooled.astype(jnp.float32)
    crossed = pooled_f * shifted + pooled_f
    logit = jnp.sum(crossed * head, axis=1)
    target = labels.astype(jnp.float32)
    objective = jnp.sum(jax.nn.softplus(logit) - target * logit)
    dlogit = jax.nn.sigmoid(logit) - target
    dcross = dlogit[:, None] * head[None, :]
    dhead = jnp.sum(dlogit[:, None] * crossed, axis=0)
    dlift_full = dcross * pooled_f
    dbias = jnp.sum(dlift_full, axis=0)
    dlift = dlift_full.astype(jnp.bfloat16)
    grad_u = lax.dot_general(
        dlift, latent, (((0,), (0,)), ((), ())), preferred_element_type=jnp.float32
    )
    dlatent = jnp.dot(dlift, proj_u, preferred_element_type=jnp.float32).astype(jnp.bfloat16)
    grad_v = lax.dot_general(
        pooled, dlatent, (((0,), (0,)), ((), ())), preferred_element_type=jnp.float32
    )
    dpooled = (
        dcross * (shifted + 1.0) + jnp.dot(dlatent, proj_v.T, preferred_element_type=jnp.float32)
    ).astype(jnp.bfloat16)

    blocks = 8
    depth = grad_u.shape[0] // blocks
    loss_row = jnp.pad(objective[None, None, None], ((0, 0), (0, 0), (0, width - 1)))
    loss_row = jnp.broadcast_to(loss_row, (blocks, 1, width))
    blank = jnp.zeros((blocks, 6, width), jnp.float32)

    def bundle(grad, vector):
        extra = jnp.concatenate([vector.reshape(blocks, 1, width), loss_row, blank], axis=1)
        return jnp.concatenate([grad.reshape(blocks, depth, width), extra], axis=1)

    with_u = bundle(grad_u, dbias)
    with_v = bundle(grad_v, dhead)
    mine = core == 0
    held = jnp.where(mine, with_u, with_v) + swap_cores(jnp.where(mine, with_v, with_u))
    held, sent = lax.optimization_barrier((held, sent))
    held = exchange(held, first_groups())
    got = cross(cross(cross(sent, 1), 16), 2)
    held, got = lax.optimization_barrier((held, got))
    held = jnp.sum(held, axis=0)
    fine = depth // 16
    pieces16 = jnp.concatenate(
        [
            held[:depth].reshape(16, fine, width),
            jnp.broadcast_to(held[None, depth:], (16, 8, width)),
        ],
        axis=1,
    )
    held = exchange(pieces16, second_groups())
    got = cross(cross(got, 4), 8)
    got_meta = got[:, per - 1, :]
    got_id = got_meta[:, per : per + cap].astype(jnp.int32)
    asked = got_meta[:, 2 * per : 3 * per].astype(jnp.int32).reshape(-1)
    flat = got_id.reshape(-1)
    table_new = table_rows.at[jnp.where(flat < 0, owned, flat)].set(
        got[:, :cap, :].reshape(-1, width), mode="drop"
    )
    stored = flat[:, None] == jnp.arange(owned, dtype=jnp.int32)[None, :]
    stored_sum = jnp.sum(jnp.where(stored, got_meta[:, :cap].reshape(-1)[:, None], 0.0), axis=0)
    accum_table = jnp.where(jnp.any(stored, axis=0), stored_sum, table_accum)
    reply_rows = jnp.take(table_new, asked, axis=0, mode="clip").reshape(owners, per, width)
    reply_accum = picked(accum_table, asked).reshape(owners, per)
    reply = jnp.where(is_meta, meta_row([reply_accum], width), reply_rows)
    held, reply = lax.optimization_barrier((held, reply))
    summed16 = jnp.sum(held, axis=0)
    extras = summed16[fine:]
    spread = jnp.broadcast_to(summed16[None, :fine], (16, fine, width))

    held = exchange(spread, second_groups())
    back = cross(cross(reply, 1), 16)
    held, back = lax.optimization_barrier((held, back))
    whole = jnp.concatenate([held.reshape(depth, width), extras], axis=0)
    whole = exchange(jnp.broadcast_to(whole[None], (blocks, depth + 8, width)), first_groups())
    back = cross(cross(cross(back, 2), 4), 8)
    whole, back = lax.optimization_barrier((whole, back))
    fetched_rows = jnp.take(back.reshape(spots, width), in_place, axis=0, mode="clip")
    fetched_accum = picked(back[:, per - 1, :per].reshape(-1), in_place)
    other = swap_cores(whole)
    sum_u = jnp.where(mine, whole, other)
    sum_v = jnp.where(mine, other, whole)

    def main_part(value):
        return value[:, :depth].reshape(1, blocks * depth, width)

    def vector_part(value):
        return value[:, depth].reshape(1, blocks * width)

    proj_sums = jnp.concatenate([main_part(sum_u), main_part(sum_v)], axis=0)
    vec_sums = jnp.concatenate([vector_part(sum_u), vector_part(sum_v)], axis=0)
    clipped_proj = proj_sums * lax.rsqrt(
        jnp.mean(proj_sums * proj_sums, axis=(1, 2), keepdims=True) + EPS
    )
    clipped_vecs = vec_sums * lax.rsqrt(jnp.mean(vec_sums * vec_sums, axis=1, keepdims=True) + EPS)
    loss = sum_v[0, depth + 1, 0] / (count * 256)

    row_grad = jnp.zeros((cells, width), jnp.float32)
    for feature in range(feats):
        block = dpooled[:, feature * width : (feature + 1) * width]
        row_grad = row_grad + lax.dot_general(
            counted[feature], block, (((0,), (0,)), ((), ())), preferred_element_type=jnp.float32
        )
    accum_new = cache_accum + jnp.mean(row_grad * row_grad, axis=1)
    rows_new = cache_rows - ETA * row_grad * lax.rsqrt(accum_new)[:, None]
    rows_new = rows_new.at[evict_slot].set(fetched_rows)
    accum_new = accum_new.at[evict_slot].set(fetched_accum)
    return (rows_new, accum_new, table_new, accum_table, clipped_proj, clipped_vecs, loss)


def solution(mesh):
    split = P(AXES)
    rows = P(AXES, None)
    return jax.shard_map(
        shards,
        mesh=mesh,
        in_specs=(
            rows,
            split,
            rows,
            split,
            rows,
            split,
            rows,
            split,
            rows,
            P(),
            P(),
            P(),
            P(),
        ),
        out_specs=(rows, split, rows, split, P(), P(), P()),
        check_vma=False,
    )
```

```python
import jax
import jax.numpy as jnp
from jax import lax
from jax.experimental import pallas as pl
from jax.experimental.pallas import tpu as pltpu
from jax.sharding import PartitionSpec as P

EPS = 1e-06
ETA = 0.05
AXES = ("trainer", "table")


def device_at(y, x, z, core):
    return (((y // 2 * 4 + x) * 2 + y % 2) * 8 + z % 8) * 2 + core


def first_groups():
    groups = []
    for y in range(4):
        for pair in range(4):
            groups.append([device_at(y, x, 2 * pair + b, 0) for x in range(4) for b in range(2)])
    for x in range(4):
        for pair in range(4):
            groups.append([device_at(y, x, 2 * pair + 1 + b, 1) for y in range(4) for b in range(2)])
    return groups


def second_groups():
    groups = []
    for x in range(4):
        for b in range(2):
            groups.append([device_at(y, x, 2 * k + b, 0) for y in range(4) for k in range(4)])
    for y in range(4):
        for b in range(2):
            groups.append([device_at(y, x, 2 * k + b, 1) for x in range(4) for k in range(4)])
    return groups


def swap_cores(value):
    return lax.ppermute(value, AXES, [(i, i ^ 1) for i in range(256)])


def exchange(value, groups):
    return lax.all_to_all(
        value, AXES, split_axis=0, concat_axis=0, tiled=True, axis_index_groups=groups
    )


def ranks(owner):
    listed = owner.shape[0]
    order = jnp.arange(listed, dtype=jnp.int32)
    earlier = (owner[:, None] == owner[None, :]) & (order[None, :] < order[:, None])
    return jnp.sum(earlier.astype(jnp.int32), axis=1)


def meta_row(columns, width):
    block = jnp.concatenate(columns, axis=1)
    return jnp.pad(block, ((0, 0), (0, width - block.shape[1])))[:, None, :]


def picked(values, index):
    hit = index[:, None] == jnp.arange(values.shape[0], dtype=jnp.int32)[None, :]
    return jnp.sum(jnp.where(hit, values[None, :], 0.0), axis=1)


def cross(value, bit):
    split = value.reshape(value.shape[0] // (2 * bit), 2, bit, *value.shape[1:])
    there = [(i, i ^ bit) for i in range(256)]
    came = lax.ppermute(split[:, 1], AXES, there)
    return jnp.stack([split[:, 0], came], axis=1).reshape(value.shape)


def dense_kernel(
    core_ref,
    slots_ref,
    labels_ref,
    cache_ref,
    u_ref,
    v_ref,
    bias_ref,
    head_ref,
    keep_ref,
    send_ref,
    dpooled_ref,
    high,
    mid,
    low,
    pooled,
    shifted,
    dlift,
):
    f32, bf16 = jnp.float32, jnp.bfloat16
    count, cells, width = slots_ref.shape[1], cache_ref.shape[0], cache_ref.shape[1]
    feats = u_ref.shape[0] // width
    looks = slots_ref.shape[0] // feats
    slots = jnp.transpose(slots_ref[...])
    rows = cache_ref[...]
    first = rows.astype(bf16)
    rest = rows - first.astype(f32)
    second = rest.astype(bf16)
    high[...] = first
    mid[...] = second
    low[...] = (rest - second.astype(f32)).astype(bf16)

    lane = lax.broadcasted_iota(jnp.int32, (count, cells), 1)
    for f in range(feats):
        counts = jnp.zeros((count, cells), f32)
        for look in range(looks):
            at = f * looks + look
            counts = counts + jnp.where(lane == slots[:, at : at + 1], 1.0, 0.0)
        counts = counts.astype(bf16)
        total = jnp.dot(counts, low[...], preferred_element_type=f32)
        total = total + jnp.dot(counts, mid[...], preferred_element_type=f32)
        total = total + jnp.dot(counts, high[...], preferred_element_type=f32)
        pooled[:, f * width : (f + 1) * width] = total.astype(bf16)

    latent = jnp.dot(pooled[...], v_ref[...], preferred_element_type=f32).astype(bf16)
    across = (((1,), (1,)), ((), ()))
    logit_wide = jnp.zeros((count, width), f32)
    for c in range(feats):
        cut = slice(c * width, (c + 1) * width)
        moved = lax.dot_general(latent, u_ref[cut, :], across, preferred_element_type=f32)
        moved = moved + bias_ref[:, cut]
        shifted[:, cut] = moved
        part = pooled[:, cut].astype(f32)
        logit_wide = logit_wide + (part * moved + part) * head_ref[:, cut]
    logit = jnp.sum(logit_wide, axis=1, keepdims=True)
    target = jnp.transpose(labels_ref[...]).astype(f32)
    small = jnp.exp(-jnp.abs(logit))
    losses = jnp.maximum(logit, 0.0) + jnp.log1p(small) - target * logit
    loss = jnp.sum(losses, axis=0, keepdims=True)
    dlogit = jnp.where(logit >= 0, 1.0, small) / (1.0 + small) - target

    mine = core_ref[0] == 0
    lane1 = lax.broadcasted_iota(jnp.int32, (1, width), 1)
    loss_row = jnp.where(lane1 == 0, loss, 0.0)
    back = jnp.zeros((count, width), f32)
    for c in range(feats):
        cut = slice(c * width, (c + 1) * width)
        part = pooled[:, cut].astype(f32)
        lift = dlogit * head_ref[:, cut] * part
        crossed = part * shifted[:, cut] + part
        dbias = jnp.sum(lift, axis=0, keepdims=True)
        dhead = jnp.sum(dlogit * crossed, axis=0, keepdims=True)
        lift = lift.astype(bf16)
        dlift[:, cut] = lift
        back = back + jnp.dot(lift, u_ref[cut, :], preferred_element_type=f32)
        keep_ref[c, width : width + 1, :] = jnp.where(mine, dbias, dhead)
        send_ref[c, width : width + 1, :] = jnp.where(mine, dhead, dbias)
        for ref in (keep_ref, send_ref):
            ref[c, width + 1 : width + 2, :] = loss_row
            ref[c, width + 2 : width + 8, :] = jnp.zeros((6, width), f32)
    dlatent = back.astype(bf16)

    down = (((0,), (0,)), ((), ()))
    right_keep = jnp.where(mine, latent, dlatent)
    right_send = jnp.where(mine, dlatent, latent)
    for c in range(feats):
        cut = slice(c * width, (c + 1) * width)
        lift, part = dlift[:, cut], pooled[:, cut]
        send_ref[c, :width, :] = lax.dot_general(
            jnp.where(mine, part, lift), right_send, down, preferred_element_type=f32
        )
        keep_ref[c, :width, :] = lax.dot_general(
            jnp.where(mine, lift, part), right_keep, down, preferred_element_type=f32
        )
    for c in range(feats):
        cut = slice(c * width, (c + 1) * width)
        through = lax.dot_general(dlatent, v_ref[cut, :], across, preferred_element_type=f32)
        through = through + dlogit * head_ref[:, cut] * (shifted[:, cut] + 1.0)
        dpooled_ref[:, cut] = through.astype(bf16)


def dense(core, slot_ids, labels, cache_rows, proj_u, proj_v, cross_bias, head):
    count, (cells, width) = slot_ids.shape[0], cache_rows.shape
    wide = proj_u.shape[0]
    blocks = wide // width
    vmem = pl.BlockSpec(memory_space=pltpu.VMEM)
    bundle = jax.ShapeDtypeStruct((blocks, width + 8, width), jnp.float32)
    return pl.pallas_call(
        dense_kernel,
        out_shape=(bundle, bundle, jax.ShapeDtypeStruct((count, wide), jnp.bfloat16)),
        in_specs=[pl.BlockSpec(memory_space=pltpu.SMEM)] + [vmem] * 7,
        out_specs=(vmem, vmem, vmem),
        scratch_shapes=[pltpu.VMEM((cells, width), jnp.bfloat16)] * 3
        + [
            pltpu.VMEM((count, wide), jnp.bfloat16),
            pltpu.VMEM((count, wide), jnp.float32),
            pltpu.VMEM((count, wide), jnp.bfloat16),
        ],
        compiler_params=pltpu.CompilerParams(vmem_limit_bytes=32 * 1024 * 1024),
        cost_estimate=pl.CostEstimate(flops=5_000_000_000, bytes_accessed=9_000_000, transcendentals=1000),
        name="dense",
    )(
        core[None],
        slot_ids.T,
        labels[None, :],
        cache_rows,
        proj_u,
        proj_v,
        cross_bias[None, :],
        head[None, :],
    )


def payload_kernel(
    slot_ref, evict_ref, miss_ref, accum_ref, cache_ref, out_ref, taken
):
    owners, per = taken.shape[0], out_ref.shape[0] // taken.shape[0]
    width = out_ref.shape[1]
    lane = lax.broadcasted_iota(jnp.int32, (1, width), 1)
    base = jnp.where((lane >= per) & (lane < 2 * per), -1.0, 0.0)

    def clear(o, _):
        taken[o] = 0
        out_ref[pl.ds(o * per, per - 1), :] = jnp.zeros((per - 1, width), jnp.float32)
        out_ref[pl.ds(o * per + per - 1, 1), :] = base
        return 0

    lax.fori_loop(0, owners, clear, 0, unroll=True)

    def leave(i, _):
        owner = evict_ref[0, i]
        rank = taken[owner]
        taken[owner] = rank + 1
        slot = slot_ref[i]
        out_ref[pl.ds(owner * per + rank, 1), :] = cache_ref[pl.ds(slot, 1), :]
        spot = pl.ds(owner * per + per - 1, 1)
        meta = jnp.where(lane == rank, accum_ref[slot], out_ref[spot, :])
        row = evict_ref[1, i].astype(jnp.float32)
        out_ref[spot, :] = jnp.where(lane == per + rank, row, meta)
        return 0

    lax.fori_loop(0, slot_ref.shape[0], leave, 0, unroll=8)

    def reset(o, _):
        taken[o] = 0
        return 0

    lax.fori_loop(0, owners, reset, 0, unroll=True)

    def ask(i, _):
        owner = miss_ref[0, i]
        rank = taken[owner]
        taken[owner] = rank + 1
        spot = pl.ds(owner * per + per - 1, 1)
        row = miss_ref[1, i].astype(jnp.float32)
        out_ref[spot, :] = jnp.where(lane == 2 * per + rank, row, out_ref[spot, :])
        return 0

    lax.fori_loop(0, slot_ref.shape[0], ask, 0, unroll=8)


def payload(evict_slot, evict_dest, miss_dest, cache_accum, cache_rows, owners, per):
    smem = pl.BlockSpec(memory_space=pltpu.SMEM)
    vmem = pl.BlockSpec(memory_space=pltpu.VMEM)
    return pl.pallas_call(
        payload_kernel,
        out_shape=jax.ShapeDtypeStruct((owners * per, cache_rows.shape[1]), jnp.float32),
        in_specs=[smem] * 4 + [vmem],
        out_specs=vmem,
        scratch_shapes=[pltpu.SMEM((owners,), jnp.int32)],
        cost_estimate=pl.CostEstimate(flops=100_000, bytes_accessed=1_500_000, transcendentals=0),
        name="payload",
    )(evict_slot, evict_dest.T, miss_dest.T, cache_accum, cache_rows)


def scaled(index, half_ref, proj_ref, stage, sems):
    blocks, width = half_ref.shape[0], half_ref.shape[2]
    squares = jnp.zeros((width, width), jnp.float32)
    for c in range(blocks):
        block = half_ref[c, :width, :]
        squares = squares + block * block
    total = jnp.sum(jnp.sum(squares, axis=0, keepdims=True), axis=1, keepdims=True)
    scale = lax.rsqrt(total / (blocks * width * width) + EPS)
    copies = []
    for c in range(blocks):
        stage[c] = half_ref[c, :width, :] * scale
        copies.append(
            pltpu.make_async_copy(
                stage.at[c], proj_ref.at[index, pl.ds(c * width, width), :], sems.at[c]
            )
        )
        copies[-1].start()
    return copies


def own_kernel(core_ref, half_ref, proj_ref, stage, sems):
    for copy in scaled(core_ref[0], half_ref, proj_ref, stage, sems):
        copy.wait()


def other_kernel(
    core_ref, proj_in, own_ref, half_ref, proj_ref, vec_ref, loss_ref, stage, sems
):
    core = core_ref[0]
    copies = scaled(1 - core, half_ref, proj_ref, stage, sems)
    blocks, width = half_ref.shape[0], half_ref.shape[2]
    mine = core == 0
    own = [own_ref[c, 0:1, :] for c in range(blocks)]
    far = [half_ref[c, width : width + 1, :] for c in range(blocks)]
    for index in (0, 1):
        rows = [jnp.where(mine, *((a, b) if index == 0 else (b, a))) for a, b in zip(own, far)]
        squares = sum(row * row for row in rows)
        total = jnp.sum(squares, axis=1, keepdims=True)
        scale = lax.rsqrt(total / (blocks * width) + EPS)
        for c in range(blocks):
            vec_ref[index : index + 1, c * width : (c + 1) * width] = rows[c] * scale
    loss_ref[...] = jnp.where(
        mine, half_ref[0, width + 1 : width + 2, :128], own_ref[0, 1:2, :128]
    )
    for copy in copies:
        copy.wait()


def normalized(core, own, other):
    blocks, depth, width = own.shape
    wide = blocks * width
    smem = pl.BlockSpec(memory_space=pltpu.SMEM)
    vmem = pl.BlockSpec(memory_space=pltpu.VMEM)
    anywhere = pl.BlockSpec(memory_space=pl.ANY)
    scratch = [
        pltpu.VMEM((blocks, width, width), jnp.float32),
        pltpu.SemaphoreType.DMA((blocks,)),
    ]
    proj = jax.ShapeDtypeStruct((2, wide, width), jnp.float32)
    limit = pltpu.CompilerParams(vmem_limit_bytes=16 * 1024 * 1024)
    half = pl.pallas_call(
        own_kernel,
        out_shape=proj,
        in_specs=[smem, vmem],
        out_specs=anywhere,
        scratch_shapes=scratch,
        compiler_params=limit,
        name="scale_own",
    )(core[None], own)
    return pl.pallas_call(
        other_kernel,
        out_shape=(
            proj,
            jax.ShapeDtypeStruct((2, wide), jnp.float32),
            jax.ShapeDtypeStruct((1, 128), jnp.float32),
        ),
        in_specs=[smem, anywhere, vmem, vmem],
        out_specs=(anywhere, vmem, vmem),
        scratch_shapes=scratch,
        input_output_aliases={1: 0},
        compiler_params=limit,
        name="scale_other",
    )(core[None], half, own[:, width:, :], other)


def shards(
    slot_ids,
    labels,
    cache_rows,
    cache_accum,
    table_rows,
    table_accum,
    miss_dest,
    evict_slot,
    evict_dest,
    proj_u,
    proj_v,
    cross_bias,
    head,
):
    owners = 32
    per = 8
    cap = 6
    width = cache_rows.shape[1]
    owned = table_rows.shape[0]
    cells = cache_rows.shape[0]
    spots = owners * per
    core = lax.axis_index("table") % 2

    me = lax.axis_index("table")
    sent = payload(
        evict_slot, evict_dest, miss_dest, cache_accum, cache_rows, owners, per
    ).reshape(owners, per, width)
    sent, slots_late = lax.optimization_barrier((sent, slot_ids))
    got = lax.all_to_all(sent, "table", split_axis=0, concat_axis=0, tiled=True)

    count = slot_ids.shape[0]
    feats = proj_u.shape[0] // width
    looks = slot_ids.shape[1] // feats
    keep, send, dpooled = dense(
        core, slots_late, labels, cache_rows, proj_u, proj_v, cross_bias, head
    )

    blocks = feats
    depth = width
    send, got = lax.optimization_barrier((send, got))
    held = keep + swap_cores(send)
    held, got = lax.optimization_barrier((held, got))

    got_meta = got[:, per - 1, :]
    got_id = got_meta[:, per : per + cap].astype(jnp.int32)
    flat = got_id.reshape(-1)
    table_new = table_rows.at[jnp.where(flat < 0, owned, flat)].set(
        got[:, :cap, :].reshape(-1, width), mode="drop"
    )
    stored = flat[:, None] == jnp.arange(owned, dtype=jnp.int32)[None, :]
    stored_sum = jnp.sum(jnp.where(stored, got_meta[:, :cap].reshape(-1)[:, None], 0.0), axis=0)
    accum_table = jnp.where(jnp.any(stored, axis=0), stored_sum, table_accum)
    order = jnp.arange(owners, dtype=jnp.int32)
    turned = (order ^ me)[:, None] == order[None, :]
    asked = jnp.sum(
        jnp.where(turned[:, :, None], got_meta[None, :, 2 * per : 3 * per], 0.0), axis=1
    )
    asked = asked.astype(jnp.int32).reshape(-1)
    is_meta = (jnp.arange(per) == per - 1)[None, :, None]
    reply_rows = jnp.take(table_new, asked, axis=0, mode="clip").reshape(owners, per, width)
    reply_accum = picked(accum_table, asked).reshape(owners, per)
    back = jnp.where(is_meta, meta_row([reply_accum], width), reply_rows)

    held = exchange(held, first_groups())
    back = cross(cross(back, 1), 16)
    held, back = lax.optimization_barrier((held, back))
    held = jnp.sum(held, axis=0)
    fine = depth // 16
    pieces16 = jnp.concatenate(
        [
            held[:depth].reshape(16, fine, width),
            jnp.broadcast_to(held[None, depth:], (16, 8, width)),
        ],
        axis=1,
    )
    held = exchange(pieces16, second_groups())
    back = cross(back, 2)
    held, back = lax.optimization_barrier((held, back))
    summed16 = jnp.sum(held, axis=0)
    extras = summed16[fine:]
    spread = jnp.broadcast_to(summed16[None, :fine], (16, fine, width))
    held = exchange(spread, second_groups())
    back = cross(back, 4)
    held, back = lax.optimization_barrier((held, back))
    whole = jnp.concatenate([held.reshape(depth, width), extras], axis=0)
    whole = exchange(jnp.broadcast_to(whole[None], (blocks, depth + 8, width)), first_groups())
    back = cross(back, 8)
    whole, back = lax.optimization_barrier((whole, back))
    in_place = (miss_dest[:, 0] ^ me) * per + ranks(miss_dest[:, 0])
    fetched_rows = jnp.take(back.reshape(spots, width), in_place, axis=0, mode="clip")
    fetched_accum = picked(back[:, per - 1, :per].reshape(-1), in_place)
    clipped_proj, clipped_vecs, loss_row = normalized(core, whole, swap_cores(whole))
    loss = loss_row[0, 0] / (count * 256)

    slot_range = jnp.arange(cells, dtype=jnp.int32)
    row_grad = jnp.zeros((cells, width), jnp.float32)
    for feature in range(feats):
        counts = jnp.zeros((count, cells), jnp.bfloat16)
        for lookup in range(looks):
            column = slot_ids[:, feature * looks + lookup]
            counts = counts + (column[:, None] == slot_range[None, :]).astype(jnp.bfloat16)
        block = dpooled[:, feature * width : (feature + 1) * width]
        row_grad = row_grad + lax.dot_general(
            counts, block, (((0,), (0,)), ((), ())), preferred_element_type=jnp.float32
        )
    accum_new = cache_accum + jnp.mean(row_grad * row_grad, axis=1)
    rows_new = cache_rows - ETA * row_grad * lax.rsqrt(accum_new)[:, None]
    rows_new = rows_new.at[evict_slot].set(fetched_rows)
    accum_new = accum_new.at[evict_slot].set(fetched_accum)
    return (rows_new, accum_new, table_new, accum_table, clipped_proj, clipped_vecs, loss)


def solution(mesh):
    split = P(AXES)
    rows = P(AXES, None)
    return jax.shard_map(
        shards,
        mesh=mesh,
        in_specs=(
            rows,
            split,
            rows,
            split,
            rows,
            split,
            rows,
            split,
            rows,
            P(),
            P(),
            P(),
            P(),
        ),
        out_specs=(rows, split, rows, split, P(), P(), P()),
        check_vma=False,
    )
```

```python
import jax
import jax.numpy as jnp
from jax import lax
from jax.experimental import pallas as pl
from jax.experimental.pallas import tpu as pltpu
from jax.sharding import PartitionSpec as P

EPS = 1e-06
ETA = 0.05
AXES = ("trainer", "table")


def device_at(y, x, z, core):
    return (((y // 2 * 4 + x) * 2 + y % 2) * 8 + z % 8) * 2 + core


def first_groups():
    groups = []
    for y in range(4):
        for pair in range(4):
            groups.append([device_at(y, x, 2 * pair + b, 0) for x in range(4) for b in range(2)])
    for x in range(4):
        for pair in range(4):
            groups.append([device_at(y, x, 2 * pair + 1 + b, 1) for y in range(4) for b in range(2)])
    return groups


def second_groups():
    groups = []
    for x in range(4):
        for b in range(2):
            groups.append([device_at(y, x, 2 * k + b, 0) for y in range(4) for k in range(4)])
    for y in range(4):
        for b in range(2):
            groups.append([device_at(y, x, 2 * k + b, 1) for x in range(4) for k in range(4)])
    return groups


def swap_cores(value):
    return lax.ppermute(value, AXES, [(i, i ^ 1) for i in range(256)])


def exchange(value, groups):
    return lax.all_to_all(
        value, AXES, split_axis=0, concat_axis=0, tiled=True, axis_index_groups=groups
    )


def ranks(owner):
    listed = owner.shape[0]
    order = jnp.arange(listed, dtype=jnp.int32)
    earlier = (owner[:, None] == owner[None, :]) & (order[None, :] < order[:, None])
    return jnp.sum(earlier.astype(jnp.int32), axis=1)


def meta_row(columns, width):
    block = jnp.concatenate(columns, axis=1)
    return jnp.pad(block, ((0, 0), (0, width - block.shape[1])))[:, None, :]


def picked(values, index):
    hit = index[:, None] == jnp.arange(values.shape[0], dtype=jnp.int32)[None, :]
    return jnp.sum(jnp.where(hit, values[None, :], 0.0), axis=1)


def cross(value, bit):
    split = value.reshape(value.shape[0] // (2 * bit), 2, bit, *value.shape[1:])
    there = [(i, i ^ bit) for i in range(256)]
    came = lax.ppermute(split[:, 1], AXES, there)
    return jnp.stack([split[:, 0], came], axis=1).reshape(value.shape)


def dense_kernel(
    core_ref,
    slots_ref,
    labels_ref,
    cache_ref,
    u_any,
    v_any,
    bias_ref,
    head_ref,
    keep_out,
    send_out,
    dpooled_out,
    u_ref,
    v_ref,
    keep_ref,
    send_ref,
    dpooled_ref,
    high,
    mid,
    low,
    pooled,
    shifted,
    dlift,
    in_sems,
    out_sems,
):
    f32, bf16 = jnp.float32, jnp.bfloat16
    load_v = pltpu.make_async_copy(v_any, v_ref, in_sems.at[0])
    load_u = pltpu.make_async_copy(u_any, u_ref, in_sems.at[1])
    load_v.start()
    load_u.start()
    count, cells, width = slots_ref.shape[1], cache_ref.shape[0], cache_ref.shape[1]
    feats = u_ref.shape[0] // width
    looks = slots_ref.shape[0] // feats
    slots = jnp.transpose(slots_ref[...])
    rows = cache_ref[...]
    first = rows.astype(bf16)
    rest = rows - first.astype(f32)
    second = rest.astype(bf16)
    high[...] = first
    mid[...] = second
    low[...] = (rest - second.astype(f32)).astype(bf16)

    lane = lax.broadcasted_iota(jnp.int32, (count, cells), 1)
    for f in range(feats):
        counts = jnp.zeros((count, cells), f32)
        for look in range(looks):
            at = f * looks + look
            counts = counts + jnp.where(lane == slots[:, at : at + 1], 1.0, 0.0)
        counts = counts.astype(bf16)
        total = jnp.dot(counts, low[...], preferred_element_type=f32)
        total = total + jnp.dot(counts, mid[...], preferred_element_type=f32)
        total = total + jnp.dot(counts, high[...], preferred_element_type=f32)
        pooled[:, f * width : (f + 1) * width] = total.astype(bf16)

    load_v.wait()
    load_u.wait()
    latent = jnp.dot(pooled[...], v_ref[...], preferred_element_type=f32).astype(bf16)
    across = (((1,), (1,)), ((), ()))
    logit_wide = jnp.zeros((count, width), f32)
    for c in range(feats):
        cut = slice(c * width, (c + 1) * width)
        moved = lax.dot_general(latent, u_ref[cut, :], across, preferred_element_type=f32)
        moved = moved + bias_ref[:, cut]
        shifted[:, cut] = moved
        part = pooled[:, cut].astype(f32)
        logit_wide = logit_wide + (part * moved + part) * head_ref[:, cut]
    logit = jnp.sum(logit_wide, axis=1, keepdims=True)
    target = jnp.transpose(labels_ref[...]).astype(f32)
    small = jnp.exp(-jnp.abs(logit))
    losses = jnp.maximum(logit, 0.0) + jnp.log1p(small) - target * logit
    loss = jnp.sum(losses, axis=0, keepdims=True)
    dlogit = jnp.where(logit >= 0, 1.0, small) / (1.0 + small) - target

    mine = core_ref[0] == 0
    lane1 = lax.broadcasted_iota(jnp.int32, (1, width), 1)
    loss_row = jnp.where(lane1 == 0, loss, 0.0)
    back = jnp.zeros((count, width), f32)
    for c in range(feats):
        cut = slice(c * width, (c + 1) * width)
        part = pooled[:, cut].astype(f32)
        lift = dlogit * head_ref[:, cut] * part
        crossed = part * shifted[:, cut] + part
        dbias = jnp.sum(lift, axis=0, keepdims=True)
        dhead = jnp.sum(dlogit * crossed, axis=0, keepdims=True)
        lift = lift.astype(bf16)
        dlift[:, cut] = lift
        back = back + jnp.dot(lift, u_ref[cut, :], preferred_element_type=f32)
        keep_ref[c, width : width + 1, :] = jnp.where(mine, dbias, dhead)
        send_ref[c, width : width + 1, :] = jnp.where(mine, dhead, dbias)
        for ref in (keep_ref, send_ref):
            ref[c, width + 1 : width + 2, :] = loss_row
            ref[c, width + 2 : width + 8, :] = jnp.zeros((6, width), f32)
    dlatent = back.astype(bf16)

    down = (((0,), (0,)), ((), ()))
    right_keep = jnp.where(mine, latent, dlatent)
    right_send = jnp.where(mine, dlatent, latent)
    copies = []

    def give(source, target):
        copies.append(pltpu.make_async_copy(source, target, out_sems.at[len(copies)]))
        copies[-1].start()

    for c in range(feats):
        cut = slice(c * width, (c + 1) * width)
        send_ref[c, :width, :] = lax.dot_general(
            jnp.where(mine, pooled[:, cut], dlift[:, cut]),
            right_send,
            down,
            preferred_element_type=f32,
        )
        give(send_ref.at[c], send_out.at[c])
    for c in range(feats):
        cut = slice(c * width, (c + 1) * width)
        keep_ref[c, :width, :] = lax.dot_general(
            jnp.where(mine, dlift[:, cut], pooled[:, cut]),
            right_keep,
            down,
            preferred_element_type=f32,
        )
        give(keep_ref.at[c], keep_out.at[c])
    for c in range(feats):
        cut = slice(c * width, (c + 1) * width)
        through = lax.dot_general(dlatent, v_ref[cut, :], across, preferred_element_type=f32)
        through = through + dlogit * head_ref[:, cut] * (shifted[:, cut] + 1.0)
        dpooled_ref[c] = through.astype(bf16)
        give(dpooled_ref.at[c], dpooled_out.at[c])
    for copy in copies:
        copy.wait()


def dense(core, slot_ids, labels, cache_rows, proj_u, proj_v, cross_bias, head):
    count, (cells, width) = slot_ids.shape[0], cache_rows.shape
    wide = proj_u.shape[0]
    blocks = wide // width
    anywhere = pl.BlockSpec(memory_space=pl.ANY)
    vmem = pl.BlockSpec(memory_space=pltpu.VMEM)
    bundle = jax.ShapeDtypeStruct((blocks, width + 8, width), jnp.float32)
    return pl.pallas_call(
        dense_kernel,
        out_shape=(
            bundle,
            bundle,
            jax.ShapeDtypeStruct((blocks, count, width), jnp.bfloat16),
        ),
        in_specs=[pl.BlockSpec(memory_space=pltpu.SMEM)]
        + [vmem] * 3
        + [anywhere] * 2
        + [vmem] * 2,
        out_specs=(anywhere, anywhere, anywhere),
        scratch_shapes=[
            pltpu.VMEM((wide, width), jnp.bfloat16),
            pltpu.VMEM((wide, width), jnp.bfloat16),
            pltpu.VMEM(bundle.shape, jnp.float32),
            pltpu.VMEM(bundle.shape, jnp.float32),
            pltpu.VMEM((blocks, count, width), jnp.bfloat16),
        ]
        + [pltpu.VMEM((cells, width), jnp.bfloat16)] * 3
        + [
            pltpu.VMEM((count, wide), jnp.bfloat16),
            pltpu.VMEM((count, wide), jnp.float32),
            pltpu.VMEM((count, wide), jnp.bfloat16),
            pltpu.SemaphoreType.DMA((2,)),
            pltpu.SemaphoreType.DMA((3 * blocks,)),
        ],
        compiler_params=pltpu.CompilerParams(vmem_limit_bytes=60 * 1024 * 1024),
        cost_estimate=pl.CostEstimate(flops=5_000_000_000, bytes_accessed=9_000_000, transcendentals=1000),
        name="dense",
    )(
        core[None],
        slot_ids.T,
        labels[None, :],
        cache_rows,
        proj_u,
        proj_v,
        cross_bias[None, :],
        head[None, :],
    )


def payload_kernel(
    slot_ref, evict_ref, miss_ref, accum_ref, cache_ref, out_ref, taken
):
    owners, per = taken.shape[0], out_ref.shape[0] // taken.shape[0]
    width = out_ref.shape[1]
    lane = lax.broadcasted_iota(jnp.int32, (1, width), 1)
    base = jnp.where((lane >= per) & (lane < 2 * per), -1.0, 0.0)

    def clear(o, _):
        taken[o] = 0
        out_ref[pl.ds(o * per, per - 1), :] = jnp.zeros((per - 1, width), jnp.float32)
        out_ref[pl.ds(o * per + per - 1, 1), :] = base
        return 0

    lax.fori_loop(0, owners, clear, 0, unroll=True)

    def leave(i, _):
        owner = evict_ref[0, i]
        rank = taken[owner]
        taken[owner] = rank + 1
        slot = slot_ref[i]
        out_ref[pl.ds(owner * per + rank, 1), :] = cache_ref[pl.ds(slot, 1), :]
        spot = pl.ds(owner * per + per - 1, 1)
        meta = jnp.where(lane == rank, accum_ref[slot], out_ref[spot, :])
        row = evict_ref[1, i].astype(jnp.float32)
        out_ref[spot, :] = jnp.where(lane == per + rank, row, meta)
        return 0

    lax.fori_loop(0, slot_ref.shape[0], leave, 0, unroll=8)

    def reset(o, _):
        taken[o] = 0
        return 0

    lax.fori_loop(0, owners, reset, 0, unroll=True)

    def ask(i, _):
        owner = miss_ref[0, i]
        rank = taken[owner]
        taken[owner] = rank + 1
        spot = pl.ds(owner * per + per - 1, 1)
        row = miss_ref[1, i].astype(jnp.float32)
        out_ref[spot, :] = jnp.where(lane == 2 * per + rank, row, out_ref[spot, :])
        return 0

    lax.fori_loop(0, slot_ref.shape[0], ask, 0, unroll=8)


def payload(evict_slot, evict_dest, miss_dest, cache_accum, cache_rows, owners, per):
    smem = pl.BlockSpec(memory_space=pltpu.SMEM)
    vmem = pl.BlockSpec(memory_space=pltpu.VMEM)
    return pl.pallas_call(
        payload_kernel,
        out_shape=jax.ShapeDtypeStruct((owners * per, cache_rows.shape[1]), jnp.float32),
        in_specs=[smem] * 4 + [vmem],
        out_specs=vmem,
        scratch_shapes=[pltpu.SMEM((owners,), jnp.int32)],
        cost_estimate=pl.CostEstimate(flops=100_000, bytes_accessed=1_500_000, transcendentals=0),
        name="payload",
    )(evict_slot, evict_dest.T, miss_dest.T, cache_accum, cache_rows)


def refill_kernel(
    slots_ref,
    evict_ref,
    place_ref,
    cache_ref,
    accum_ref,
    dpooled_ref,
    back_ref,
    rows_ref,
    accum_out,
):
    f32, bf16 = jnp.float32, jnp.bfloat16
    (cells, width), (feats, count, _) = cache_ref.shape, dpooled_ref.shape
    looks = slots_ref.shape[0] // feats
    cell = lax.broadcasted_iota(jnp.int32, (cells, count), 0)
    grad = jnp.zeros((cells, width), f32)
    for f in range(feats):
        counts = jnp.zeros((cells, count), f32)
        for look in range(looks):
            at = f * looks + look
            counts = counts + jnp.where(cell == slots_ref[at : at + 1, :], 1.0, 0.0)
        grad = grad + jnp.dot(counts.astype(bf16), dpooled_ref[f], preferred_element_type=f32)
    mean = jnp.sum(grad * grad, axis=1, keepdims=True) / width
    accum = jnp.transpose(accum_ref[...]) + mean
    rows_ref[...] = cache_ref[...] - ETA * grad * lax.rsqrt(accum)
    accum_out[...] = jnp.transpose(accum)

    def refill(i, _):
        rows_ref[pl.ds(evict_ref[i], 1), :] = back_ref[pl.ds(place_ref[i], 1), :]
        return 0

    lax.fori_loop(0, evict_ref.shape[0], refill, 0, unroll=8)


def refilled(slot_ids, evict_slot, place, cache_rows, cache_accum, dpooled, back):
    cells = cache_rows.shape[0]
    smem = pl.BlockSpec(memory_space=pltpu.SMEM)
    vmem = pl.BlockSpec(memory_space=pltpu.VMEM)
    return pl.pallas_call(
        refill_kernel,
        out_shape=(
            jax.ShapeDtypeStruct(cache_rows.shape, jnp.float32),
            jax.ShapeDtypeStruct((1, cells), jnp.float32),
        ),
        in_specs=[vmem, smem, smem, vmem, vmem, vmem, vmem],
        out_specs=(vmem, vmem),
        compiler_params=pltpu.CompilerParams(vmem_limit_bytes=60 * 1024 * 1024),
        cost_estimate=pl.CostEstimate(flops=1_100_000_000, bytes_accessed=4_000_000, transcendentals=1000),
        name="refill",
    )(
        slot_ids.T,
        evict_slot,
        place,
        cache_rows,
        cache_accum[None, :],
        dpooled,
        back,
    )


def scaled(index, half_any, proj_ref, half, stage, in_sems, out_sems):
    blocks, width = half.shape[0], half.shape[2]
    loads = []
    for c in range(blocks):
        loads.append(pltpu.make_async_copy(half_any.at[c], half.at[c], in_sems.at[c]))
        loads[-1].start()
    squares = jnp.zeros((width, width), jnp.float32)
    for c in range(blocks):
        loads[c].wait()
        block = half[c, :width, :]
        squares = squares + block * block
    total = jnp.sum(jnp.sum(squares, axis=0, keepdims=True), axis=1, keepdims=True)
    scale = lax.rsqrt(total / (blocks * width * width) + EPS)
    copies = []
    for c in range(blocks):
        stage[c] = half[c, :width, :] * scale
        copies.append(
            pltpu.make_async_copy(
                stage.at[c], proj_ref.at[index, pl.ds(c * width, width), :], out_sems.at[c]
            )
        )
        copies[-1].start()
    return copies


def own_kernel(core_ref, half_any, proj_ref, half, stage, in_sems, out_sems):
    for copy in scaled(core_ref[0], half_any, proj_ref, half, stage, in_sems, out_sems):
        copy.wait()


def other_kernel(
    core_ref,
    proj_in,
    own_ref,
    half_any,
    proj_ref,
    vec_ref,
    loss_ref,
    half,
    stage,
    in_sems,
    out_sems,
):
    core = core_ref[0]
    copies = scaled(1 - core, half_any, proj_ref, half, stage, in_sems, out_sems)
    blocks, width = half.shape[0], half.shape[2]
    mine = core == 0
    own = [own_ref[c, 0:1, :] for c in range(blocks)]
    far = [half[c, width : width + 1, :] for c in range(blocks)]
    for index in (0, 1):
        rows = [jnp.where(mine, *((a, b) if index == 0 else (b, a))) for a, b in zip(own, far)]
        squares = sum(row * row for row in rows)
        total = jnp.sum(squares, axis=1, keepdims=True)
        scale = lax.rsqrt(total / (blocks * width) + EPS)
        for c in range(blocks):
            vec_ref[index : index + 1, c * width : (c + 1) * width] = rows[c] * scale
    loss_ref[...] = jnp.where(
        mine, half[0, width + 1 : width + 2, :128], own_ref[0, 1:2, :128]
    )
    for copy in copies:
        copy.wait()


def normalized(core, own, other):
    blocks, depth, width = own.shape
    wide = blocks * width
    smem = pl.BlockSpec(memory_space=pltpu.SMEM)
    vmem = pl.BlockSpec(memory_space=pltpu.VMEM)
    anywhere = pl.BlockSpec(memory_space=pl.ANY)
    scratch = [
        pltpu.VMEM((blocks, depth, width), jnp.float32),
        pltpu.VMEM((blocks, width, width), jnp.float32),
        pltpu.SemaphoreType.DMA((blocks,)),
        pltpu.SemaphoreType.DMA((blocks,)),
    ]
    proj = jax.ShapeDtypeStruct((2, wide, width), jnp.float32)
    limit = pltpu.CompilerParams(vmem_limit_bytes=16 * 1024 * 1024)
    half = pl.pallas_call(
        own_kernel,
        out_shape=proj,
        in_specs=[smem, anywhere],
        out_specs=anywhere,
        scratch_shapes=scratch,
        compiler_params=limit,
        name="scale_own",
    )(core[None], own)
    return pl.pallas_call(
        other_kernel,
        out_shape=(
            proj,
            jax.ShapeDtypeStruct((2, wide), jnp.float32),
            jax.ShapeDtypeStruct((1, 128), jnp.float32),
        ),
        in_specs=[smem, anywhere, vmem, anywhere],
        out_specs=(anywhere, vmem, vmem),
        scratch_shapes=scratch,
        input_output_aliases={1: 0},
        compiler_params=limit,
        name="scale_other",
    )(core[None], half, own[:, width:, :], other)


def shards(
    slot_ids,
    labels,
    cache_rows,
    cache_accum,
    table_rows,
    table_accum,
    miss_dest,
    evict_slot,
    evict_dest,
    proj_u,
    proj_v,
    cross_bias,
    head,
):
    owners = 32
    per = 8
    cap = 6
    width = cache_rows.shape[1]
    owned = table_rows.shape[0]
    cells = cache_rows.shape[0]
    spots = owners * per
    core = lax.axis_index("table") % 2

    me = lax.axis_index("table")
    sent = payload(
        evict_slot, evict_dest, miss_dest, cache_accum, cache_rows, owners, per
    ).reshape(owners, per, width)
    sent, slots_late = lax.optimization_barrier((sent, slot_ids))
    got = lax.all_to_all(sent, "table", split_axis=0, concat_axis=0, tiled=True)

    count = slot_ids.shape[0]
    feats = proj_u.shape[0] // width
    keep, send, dpooled = dense(
        core, slots_late, labels, cache_rows, proj_u, proj_v, cross_bias, head
    )

    blocks = feats
    depth = width
    send, got = lax.optimization_barrier((send, got))
    held = keep + swap_cores(send)
    held, got = lax.optimization_barrier((held, got))

    got_meta = got[:, per - 1, :]
    got_id = got_meta[:, per : per + cap].astype(jnp.int32)
    flat = got_id.reshape(-1)
    table_new = table_rows.at[jnp.where(flat < 0, owned, flat)].set(
        got[:, :cap, :].reshape(-1, width), mode="drop"
    )
    stored = flat[:, None] == jnp.arange(owned, dtype=jnp.int32)[None, :]
    stored_sum = jnp.sum(jnp.where(stored, got_meta[:, :cap].reshape(-1)[:, None], 0.0), axis=0)
    accum_table = jnp.where(jnp.any(stored, axis=0), stored_sum, table_accum)
    order = jnp.arange(owners, dtype=jnp.int32)
    turned = (order ^ me)[:, None] == order[None, :]
    asked = jnp.sum(
        jnp.where(turned[:, :, None], got_meta[None, :, 2 * per : 3 * per], 0.0), axis=1
    )
    asked = asked.astype(jnp.int32).reshape(-1)
    is_meta = (jnp.arange(per) == per - 1)[None, :, None]
    reply_rows = jnp.take(table_new, asked, axis=0, mode="clip").reshape(owners, per, width)
    reply_accum = picked(accum_table, asked).reshape(owners, per)
    back = jnp.where(is_meta, meta_row([reply_accum], width), reply_rows)

    held = exchange(held, first_groups())
    back = cross(cross(back, 1), 16)
    held, back = lax.optimization_barrier((held, back))
    held = jnp.sum(held, axis=0)
    fine = depth // 16
    pieces16 = jnp.concatenate(
        [
            held[:depth].reshape(16, fine, width),
            jnp.broadcast_to(held[None, depth:], (16, 8, width)),
        ],
        axis=1,
    )
    held = exchange(pieces16, second_groups())
    back = cross(cross(back, 2), 4)
    held, back = lax.optimization_barrier((held, back))
    summed16 = jnp.sum(held, axis=0)
    extras = summed16[fine:]
    spread = jnp.broadcast_to(summed16[None, :fine], (16, fine, width))
    held = exchange(spread, second_groups())
    back = cross(back, 8)
    held, back = lax.optimization_barrier((held, back))
    whole = jnp.concatenate([held.reshape(depth, width), extras], axis=0)
    whole = exchange(jnp.broadcast_to(whole[None], (blocks, depth + 8, width)), first_groups())
    in_place = (miss_dest[:, 0] ^ me) * per + ranks(miss_dest[:, 0])
    rows_new, accum_new = refilled(
        slot_ids, evict_slot, in_place, cache_rows, cache_accum, dpooled, back.reshape(spots, width)
    )
    fetched_accum = picked(back[:, per - 1, :per].reshape(-1), in_place)
    filled = evict_slot[:, None] == jnp.arange(cells, dtype=jnp.int32)[None, :]
    filled_sum = jnp.sum(jnp.where(filled, fetched_accum[:, None], 0.0), axis=0)
    accum_new = jnp.where(jnp.any(filled, axis=0), filled_sum, accum_new.reshape(cells))
    whole, rows_new, accum_new = lax.optimization_barrier((whole, rows_new, accum_new))
    clipped_proj, clipped_vecs, loss_row = normalized(core, whole, swap_cores(whole))
    loss = loss_row[0, 0] / (count * 256)
    return (rows_new, accum_new, table_new, accum_table, clipped_proj, clipped_vecs, loss)


def solution(mesh):
    split = P(AXES)
    rows = P(AXES, None)
    return jax.shard_map(
        shards,
        mesh=mesh,
        in_specs=(
            rows,
            split,
            rows,
            split,
            rows,
            split,
            rows,
            split,
            rows,
            P(),
            P(),
            P(),
            P(),
        ),
        out_specs=(rows, split, rows, split, P(), P(), P()),
        check_vma=False,
    )
```

```python
import jax
import jax.numpy as jnp
from jax import lax
from jax.experimental import pallas as pl
from jax.experimental.pallas import tpu as pltpu
from jax.sharding import PartitionSpec as P

EPS = 1e-06
ETA = 0.05
AXES = ("trainer", "table")


def device_at(y, x, z, core):
    return (((y // 2 * 4 + x) * 2 + y % 2) * 8 + z % 8) * 2 + core


def first_groups():
    groups = []
    for y in range(4):
        for pair in range(4):
            groups.append([device_at(y, x, 2 * pair + b, 0) for x in range(4) for b in range(2)])
    for x in range(4):
        for pair in range(4):
            groups.append([device_at(y, x, 2 * pair + 1 + b, 1) for y in range(4) for b in range(2)])
    return groups


def second_groups():
    groups = []
    for x in range(4):
        for b in range(2):
            groups.append([device_at(y, x, 2 * k + b, 0) for y in range(4) for k in range(4)])
    for y in range(4):
        for b in range(2):
            groups.append([device_at(y, x, 2 * k + b, 1) for x in range(4) for k in range(4)])
    return groups


def swap_cores(value):
    return lax.ppermute(value, AXES, [(i, i ^ 1) for i in range(256)])


def exchange(value, groups):
    return lax.all_to_all(
        value, AXES, split_axis=0, concat_axis=0, tiled=True, axis_index_groups=groups
    )


def ranks(owner):
    listed = owner.shape[0]
    order = jnp.arange(listed, dtype=jnp.int32)
    earlier = (owner[:, None] == owner[None, :]) & (order[None, :] < order[:, None])
    return jnp.sum(earlier.astype(jnp.int32), axis=1)


def meta_row(columns, width):
    block = jnp.concatenate(columns, axis=1)
    return jnp.pad(block, ((0, 0), (0, width - block.shape[1])))[:, None, :]


def picked(values, index):
    hit = index[:, None] == jnp.arange(values.shape[0], dtype=jnp.int32)[None, :]
    return jnp.sum(jnp.where(hit, values[None, :], 0.0), axis=1)


def cross(value, bit):
    split = value.reshape(value.shape[0] // (2 * bit), 2, bit, *value.shape[1:])
    there = [(i, i ^ bit) for i in range(256)]
    came = lax.ppermute(split[:, 1], AXES, there)
    return jnp.stack([split[:, 0], came], axis=1).reshape(value.shape)


def cross_z(value):
    split = value.reshape(2, 8, 2, *value.shape[1:])
    came = [split[:, 0]]
    for step in range(1, 8):
        there = [(i, i ^ (2 * step)) for i in range(256)]
        came.append(lax.ppermute(split[:, step], AXES, there))
    return jnp.stack(came, axis=1).reshape(value.shape)


def dense_kernel(
    core_ref,
    slots_ref,
    labels_ref,
    cache_ref,
    u_any,
    v_any,
    bias_ref,
    head_ref,
    keep_out,
    send_out,
    latent_ref,
    dlatent_ref,
    dlogit_ref,
    u_ref,
    v_ref,
    keep_ref,
    send_ref,
    high,
    mid,
    low,
    pooled,
    shifted,
    dlift,
    in_sems,
    out_sems,
):
    f32, bf16 = jnp.float32, jnp.bfloat16
    load_v = pltpu.make_async_copy(v_any, v_ref, in_sems.at[0])
    load_u = pltpu.make_async_copy(u_any, u_ref, in_sems.at[1])
    load_v.start()
    load_u.start()
    count, cells, width = slots_ref.shape[1], cache_ref.shape[0], cache_ref.shape[1]
    feats = u_ref.shape[0] // width
    looks = slots_ref.shape[0] // feats
    slots = jnp.transpose(slots_ref[...])
    rows = cache_ref[...]
    first = rows.astype(bf16)
    rest = rows - first.astype(f32)
    second = rest.astype(bf16)
    high[...] = first
    mid[...] = second
    low[...] = (rest - second.astype(f32)).astype(bf16)

    lane = lax.broadcasted_iota(jnp.int32, (count, cells), 1)
    for f in range(feats):
        counts = jnp.zeros((count, cells), f32)
        for look in range(looks):
            at = f * looks + look
            counts = counts + jnp.where(lane == slots[:, at : at + 1], 1.0, 0.0)
        counts = counts.astype(bf16)
        total = jnp.dot(counts, low[...], preferred_element_type=f32)
        total = total + jnp.dot(counts, mid[...], preferred_element_type=f32)
        total = total + jnp.dot(counts, high[...], preferred_element_type=f32)
        pooled[:, f * width : (f + 1) * width] = total.astype(bf16)

    load_v.wait()
    load_u.wait()
    latent = jnp.dot(pooled[...], v_ref[...], preferred_element_type=f32).astype(bf16)
    latent_ref[...] = latent
    across = (((1,), (1,)), ((), ()))
    logit_wide = jnp.zeros((count, width), f32)
    for c in range(feats):
        cut = slice(c * width, (c + 1) * width)
        moved = lax.dot_general(latent, u_ref[cut, :], across, preferred_element_type=f32)
        moved = moved + bias_ref[:, cut]
        shifted[:, cut] = moved
        part = pooled[:, cut].astype(f32)
        logit_wide = logit_wide + (part * moved + part) * head_ref[:, cut]
    logit = jnp.sum(logit_wide, axis=1, keepdims=True)
    target = jnp.transpose(labels_ref[...]).astype(f32)
    small = jnp.exp(-jnp.abs(logit))
    losses = jnp.maximum(logit, 0.0) + jnp.log1p(small) - target * logit
    loss = jnp.sum(losses, axis=0, keepdims=True)
    dlogit = jnp.where(logit >= 0, 1.0, small) / (1.0 + small) - target

    mine = core_ref[0] == 0
    lane1 = lax.broadcasted_iota(jnp.int32, (1, width), 1)
    loss_row = jnp.where(lane1 == 0, loss, 0.0)
    back = jnp.zeros((count, width), f32)
    for c in range(feats):
        cut = slice(c * width, (c + 1) * width)
        part = pooled[:, cut].astype(f32)
        lift = dlogit * head_ref[:, cut] * part
        crossed = part * shifted[:, cut] + part
        dbias = jnp.sum(lift, axis=0, keepdims=True)
        dhead = jnp.sum(dlogit * crossed, axis=0, keepdims=True)
        lift = lift.astype(bf16)
        dlift[:, cut] = lift
        back = back + jnp.dot(lift, u_ref[cut, :], preferred_element_type=f32)
        keep_ref[c, width : width + 1, :] = jnp.where(mine, dbias, dhead)
        send_ref[c, width : width + 1, :] = jnp.where(mine, dhead, dbias)
        for ref in (keep_ref, send_ref):
            ref[c, width + 1 : width + 2, :] = loss_row
            ref[c, width + 2 : width + 8, :] = jnp.zeros((6, width), f32)
    dlatent = back.astype(bf16)
    dlatent_ref[...] = dlatent
    dlogit_ref[...] = jnp.transpose(dlogit)

    down = (((0,), (0,)), ((), ()))
    right_keep = jnp.where(mine, latent, dlatent)
    right_send = jnp.where(mine, dlatent, latent)
    copies = []

    def give(source, target):
        copies.append(pltpu.make_async_copy(source, target, out_sems.at[len(copies)]))
        copies[-1].start()

    for c in range(feats):
        cut = slice(c * width, (c + 1) * width)
        send_ref[c, :width, :] = lax.dot_general(
            jnp.where(mine, pooled[:, cut], dlift[:, cut]),
            right_send,
            down,
            preferred_element_type=f32,
        )
        give(send_ref.at[c], send_out.at[c])
    for c in range(feats):
        cut = slice(c * width, (c + 1) * width)
        keep_ref[c, :width, :] = lax.dot_general(
            jnp.where(mine, dlift[:, cut], pooled[:, cut]),
            right_keep,
            down,
            preferred_element_type=f32,
        )
        give(keep_ref.at[c], keep_out.at[c])
    for copy in copies:
        copy.wait()


def dense(core, slot_ids, labels, cache_rows, proj_u, proj_v, cross_bias, head):
    count, (cells, width) = slot_ids.shape[0], cache_rows.shape
    wide = proj_u.shape[0]
    blocks = wide // width
    anywhere = pl.BlockSpec(memory_space=pl.ANY)
    vmem = pl.BlockSpec(memory_space=pltpu.VMEM)
    bundle = jax.ShapeDtypeStruct((blocks, width + 8, width), jnp.float32)
    return pl.pallas_call(
        dense_kernel,
        out_shape=(
            bundle,
            bundle,
            jax.ShapeDtypeStruct((count, width), jnp.bfloat16),
            jax.ShapeDtypeStruct((count, width), jnp.bfloat16),
            jax.ShapeDtypeStruct((1, count), jnp.float32),
        ),
        in_specs=[pl.BlockSpec(memory_space=pltpu.SMEM)]
        + [vmem] * 3
        + [anywhere] * 2
        + [vmem] * 2,
        out_specs=(anywhere, anywhere, vmem, vmem, vmem),
        scratch_shapes=[
            pltpu.VMEM((wide, width), jnp.bfloat16),
            pltpu.VMEM((wide, width), jnp.bfloat16),
            pltpu.VMEM(bundle.shape, jnp.float32),
            pltpu.VMEM(bundle.shape, jnp.float32),
        ]
        + [pltpu.VMEM((cells, width), jnp.bfloat16)] * 3
        + [
            pltpu.VMEM((count, wide), jnp.bfloat16),
            pltpu.VMEM((count, wide), jnp.float32),
            pltpu.VMEM((count, wide), jnp.bfloat16),
            pltpu.SemaphoreType.DMA((2,)),
            pltpu.SemaphoreType.DMA((2 * blocks,)),
        ],
        compiler_params=pltpu.CompilerParams(vmem_limit_bytes=60 * 1024 * 1024),
        cost_estimate=pl.CostEstimate(flops=5_000_000_000, bytes_accessed=9_000_000, transcendentals=1000),
        name="dense",
    )(
        core[None],
        slot_ids.T,
        labels[None, :],
        cache_rows,
        proj_u,
        proj_v,
        cross_bias[None, :],
        head[None, :],
    )


def payload_kernel(
    slot_ref, evict_ref, miss_ref, accum_ref, cache_ref, out_ref, taken
):
    owners, per = taken.shape[0], out_ref.shape[0] // taken.shape[0]
    width = out_ref.shape[1]
    lane = lax.broadcasted_iota(jnp.int32, (1, width), 1)
    base = jnp.where((lane >= per) & (lane < 2 * per), -1.0, 0.0)

    def clear(o, _):
        taken[o] = 0
        out_ref[pl.ds(o * per, per - 1), :] = jnp.zeros((per - 1, width), jnp.float32)
        out_ref[pl.ds(o * per + per - 1, 1), :] = base
        return 0

    lax.fori_loop(0, owners, clear, 0, unroll=True)

    def leave(i, _):
        owner = evict_ref[0, i]
        rank = taken[owner]
        taken[owner] = rank + 1
        slot = slot_ref[i]
        out_ref[pl.ds(owner * per + rank, 1), :] = cache_ref[pl.ds(slot, 1), :]
        spot = pl.ds(owner * per + per - 1, 1)
        meta = jnp.where(lane == rank, accum_ref[slot], out_ref[spot, :])
        row = evict_ref[1, i].astype(jnp.float32)
        out_ref[spot, :] = jnp.where(lane == per + rank, row, meta)
        return 0

    lax.fori_loop(0, slot_ref.shape[0], leave, 0, unroll=8)

    def reset(o, _):
        taken[o] = 0
        return 0

    lax.fori_loop(0, owners, reset, 0, unroll=True)

    def ask(i, _):
        owner = miss_ref[0, i]
        rank = taken[owner]
        taken[owner] = rank + 1
        spot = pl.ds(owner * per + per - 1, 1)
        row = miss_ref[1, i].astype(jnp.float32)
        out_ref[spot, :] = jnp.where(lane == 2 * per + rank, row, out_ref[spot, :])
        return 0

    lax.fori_loop(0, slot_ref.shape[0], ask, 0, unroll=8)


def payload(evict_slot, evict_dest, miss_dest, cache_accum, cache_rows, owners, per):
    smem = pl.BlockSpec(memory_space=pltpu.SMEM)
    vmem = pl.BlockSpec(memory_space=pltpu.VMEM)
    return pl.pallas_call(
        payload_kernel,
        out_shape=jax.ShapeDtypeStruct((owners * per, cache_rows.shape[1]), jnp.float32),
        in_specs=[smem] * 4 + [vmem],
        out_specs=vmem,
        scratch_shapes=[pltpu.SMEM((owners,), jnp.int32)],
        cost_estimate=pl.CostEstimate(flops=100_000, bytes_accessed=1_500_000, transcendentals=0),
        name="payload",
    )(evict_slot, evict_dest.T, miss_dest.T, cache_accum, cache_rows)


def add_kernel(keep_any, came_any, out_any, keep, came, total, in_sems, out_sems):
    blocks = keep.shape[0]
    loads, stores = [], []
    for c in range(blocks):
        for k, (source, target) in enumerate(((keep_any, keep), (came_any, came))):
            loads.append(
                pltpu.make_async_copy(source.at[c], target.at[c], in_sems.at[2 * c + k])
            )
            loads[-1].start()
    for c in range(blocks):
        loads[2 * c].wait()
        loads[2 * c + 1].wait()
        total[c] = keep[c] + came[c]
        stores.append(pltpu.make_async_copy(total.at[c], out_any.at[c], out_sems.at[c]))
        stores[-1].start()
    for store in stores:
        store.wait()


def added(keep, came):
    anywhere = pl.BlockSpec(memory_space=pl.ANY)
    return pl.pallas_call(
        add_kernel,
        out_shape=jax.ShapeDtypeStruct(keep.shape, jnp.float32),
        in_specs=[anywhere, anywhere],
        out_specs=anywhere,
        scratch_shapes=[pltpu.VMEM(keep.shape, jnp.float32)] * 3
        + [
            pltpu.SemaphoreType.DMA((2 * keep.shape[0],)),
            pltpu.SemaphoreType.DMA((keep.shape[0],)),
        ],
        compiler_params=pltpu.CompilerParams(vmem_limit_bytes=44 * 1024 * 1024),
        name="add_halves",
    )(keep, came)


def refill_kernel(
    slots_ref,
    evict_ref,
    place_ref,
    cache_ref,
    accum_ref,
    latent_ref,
    dlatent_ref,
    dlogit_ref,
    u_ref,
    v_ref,
    bias_ref,
    head_ref,
    back_ref,
    rows_ref,
    accum_out,
):
    f32, bf16 = jnp.float32, jnp.bfloat16
    (cells, width), count = cache_ref.shape, latent_ref.shape[0]
    feats = u_ref.shape[0] // width
    looks = slots_ref.shape[0] // feats
    across = (((1,), (1,)), ((), ()))
    latent, dlatent = latent_ref[...], dlatent_ref[...]
    dlogit = jnp.transpose(dlogit_ref[...])
    cell = lax.broadcasted_iota(jnp.int32, (cells, count), 0)
    grad = jnp.zeros((cells, width), f32)
    for f in range(feats):
        counts = jnp.zeros((cells, count), f32)
        for look in range(looks):
            at = f * looks + look
            counts = counts + jnp.where(cell == slots_ref[at : at + 1, :], 1.0, 0.0)
        cut = slice(f * width, (f + 1) * width)
        moved = lax.dot_general(latent, u_ref[cut, :], across, preferred_element_type=f32)
        moved = moved + bias_ref[:, cut]
        through = lax.dot_general(dlatent, v_ref[cut, :], across, preferred_element_type=f32)
        dpooled = (dlogit * head_ref[:, cut] * (moved + 1.0) + through).astype(bf16)
        grad = grad + jnp.dot(counts.astype(bf16), dpooled, preferred_element_type=f32)
    mean = jnp.sum(grad * grad, axis=1, keepdims=True) / width
    accum = jnp.transpose(accum_ref[...]) + mean
    rows_ref[...] = cache_ref[...] - ETA * grad * lax.rsqrt(accum)
    accum_out[...] = jnp.transpose(accum)

    def refill(i, _):
        rows_ref[pl.ds(evict_ref[i], 1), :] = back_ref[pl.ds(place_ref[i], 1), :]
        return 0

    lax.fori_loop(0, evict_ref.shape[0], refill, 0, unroll=8)


def refilled(slot_ids, evict_slot, place, cache_rows, cache_accum, saved, params, back):
    cells = cache_rows.shape[0]
    smem = pl.BlockSpec(memory_space=pltpu.SMEM)
    vmem = pl.BlockSpec(memory_space=pltpu.VMEM)
    return pl.pallas_call(
        refill_kernel,
        out_shape=(
            jax.ShapeDtypeStruct(cache_rows.shape, jnp.float32),
            jax.ShapeDtypeStruct((1, cells), jnp.float32),
        ),
        in_specs=[vmem, smem, smem] + [vmem] * 10,
        out_specs=(vmem, vmem),
        compiler_params=pltpu.CompilerParams(vmem_limit_bytes=60 * 1024 * 1024),
        cost_estimate=pl.CostEstimate(flops=1_100_000_000, bytes_accessed=4_000_000, transcendentals=1000),
        name="refill",
    )(
        slot_ids.T,
        evict_slot,
        place,
        cache_rows,
        cache_accum[None, :],
        *saved,
        *params,
        back,
    )


def scaled(index, half_any, proj_ref, half, stage, in_sems, out_sems):
    blocks, width = half.shape[0], half.shape[2]
    loads = []
    for c in range(blocks):
        loads.append(pltpu.make_async_copy(half_any.at[c], half.at[c], in_sems.at[c]))
        loads[-1].start()
    squares = jnp.zeros((width, width), jnp.float32)
    for c in range(blocks):
        loads[c].wait()
        block = half[c, :width, :]
        squares = squares + block * block
    total = jnp.sum(jnp.sum(squares, axis=0, keepdims=True), axis=1, keepdims=True)
    scale = lax.rsqrt(total / (blocks * width * width) + EPS)
    copies = []
    for c in range(blocks):
        stage[c] = half[c, :width, :] * scale
        copies.append(
            pltpu.make_async_copy(
                stage.at[c], proj_ref.at[index, pl.ds(c * width, width), :], out_sems.at[c]
            )
        )
        copies[-1].start()
    return copies


def own_kernel(core_ref, half_any, proj_ref, half, stage, in_sems, out_sems):
    for copy in scaled(core_ref[0], half_any, proj_ref, half, stage, in_sems, out_sems):
        copy.wait()


def other_kernel(
    core_ref,
    proj_in,
    own_ref,
    half_any,
    proj_ref,
    vec_ref,
    loss_ref,
    half,
    stage,
    in_sems,
    out_sems,
):
    core = core_ref[0]
    copies = scaled(1 - core, half_any, proj_ref, half, stage, in_sems, out_sems)
    blocks, width = half.shape[0], half.shape[2]
    mine = core == 0
    own = [own_ref[c, 0:1, :] for c in range(blocks)]
    far = [half[c, width : width + 1, :] for c in range(blocks)]
    for index in (0, 1):
        rows = [jnp.where(mine, *((a, b) if index == 0 else (b, a))) for a, b in zip(own, far)]
        squares = sum(row * row for row in rows)
        total = jnp.sum(squares, axis=1, keepdims=True)
        scale = lax.rsqrt(total / (blocks * width) + EPS)
        for c in range(blocks):
            vec_ref[index : index + 1, c * width : (c + 1) * width] = rows[c] * scale
    loss_ref[...] = jnp.where(
        mine, half[0, width + 1 : width + 2, :128], own_ref[0, 1:2, :128]
    )
    for copy in copies:
        copy.wait()


def normalized(core, own, other):
    blocks, depth, width = own.shape
    wide = blocks * width
    smem = pl.BlockSpec(memory_space=pltpu.SMEM)
    vmem = pl.BlockSpec(memory_space=pltpu.VMEM)
    anywhere = pl.BlockSpec(memory_space=pl.ANY)
    scratch = [
        pltpu.VMEM((blocks, depth, width), jnp.float32),
        pltpu.VMEM((blocks, width, width), jnp.float32),
        pltpu.SemaphoreType.DMA((blocks,)),
        pltpu.SemaphoreType.DMA((blocks,)),
    ]
    proj = jax.ShapeDtypeStruct((2, wide, width), jnp.float32)
    limit = pltpu.CompilerParams(vmem_limit_bytes=16 * 1024 * 1024)
    half = pl.pallas_call(
        own_kernel,
        out_shape=proj,
        in_specs=[smem, anywhere],
        out_specs=anywhere,
        scratch_shapes=scratch,
        compiler_params=limit,
        name="scale_own",
    )(core[None], own)
    return pl.pallas_call(
        other_kernel,
        out_shape=(
            proj,
            jax.ShapeDtypeStruct((2, wide), jnp.float32),
            jax.ShapeDtypeStruct((1, 128), jnp.float32),
        ),
        in_specs=[smem, anywhere, vmem, anywhere],
        out_specs=(anywhere, vmem, vmem),
        scratch_shapes=scratch,
        input_output_aliases={1: 0},
        compiler_params=limit,
        name="scale_other",
    )(core[None], half, own[:, width:, :], other)


def shards(
    slot_ids,
    labels,
    cache_rows,
    cache_accum,
    table_rows,
    table_accum,
    miss_dest,
    evict_slot,
    evict_dest,
    proj_u,
    proj_v,
    cross_bias,
    head,
):
    owners = 32
    per = 8
    cap = 6
    width = cache_rows.shape[1]
    owned = table_rows.shape[0]
    cells = cache_rows.shape[0]
    spots = owners * per
    core = lax.axis_index("table") % 2

    me = lax.axis_index("table")
    sent = payload(
        evict_slot, evict_dest, miss_dest, cache_accum, cache_rows, owners, per
    ).reshape(owners, per, width)
    sent, slots_late = lax.optimization_barrier((sent, slot_ids))
    got = lax.all_to_all(sent, "table", split_axis=0, concat_axis=0, tiled=True)

    count = slot_ids.shape[0]
    feats = proj_u.shape[0] // width
    keep, send, *saved = dense(
        core, slots_late, labels, cache_rows, proj_u, proj_v, cross_bias, head
    )

    blocks = feats
    depth = width
    send, got = lax.optimization_barrier((send, got))
    held = added(keep, swap_cores(send))
    held, got = lax.optimization_barrier((held, got))

    got_meta = got[:, per - 1, :]
    got_id = got_meta[:, per : per + cap].astype(jnp.int32)
    flat = got_id.reshape(-1)
    table_new = table_rows.at[jnp.where(flat < 0, owned, flat)].set(
        got[:, :cap, :].reshape(-1, width), mode="drop"
    )
    stored = flat[:, None] == jnp.arange(owned, dtype=jnp.int32)[None, :]
    stored_sum = jnp.sum(jnp.where(stored, got_meta[:, :cap].reshape(-1)[:, None], 0.0), axis=0)
    accum_table = jnp.where(jnp.any(stored, axis=0), stored_sum, table_accum)
    order = jnp.arange(owners, dtype=jnp.int32)
    turned = (order ^ me)[:, None] == order[None, :]
    asked = jnp.sum(
        jnp.where(turned[:, :, None], got_meta[None, :, 2 * per : 3 * per], 0.0), axis=1
    )
    asked = asked.astype(jnp.int32).reshape(-1)
    is_meta = (jnp.arange(per) == per - 1)[None, :, None]
    reply_rows = jnp.take(table_new, asked, axis=0, mode="clip").reshape(owners, per, width)
    reply_accum = picked(accum_table, asked).reshape(owners, per)
    back = jnp.where(is_meta, meta_row([reply_accum], width), reply_rows)

    held = exchange(held, first_groups())
    back = cross(cross(back, 1), 16)
    held, back = lax.optimization_barrier((held, back))
    held = jnp.sum(held, axis=0)
    fine = depth // 16
    pieces16 = jnp.concatenate(
        [
            held[:depth].reshape(16, fine, width),
            jnp.broadcast_to(held[None, depth:], (16, 8, width)),
        ],
        axis=1,
    )
    held = exchange(pieces16, second_groups())
    back = cross_z(back)
    held, back = lax.optimization_barrier((held, back))
    summed16 = jnp.sum(held, axis=0)
    extras = summed16[fine:]
    spread = jnp.broadcast_to(summed16[None, :fine], (16, fine, width))
    held = exchange(spread, second_groups())
    whole = jnp.concatenate([held.reshape(depth, width), extras], axis=0)
    whole = exchange(jnp.broadcast_to(whole[None], (blocks, depth + 8, width)), first_groups())
    in_place = (miss_dest[:, 0] ^ me) * per + ranks(miss_dest[:, 0])
    rows_new, accum_new = refilled(
        slot_ids,
        evict_slot,
        in_place,
        cache_rows,
        cache_accum,
        saved,
        (proj_u, proj_v, cross_bias[None, :], head[None, :]),
        back.reshape(spots, width),
    )
    fetched_accum = picked(back[:, per - 1, :per].reshape(-1), in_place)
    filled = evict_slot[:, None] == jnp.arange(cells, dtype=jnp.int32)[None, :]
    filled_sum = jnp.sum(jnp.where(filled, fetched_accum[:, None], 0.0), axis=0)
    accum_new = jnp.where(jnp.any(filled, axis=0), filled_sum, accum_new.reshape(cells))
    whole, rows_new, accum_new = lax.optimization_barrier((whole, rows_new, accum_new))
    clipped_proj, clipped_vecs, loss_row = normalized(core, whole, swap_cores(whole))
    loss = loss_row[0, 0] / (count * 256)
    return (rows_new, accum_new, table_new, accum_table, clipped_proj, clipped_vecs, loss)


def solution(mesh):
    split = P(AXES)
    rows = P(AXES, None)
    return jax.shard_map(
        shards,
        mesh=mesh,
        in_specs=(
            rows,
            split,
            rows,
            split,
            rows,
            split,
            rows,
            split,
            rows,
            P(),
            P(),
            P(),
            P(),
        ),
        out_specs=(rows, split, rows, split, P(), P(), P()),
        check_vma=False,
    )
```

```python
import jax
import jax.numpy as jnp
from jax import lax
from jax.experimental import pallas as pl
from jax.experimental.pallas import tpu as pltpu
from jax.sharding import PartitionSpec as P

EPS = 1e-06
ETA = 0.05
AXES = ("trainer", "table")


def device_at(y, x, z, core):
    return (((y // 2 * 4 + x) * 2 + y % 2) * 8 + z % 8) * 2 + core


def first_groups():
    groups = []
    for y in range(4):
        for pair in range(4):
            groups.append([device_at(y, x, 2 * pair + b, 0) for x in range(4) for b in range(2)])
    for x in range(4):
        for pair in range(4):
            groups.append([device_at(y, x, 2 * pair + 1 + b, 1) for y in range(4) for b in range(2)])
    return groups


def second_groups():
    groups = []
    for x in range(4):
        for b in range(2):
            groups.append([device_at(y, x, 2 * k + b, 0) for y in range(4) for k in range(4)])
    for y in range(4):
        for b in range(2):
            groups.append([device_at(y, x, 2 * k + b, 1) for x in range(4) for k in range(4)])
    return groups


def swap_cores(value):
    return lax.ppermute(value, AXES, [(i, i ^ 1) for i in range(256)])


def exchange(value, groups):
    return lax.all_to_all(
        value, AXES, split_axis=0, concat_axis=0, tiled=True, axis_index_groups=groups
    )


def ranks(owner):
    listed = owner.shape[0]
    order = jnp.arange(listed, dtype=jnp.int32)
    earlier = (owner[:, None] == owner[None, :]) & (order[None, :] < order[:, None])
    return jnp.sum(earlier.astype(jnp.int32), axis=1)


def meta_row(columns, width):
    block = jnp.concatenate(columns, axis=1)
    return jnp.pad(block, ((0, 0), (0, width - block.shape[1])))[:, None, :]


def picked(values, index):
    hit = index[:, None] == jnp.arange(values.shape[0], dtype=jnp.int32)[None, :]
    return jnp.sum(jnp.where(hit, values[None, :], 0.0), axis=1)


def cross(value, bit):
    split = value.reshape(value.shape[0] // (2 * bit), 2, bit, *value.shape[1:])
    there = [(i, i ^ bit) for i in range(256)]
    came = lax.ppermute(split[:, 1], AXES, there)
    return jnp.stack([split[:, 0], came], axis=1).reshape(value.shape)


def dense_kernel(
    core_ref,
    slots_ref,
    labels_ref,
    cache_any,
    u_any,
    v_any,
    bias_ref,
    head_ref,
    send_out,
    left_out,
    latent_ref,
    dlatent_ref,
    dlogit_ref,
    extra_ref,
    cache,
    u_ref,
    v_ref,
    send_ref,
    left,
    high,
    mid,
    low,
    pooled,
    shifted,
    dlift,
    in_sems,
    out_sems,
):
    f32, bf16 = jnp.float32, jnp.bfloat16
    count, (cells, width) = slots_ref.shape[1], cache.shape
    feats = u_ref.shape[0] // width
    looks = slots_ref.shape[0] // feats
    cuts = [slice(c * width, (c + 1) * width) for c in range(feats)]
    loads = []
    for source, target in ((cache_any, cache), (v_any, v_ref), (u_any, u_ref)):
        step = target.shape[0] // 4
        for part in range(4):
            rows = pl.ds(part * step, step)
            loads.append(
                pltpu.make_async_copy(source.at[rows], target.at[rows], in_sems.at[len(loads)])
            )
            loads[-1].start()
    slots = jnp.transpose(slots_ref[...])
    lane = lax.broadcasted_iota(jnp.int32, (count, cells), 1)

    def counted(f):
        counts = jnp.zeros((count, cells), f32)
        for look in range(looks):
            at = f * looks + look
            counts = counts + jnp.where(lane == slots[:, at : at + 1], 1.0, 0.0)
        return counts.astype(bf16)

    counts = counted(0)
    step = cells // 4
    for part in range(4):
        loads[part].wait()
        rows = cache[part * step : (part + 1) * step, :]
        first = rows.astype(bf16)
        rest = rows - first.astype(f32)
        second = rest.astype(bf16)
        high[part * step : (part + 1) * step, :] = first
        mid[part * step : (part + 1) * step, :] = second
        low[part * step : (part + 1) * step, :] = (rest - second.astype(f32)).astype(bf16)
    for f in range(feats):
        if f > 0:
            counts = counted(f)
        total = jnp.dot(counts, low[...], preferred_element_type=f32)
        total = total + jnp.dot(counts, mid[...], preferred_element_type=f32)
        total = total + jnp.dot(counts, high[...], preferred_element_type=f32)
        pooled[:, cuts[f]] = total.astype(bf16)

    for load in loads[4:]:
        load.wait()
    latent = jnp.dot(pooled[...], v_ref[...], preferred_element_type=f32).astype(bf16)
    latent_ref[...] = latent
    across = (((1,), (1,)), ((), ()))
    logit_wide = jnp.zeros((count, width), f32)
    for cut in cuts:
        moved = lax.dot_general(latent, u_ref[cut, :], across, preferred_element_type=f32)
        moved = moved + bias_ref[:, cut]
        shifted[:, cut] = moved
        part = pooled[:, cut].astype(f32)
        logit_wide = logit_wide + (part * moved + part) * head_ref[:, cut]
    logit = jnp.sum(logit_wide, axis=1, keepdims=True)
    target = jnp.transpose(labels_ref[...]).astype(f32)
    small = jnp.exp(-jnp.abs(logit))
    losses = jnp.maximum(logit, 0.0) + jnp.log1p(small) - target * logit
    loss = jnp.sum(losses, axis=0, keepdims=True)
    dlogit = jnp.where(logit >= 0, 1.0, small) / (1.0 + small) - target
    dlogit_ref[...] = jnp.transpose(dlogit)

    mine = core_ref[0] == 0
    lane1 = lax.broadcasted_iota(jnp.int32, (1, width), 1)
    loss_row = jnp.where(lane1 == 0, loss, 0.0)
    back = jnp.zeros((count, width), f32)
    for c, cut in enumerate(cuts):
        part = pooled[:, cut].astype(f32)
        lift = dlogit * head_ref[:, cut] * part
        crossed = part * shifted[:, cut] + part
        dbias = jnp.sum(lift, axis=0, keepdims=True)
        dhead = jnp.sum(dlogit * crossed, axis=0, keepdims=True)
        lift = lift.astype(bf16)
        dlift[:, cut] = lift
        back = back + jnp.dot(lift, u_ref[cut, :], preferred_element_type=f32)
        extra_ref[c, 0:1, :] = jnp.where(mine, dbias, dhead)
        extra_ref[c, 1:2, :] = loss_row
        extra_ref[c, 2:8, :] = jnp.zeros((6, width), f32)
        send_ref[c, width : width + 1, :] = jnp.where(mine, dhead, dbias)
        send_ref[c, width + 1 : width + 2, :] = loss_row
        send_ref[c, width + 2 : width + 8, :] = jnp.zeros((6, width), f32)
        left[:, cut] = jnp.where(mine, lift, pooled[:, cut])
    dlatent = back.astype(bf16)
    dlatent_ref[...] = dlatent
    copies = [pltpu.make_async_copy(left, left_out, out_sems.at[feats])]
    copies[0].start()
    right = jnp.where(mine, dlatent, latent)
    for c, cut in enumerate(cuts):
        send_ref[c, :width, :] = lax.dot_general(
            jnp.where(mine, pooled[:, cut], dlift[:, cut]),
            right,
            (((0,), (0,)), ((), ())),
            preferred_element_type=f32,
        )
        copies.append(pltpu.make_async_copy(send_ref.at[c], send_out.at[c], out_sems.at[c]))
        copies[-1].start()
    for copy in copies:
        copy.wait()


def dense(core, slot_ids, labels, cache_rows, proj_u, proj_v, cross_bias, head):
    count, (cells, width) = slot_ids.shape[0], cache_rows.shape
    wide = proj_u.shape[0]
    blocks = wide // width
    f32, bf16 = jnp.float32, jnp.bfloat16
    vmem = pl.BlockSpec(memory_space=pltpu.VMEM)
    anywhere = pl.BlockSpec(memory_space=pl.ANY)
    bundle = (blocks, width + 8, width)
    return pl.pallas_call(
        dense_kernel,
        out_shape=(
            jax.ShapeDtypeStruct(bundle, f32),
            jax.ShapeDtypeStruct((count, wide), bf16),
            jax.ShapeDtypeStruct((count, width), bf16),
            jax.ShapeDtypeStruct((count, width), bf16),
            jax.ShapeDtypeStruct((1, count), f32),
            jax.ShapeDtypeStruct((blocks, 8, width), f32),
        ),
        in_specs=[pl.BlockSpec(memory_space=pltpu.SMEM)]
        + [vmem] * 2
        + [anywhere] * 3
        + [vmem] * 2,
        out_specs=[anywhere] * 2 + [vmem] * 4,
        scratch_shapes=[
            pltpu.VMEM((cells, width), f32),
            pltpu.VMEM((wide, width), bf16),
            pltpu.VMEM((wide, width), bf16),
            pltpu.VMEM(bundle, f32),
            pltpu.VMEM((count, wide), bf16),
        ]
        + [pltpu.VMEM((cells, width), bf16)] * 3
        + [
            pltpu.VMEM((count, wide), bf16),
            pltpu.VMEM((count, wide), f32),
            pltpu.VMEM((count, wide), bf16),
            pltpu.SemaphoreType.DMA((12,)),
            pltpu.SemaphoreType.DMA((blocks + 1,)),
        ],
        compiler_params=pltpu.CompilerParams(vmem_limit_bytes=60 * 1024 * 1024),
        cost_estimate=pl.CostEstimate(
            flops=5_000_000_000, bytes_accessed=9_000_000, transcendentals=1000
        ),
        name="dense",
    )(
        core[None],
        slot_ids.T,
        labels[None, :],
        cache_rows,
        proj_u,
        proj_v,
        cross_bias[None, :],
        head[None, :],
    )


def keep_kernel(core_ref, left_ref, latent_ref, dlatent_ref, extra_ref, keep_ref):
    width = latent_ref.shape[1]
    right = jnp.where(core_ref[0] == 0, latent_ref[...], dlatent_ref[...])
    for c in range(keep_ref.shape[0]):
        keep_ref[c, :width, :] = lax.dot_general(
            left_ref[:, c * width : (c + 1) * width],
            right,
            (((0,), (0,)), ((), ())),
            preferred_element_type=jnp.float32,
        )
        keep_ref[c, width : width + 8, :] = extra_ref[c]


def kept(core, left, latent, dlatent, extra):
    blocks, _, width = extra.shape
    vmem = pl.BlockSpec(memory_space=pltpu.VMEM)
    return pl.pallas_call(
        keep_kernel,
        out_shape=jax.ShapeDtypeStruct((blocks, width + 8, width), jnp.float32),
        in_specs=[pl.BlockSpec(memory_space=pltpu.SMEM)] + [vmem] * 4,
        out_specs=vmem,
        compiler_params=pltpu.CompilerParams(vmem_limit_bytes=16 * 1024 * 1024),
        cost_estimate=pl.CostEstimate(
            flops=300_000_000, bytes_accessed=4_000_000, transcendentals=0
        ),
        name="kept",
    )(core[None], left, latent, dlatent, extra)


def payload_kernel(
    slot_ref, evict_ref, miss_ref, accum_ref, cache_any, out_ref, taken, place, cache, sems
):
    owners, per = taken.shape[0], out_ref.shape[0] // taken.shape[0]
    width = out_ref.shape[1]
    listed = slot_ref.shape[0]
    step = cache.shape[0] // 4
    loads = []
    for part in range(4):
        rows = pl.ds(part * step, step)
        loads.append(pltpu.make_async_copy(cache_any.at[rows], cache.at[rows], sems.at[part]))
        loads[-1].start()
    lane = lax.broadcasted_iota(jnp.int32, (1, width), 1)
    base = jnp.where((lane >= per) & (lane < 2 * per), -1.0, 0.0)
    for o in range(owners):
        taken[o] = 0
        out_ref[o * per : o * per + per - 1, :] = jnp.zeros((per - 1, width), jnp.float32)
        out_ref[o * per + per - 1 : (o + 1) * per, :] = base

    def leave(i, _):
        owner = evict_ref[0, i]
        rank = taken[owner]
        taken[owner] = rank + 1
        place[i] = owner * per + rank
        spot = pl.ds(owner * per + per - 1, 1)
        meta = jnp.where(lane == rank, accum_ref[slot_ref[i]], out_ref[spot, :])
        row = evict_ref[1, i].astype(jnp.float32)
        out_ref[spot, :] = jnp.where(lane == per + rank, row, meta)
        return 0

    lax.fori_loop(0, listed, leave, 0, unroll=8)
    for o in range(owners):
        taken[o] = 0

    def ask(i, _):
        owner = miss_ref[0, i]
        rank = taken[owner]
        taken[owner] = rank + 1
        spot = pl.ds(owner * per + per - 1, 1)
        row = miss_ref[1, i].astype(jnp.float32)
        out_ref[spot, :] = jnp.where(lane == 2 * per + rank, row, out_ref[spot, :])
        return 0

    lax.fori_loop(0, listed, ask, 0, unroll=8)
    for load in loads:
        load.wait()

    def move(i, _):
        out_ref[pl.ds(place[i], 1), :] = cache[pl.ds(slot_ref[i], 1), :]
        return 0

    lax.fori_loop(0, listed, move, 0, unroll=8)


def payload(evict_slot, evict_dest, miss_dest, cache_accum, cache_rows, owners, per):
    smem = pl.BlockSpec(memory_space=pltpu.SMEM)
    return pl.pallas_call(
        payload_kernel,
        out_shape=jax.ShapeDtypeStruct((owners * per, cache_rows.shape[1]), jnp.float32),
        in_specs=[smem] * 4 + [pl.BlockSpec(memory_space=pl.ANY)],
        out_specs=pl.BlockSpec(memory_space=pltpu.VMEM),
        scratch_shapes=[
            pltpu.SMEM((owners,), jnp.int32),
            pltpu.SMEM(evict_slot.shape, jnp.int32),
            pltpu.VMEM(cache_rows.shape, jnp.float32),
            pltpu.SemaphoreType.DMA((4,)),
        ],
        compiler_params=pltpu.CompilerParams(vmem_limit_bytes=60 * 1024 * 1024),
        cost_estimate=pl.CostEstimate(flops=100_000, bytes_accessed=1_500_000, transcendentals=0),
        name="payload",
    )(evict_slot, evict_dest.T, miss_dest.T, cache_accum, cache_rows)


def update_kernel(
    slots_ref,
    cache_ref,
    accum_ref,
    latent_ref,
    dlatent_ref,
    dlogit_ref,
    u_ref,
    v_ref,
    bias_ref,
    head_ref,
    rows_ref,
    accum_out,
):
    f32, bf16 = jnp.float32, jnp.bfloat16
    (cells, width), count = cache_ref.shape, latent_ref.shape[0]
    feats = u_ref.shape[0] // width
    looks = slots_ref.shape[0] // feats
    across = (((1,), (1,)), ((), ()))
    latent, dlatent = latent_ref[...], dlatent_ref[...]
    dlogit = jnp.transpose(dlogit_ref[...])
    cell = lax.broadcasted_iota(jnp.int32, (cells, count), 0)
    grad = jnp.zeros((cells, width), f32)
    for f in range(feats):
        counts = jnp.zeros((cells, count), f32)
        for look in range(looks):
            at = f * looks + look
            counts = counts + jnp.where(cell == slots_ref[at : at + 1, :], 1.0, 0.0)
        cut = slice(f * width, (f + 1) * width)
        moved = lax.dot_general(latent, u_ref[cut, :], across, preferred_element_type=f32)
        moved = moved + bias_ref[:, cut]
        through = lax.dot_general(dlatent, v_ref[cut, :], across, preferred_element_type=f32)
        dpooled = (dlogit * head_ref[:, cut] * (moved + 1.0) + through).astype(bf16)
        grad = grad + jnp.dot(counts.astype(bf16), dpooled, preferred_element_type=f32)
    mean = jnp.sum(grad * grad, axis=1, keepdims=True) / width
    accum = jnp.transpose(accum_ref[...]) + mean
    rows_ref[...] = cache_ref[...] - ETA * grad * lax.rsqrt(accum)
    accum_out[...] = jnp.transpose(accum)


def refill_kernel(evict_ref, place_ref, back_ref, old_ref, rows_ref):
    rows_ref[...] = old_ref[...]

    def refill(i, _):
        rows_ref[pl.ds(evict_ref[i], 1), :] = back_ref[pl.ds(place_ref[i], 1), :]
        return 0

    lax.fori_loop(0, evict_ref.shape[0], refill, 0, unroll=8)


def updated(slot_ids, cache_rows, cache_accum, saved, params):
    cells = cache_rows.shape[0]
    vmem = pl.BlockSpec(memory_space=pltpu.VMEM)
    return pl.pallas_call(
        update_kernel,
        out_shape=(
            jax.ShapeDtypeStruct(cache_rows.shape, jnp.float32),
            jax.ShapeDtypeStruct((1, cells), jnp.float32),
        ),
        in_specs=[vmem] * 10,
        out_specs=(vmem, vmem),
        compiler_params=pltpu.CompilerParams(vmem_limit_bytes=60 * 1024 * 1024),
        cost_estimate=pl.CostEstimate(
            flops=1_100_000_000, bytes_accessed=4_000_000, transcendentals=1000
        ),
        name="update",
    )(slot_ids.T, cache_rows, cache_accum[None, :], *saved, *params)


def refilled(evict_slot, place, back, rows):
    smem = pl.BlockSpec(memory_space=pltpu.SMEM)
    vmem = pl.BlockSpec(memory_space=pltpu.VMEM)
    return pl.pallas_call(
        refill_kernel,
        out_shape=jax.ShapeDtypeStruct(rows.shape, jnp.float32),
        in_specs=[smem, smem, vmem, vmem],
        out_specs=vmem,
        compiler_params=pltpu.CompilerParams(vmem_limit_bytes=60 * 1024 * 1024),
        cost_estimate=pl.CostEstimate(flops=100_000, bytes_accessed=2_000_000, transcendentals=0),
        name="refill",
    )(evict_slot, place, back, rows)


def scaled(index, half_any, proj_ref, half, stage, in_sems, out_sems):
    blocks, width = half.shape[0], half.shape[2]
    loads = []
    for c in range(blocks):
        loads.append(pltpu.make_async_copy(half_any.at[c], half.at[c], in_sems.at[c]))
        loads[-1].start()
    squares = jnp.zeros((width, width), jnp.float32)
    for c in range(blocks):
        loads[c].wait()
        block = half[c, :width, :]
        squares = squares + block * block
    total = jnp.sum(jnp.sum(squares, axis=0, keepdims=True), axis=1, keepdims=True)
    scale = lax.rsqrt(total / (blocks * width * width) + EPS)
    copies = []
    for c in range(blocks):
        stage[c] = half[c, :width, :] * scale
        copies.append(
            pltpu.make_async_copy(
                stage.at[c], proj_ref.at[index, pl.ds(c * width, width), :], out_sems.at[c]
            )
        )
        copies[-1].start()
    return copies


def own_kernel(core_ref, half_any, proj_ref, half, stage, in_sems, out_sems):
    for copy in scaled(core_ref[0], half_any, proj_ref, half, stage, in_sems, out_sems):
        copy.wait()


def other_kernel(
    core_ref,
    proj_in,
    own_ref,
    half_any,
    proj_ref,
    vec_ref,
    loss_ref,
    half,
    stage,
    in_sems,
    out_sems,
):
    core = core_ref[0]
    copies = scaled(1 - core, half_any, proj_ref, half, stage, in_sems, out_sems)
    blocks, width = half.shape[0], half.shape[2]
    mine = core == 0
    own = [own_ref[c, 0:1, :] for c in range(blocks)]
    far = [half[c, width : width + 1, :] for c in range(blocks)]
    for index in (0, 1):
        rows = [jnp.where(mine, *((a, b) if index == 0 else (b, a))) for a, b in zip(own, far)]
        squares = sum(row * row for row in rows)
        total = jnp.sum(squares, axis=1, keepdims=True)
        scale = lax.rsqrt(total / (blocks * width) + EPS)
        for c in range(blocks):
            vec_ref[index : index + 1, c * width : (c + 1) * width] = rows[c] * scale
    loss_ref[...] = jnp.where(
        mine, half[0, width + 1 : width + 2, :128], own_ref[0, 1:2, :128]
    )
    for copy in copies:
        copy.wait()


def normalized(core, own, other):
    blocks, depth, width = own.shape
    wide = blocks * width
    smem = pl.BlockSpec(memory_space=pltpu.SMEM)
    vmem = pl.BlockSpec(memory_space=pltpu.VMEM)
    anywhere = pl.BlockSpec(memory_space=pl.ANY)
    scratch = [
        pltpu.VMEM((blocks, depth, width), jnp.float32),
        pltpu.VMEM((blocks, width, width), jnp.float32),
        pltpu.SemaphoreType.DMA((blocks,)),
        pltpu.SemaphoreType.DMA((blocks,)),
    ]
    proj = jax.ShapeDtypeStruct((2, wide, width), jnp.float32)
    limit = pltpu.CompilerParams(vmem_limit_bytes=16 * 1024 * 1024)
    half = pl.pallas_call(
        own_kernel,
        out_shape=proj,
        in_specs=[smem, anywhere],
        out_specs=anywhere,
        scratch_shapes=scratch,
        compiler_params=limit,
        name="scale_own",
    )(core[None], own)
    return pl.pallas_call(
        other_kernel,
        out_shape=(
            proj,
            jax.ShapeDtypeStruct((2, wide), jnp.float32),
            jax.ShapeDtypeStruct((1, 128), jnp.float32),
        ),
        in_specs=[smem, anywhere, vmem, anywhere],
        out_specs=(anywhere, vmem, vmem),
        scratch_shapes=scratch,
        input_output_aliases={1: 0},
        compiler_params=limit,
        name="scale_other",
    )(core[None], half, own[:, width:, :], other)


def shards(
    slot_ids,
    labels,
    cache_rows,
    cache_accum,
    table_rows,
    table_accum,
    miss_dest,
    evict_slot,
    evict_dest,
    proj_u,
    proj_v,
    cross_bias,
    head,
):
    owners = 32
    per = 8
    cap = 6
    width = cache_rows.shape[1]
    owned = table_rows.shape[0]
    cells = cache_rows.shape[0]
    spots = owners * per
    core = lax.axis_index("table") % 2

    me = lax.axis_index("table")
    sent = payload(
        evict_slot, evict_dest, miss_dest, cache_accum, cache_rows, owners, per
    ).reshape(owners, per, width)
    sent, slots_late = lax.optimization_barrier((sent, slot_ids))
    got = lax.all_to_all(sent, "table", split_axis=0, concat_axis=0, tiled=True)

    count = slot_ids.shape[0]
    feats = proj_u.shape[0] // width
    send, left, latent, dlatent, dlogit, extra = dense(
        core, slots_late, labels, cache_rows, proj_u, proj_v, cross_bias, head
    )

    blocks = feats
    depth = width
    send, got = lax.optimization_barrier((send, got))
    held = kept(core, left, latent, dlatent, extra) + swap_cores(send)
    held, got = lax.optimization_barrier((held, got))

    got_meta = got[:, per - 1, :]
    got_id = got_meta[:, per : per + cap].astype(jnp.int32)
    flat = got_id.reshape(-1)
    table_new = table_rows.at[jnp.where(flat < 0, owned, flat)].set(
        got[:, :cap, :].reshape(-1, width), mode="drop"
    )
    stored = flat[:, None] == jnp.arange(owned, dtype=jnp.int32)[None, :]
    stored_sum = jnp.sum(jnp.where(stored, got_meta[:, :cap].reshape(-1)[:, None], 0.0), axis=0)
    accum_table = jnp.where(jnp.any(stored, axis=0), stored_sum, table_accum)
    order = jnp.arange(owners, dtype=jnp.int32)
    turned = (order ^ me)[:, None] == order[None, :]
    asked = jnp.sum(
        jnp.where(turned[:, :, None], got_meta[None, :, 2 * per : 3 * per], 0.0), axis=1
    )
    asked = asked.astype(jnp.int32).reshape(-1)
    is_meta = (jnp.arange(per) == per - 1)[None, :, None]
    reply_rows = jnp.take(table_new, asked, axis=0, mode="clip").reshape(owners, per, width)
    reply_accum = picked(accum_table, asked).reshape(owners, per)
    back = jnp.where(is_meta, meta_row([reply_accum], width), reply_rows)

    held = exchange(held, first_groups())
    back = cross(cross(back, 1), 8)
    held, back = lax.optimization_barrier((held, back))
    held = jnp.sum(held, axis=0)
    fine = depth // 16
    pieces16 = jnp.concatenate(
        [
            held[:depth].reshape(16, fine, width),
            jnp.broadcast_to(held[None, depth:], (16, 8, width)),
        ],
        axis=1,
    )
    held = exchange(pieces16, second_groups())
    back = cross(back, 2)
    rows_new, accum_new = updated(
        slot_ids,
        cache_rows,
        cache_accum,
        (latent, dlatent, dlogit),
        (proj_u, proj_v, cross_bias[None, :], head[None, :]),
    )
    held, back, rows_new, accum_new = lax.optimization_barrier(
        (held, back, rows_new, accum_new)
    )
    summed16 = jnp.sum(held, axis=0)
    extras = summed16[fine:]
    spread = jnp.broadcast_to(summed16[None, :fine], (16, fine, width))
    held = exchange(spread, second_groups())
    back = cross(back, 16)
    held, back = lax.optimization_barrier((held, back))
    whole = jnp.concatenate([held.reshape(depth, width), extras], axis=0)
    whole = exchange(jnp.broadcast_to(whole[None], (blocks, depth + 8, width)), first_groups())
    in_place = (miss_dest[:, 0] ^ me) * per + ranks(miss_dest[:, 0])
    back = cross(back, 4)
    rows_new = refilled(evict_slot, in_place, back.reshape(spots, width), rows_new)
    fetched_accum = picked(back[:, per - 1, :per].reshape(-1), in_place)
    filled = evict_slot[:, None] == jnp.arange(cells, dtype=jnp.int32)[None, :]
    filled_sum = jnp.sum(jnp.where(filled, fetched_accum[:, None], 0.0), axis=0)
    accum_new = jnp.where(jnp.any(filled, axis=0), filled_sum, accum_new.reshape(cells))
    whole, rows_new, accum_new = lax.optimization_barrier((whole, rows_new, accum_new))
    clipped_proj, clipped_vecs, loss_row = normalized(core, whole, swap_cores(whole))
    loss = loss_row[0, 0] / (count * 256)
    return (rows_new, accum_new, table_new, accum_table, clipped_proj, clipped_vecs, loss)


def solution(mesh):
    split = P(AXES)
    rows = P(AXES, None)
    return jax.shard_map(
        shards,
        mesh=mesh,
        in_specs=(
            rows,
            split,
            rows,
            split,
            rows,
            split,
            rows,
            split,
            rows,
            P(),
            P(),
            P(),
            P(),
        ),
        out_specs=(rows, split, rows, split, P(), P(), P()),
        check_vma=False,
    )
```

```python
import jax
import jax.numpy as jnp
from jax import lax
from jax.experimental import pallas as pl
from jax.experimental.pallas import tpu as pltpu
from jax.sharding import PartitionSpec as P

EPS = 1e-06
ETA = 0.05
AXES = ("trainer", "table")


def device_at(y, x, z, core):
    return (((y // 2 * 4 + x) * 2 + y % 2) * 8 + z % 8) * 2 + core


def first_groups():
    groups = []
    for y in range(4):
        for pair in range(4):
            groups.append([device_at(y, x, 2 * pair + b, 0) for x in range(4) for b in range(2)])
    for x in range(4):
        for pair in range(4):
            groups.append([device_at(y, x, 2 * pair + 1 + b, 1) for y in range(4) for b in range(2)])
    return groups


def second_groups():
    groups = []
    for x in range(4):
        for b in range(2):
            groups.append([device_at(y, x, 2 * k + b, 0) for y in range(4) for k in range(4)])
    for y in range(4):
        for b in range(2):
            groups.append([device_at(y, x, 2 * k + b, 1) for x in range(4) for k in range(4)])
    return groups


def swap_cores(value):
    return lax.ppermute(value, AXES, [(i, i ^ 1) for i in range(256)])


def exchange(value, groups):
    return lax.all_to_all(
        value, AXES, split_axis=0, concat_axis=0, tiled=True, axis_index_groups=groups
    )


def ranks(owner):
    listed = owner.shape[0]
    order = jnp.arange(listed, dtype=jnp.int32)
    earlier = (owner[:, None] == owner[None, :]) & (order[None, :] < order[:, None])
    return jnp.sum(earlier.astype(jnp.int32), axis=1)


def picked(values, index):
    hit = index[:, None] == jnp.arange(values.shape[0], dtype=jnp.int32)[None, :]
    return jnp.sum(jnp.where(hit, values[None, :], 0.0), axis=1)


def pool_kernel(slots_ref, cache_any, pooled_out, cache, high, mid, low, pooled, in_sems, out_sems):
    f32, bf16 = jnp.float32, jnp.bfloat16
    count, (cells, width) = slots_ref.shape[1], cache.shape
    feats = pooled.shape[0]
    looks = slots_ref.shape[0] // feats
    loads = []
    step = cells // 4
    for part in range(4):
        rows = pl.ds(part * step, step)
        loads.append(pltpu.make_async_copy(cache_any.at[rows], cache.at[rows], in_sems.at[part]))
        loads[-1].start()
    slots = jnp.transpose(slots_ref[...])
    lane = lax.broadcasted_iota(jnp.int32, (count, cells), 1)

    def counted(f):
        counts = jnp.zeros((count, cells), f32)
        for look in range(looks):
            at = f * looks + look
            counts = counts + jnp.where(lane == slots[:, at : at + 1], 1.0, 0.0)
        return counts.astype(bf16)

    counts = counted(0)
    for part in range(4):
        loads[part].wait()
        rows = cache[part * step : (part + 1) * step, :]
        first = rows.astype(bf16)
        rest = rows - first.astype(f32)
        second = rest.astype(bf16)
        high[part * step : (part + 1) * step, :] = first
        mid[part * step : (part + 1) * step, :] = second
        low[part * step : (part + 1) * step, :] = (rest - second.astype(f32)).astype(bf16)
    copies = []
    for f in range(feats):
        if f > 0:
            counts = counted(f)
        total = jnp.dot(counts, low[...], preferred_element_type=f32)
        total = total + jnp.dot(counts, mid[...], preferred_element_type=f32)
        total = total + jnp.dot(counts, high[...], preferred_element_type=f32)
        pooled[f] = total.astype(bf16)
        copies.append(pltpu.make_async_copy(pooled.at[f], pooled_out.at[f], out_sems.at[f]))
        copies[-1].start()
    for copy in copies:
        copy.wait()

def pool(slot_ids, cache_rows, feats):
    count, (cells, width) = slot_ids.shape[0], cache_rows.shape
    f32, bf16 = jnp.float32, jnp.bfloat16
    anywhere = pl.BlockSpec(memory_space=pl.ANY)
    return pl.pallas_call(
        pool_kernel,
        out_shape=jax.ShapeDtypeStruct((feats, count, width), bf16),
        in_specs=[pl.BlockSpec(memory_space=pltpu.VMEM), anywhere],
        out_specs=anywhere,
        scratch_shapes=[pltpu.VMEM((cells, width), f32)]
        + [pltpu.VMEM((cells, width), bf16)] * 3
        + [
            pltpu.VMEM((feats, count, width), bf16),
            pltpu.SemaphoreType.DMA((4,)),
            pltpu.SemaphoreType.DMA((feats,)),
        ],
        compiler_params=pltpu.CompilerParams(vmem_limit_bytes=60 * 1024 * 1024),
        cost_estimate=pl.CostEstimate(
            flops=3_200_000_000, bytes_accessed=2_000_000, transcendentals=0
        ),
        name="pool",
    )(slot_ids.T, cache_rows)


def dense_kernel(
    core_ref,
    labels_ref,
    pooled_any,
    u_any,
    v_any,
    bias_ref,
    head_ref,
    send_out,
    left_out,
    latent_ref,
    dlatent_ref,
    dlogit_ref,
    extra_ref,
    u_ref,
    v_ref,
    send_ref,
    left,
    pooled,
    shifted,
    dlift,
    in_sems,
    out_sems,
):
    f32, bf16 = jnp.float32, jnp.bfloat16
    feats, count, width = pooled.shape
    cuts = [slice(c * width, (c + 1) * width) for c in range(feats)]
    loads = []
    for c, cut in enumerate(cuts):
        rows = pl.ds(c * width, width)
        for k, (source, target) in enumerate(
            (
                (pooled_any.at[c], pooled.at[c]),
                (v_any.at[rows], v_ref.at[rows]),
                (u_any.at[rows], u_ref.at[rows]),
            )
        ):
            loads.append(pltpu.make_async_copy(source, target, in_sems.at[3 * c + k]))
            loads[-1].start()
    forward = jnp.zeros((count, width), f32)
    for c, cut in enumerate(cuts):
        loads[3 * c].wait()
        loads[3 * c + 1].wait()
        forward = forward + jnp.dot(pooled[c], v_ref[cut, :], preferred_element_type=f32)
    latent = forward.astype(bf16)
    for c in range(feats):
        loads[3 * c + 2].wait()
    latent_ref[...] = latent
    across = (((1,), (1,)), ((), ()))
    logit_wide = jnp.zeros((count, width), f32)
    for c, cut in enumerate(cuts):
        moved = lax.dot_general(latent, u_ref[cut, :], across, preferred_element_type=f32)
        moved = moved + bias_ref[:, cut]
        shifted[:, cut] = moved
        part = pooled[c].astype(f32)
        logit_wide = logit_wide + (part * moved + part) * head_ref[:, cut]
    logit = jnp.sum(logit_wide, axis=1, keepdims=True)
    target = jnp.transpose(labels_ref[...]).astype(f32)
    small = jnp.exp(-jnp.abs(logit))
    losses = jnp.maximum(logit, 0.0) + jnp.log1p(small) - target * logit
    loss = jnp.sum(losses, axis=0, keepdims=True)
    dlogit = jnp.where(logit >= 0, 1.0, small) / (1.0 + small) - target
    dlogit_ref[...] = jnp.transpose(dlogit)

    mine = core_ref[0] == 0
    lane1 = lax.broadcasted_iota(jnp.int32, (1, width), 1)
    loss_row = jnp.where(lane1 == 0, loss, 0.0)
    back = jnp.zeros((count, width), f32)
    for c, cut in enumerate(cuts):
        part = pooled[c].astype(f32)
        lift = dlogit * head_ref[:, cut] * part
        crossed = part * shifted[:, cut] + part
        dbias = jnp.sum(lift, axis=0, keepdims=True)
        dhead = jnp.sum(dlogit * crossed, axis=0, keepdims=True)
        lift = lift.astype(bf16)
        dlift[:, cut] = lift
        back = back + jnp.dot(lift, u_ref[cut, :], preferred_element_type=f32)
        extra_ref[c, 0:1, :] = jnp.where(mine, dbias, dhead)
        extra_ref[c, 1:2, :] = loss_row
        extra_ref[c, 2:8, :] = jnp.zeros((6, width), f32)
        send_ref[c, width : width + 1, :] = jnp.where(mine, dhead, dbias)
        send_ref[c, width + 1 : width + 2, :] = loss_row
        send_ref[c, width + 2 : width + 8, :] = jnp.zeros((6, width), f32)
        left[:, cut] = jnp.where(mine, lift, pooled[c])
    dlatent = back.astype(bf16)
    dlatent_ref[...] = dlatent
    copies = [pltpu.make_async_copy(left, left_out, out_sems.at[feats])]
    copies[0].start()
    right = jnp.where(mine, dlatent, latent)
    for c, cut in enumerate(cuts):
        send_ref[c, :width, :] = lax.dot_general(
            jnp.where(mine, pooled[c], dlift[:, cut]),
            right,
            (((0,), (0,)), ((), ())),
            preferred_element_type=f32,
        )
        copies.append(pltpu.make_async_copy(send_ref.at[c], send_out.at[c], out_sems.at[c]))
        copies[-1].start()
    for copy in copies:
        copy.wait()


def dense(core, labels, pooled, proj_u, proj_v, cross_bias, head):
    blocks, count, width = pooled.shape
    wide = blocks * width
    f32, bf16 = jnp.float32, jnp.bfloat16
    vmem = pl.BlockSpec(memory_space=pltpu.VMEM)
    anywhere = pl.BlockSpec(memory_space=pl.ANY)
    bundle = (blocks, width + 8, width)
    return pl.pallas_call(
        dense_kernel,
        out_shape=(
            jax.ShapeDtypeStruct(bundle, f32),
            jax.ShapeDtypeStruct((count, wide), bf16),
            jax.ShapeDtypeStruct((count, width), bf16),
            jax.ShapeDtypeStruct((count, width), bf16),
            jax.ShapeDtypeStruct((1, count), f32),
            jax.ShapeDtypeStruct((blocks, 8, width), f32),
        ),
        in_specs=[pl.BlockSpec(memory_space=pltpu.SMEM)]
        + [vmem]
        + [anywhere] * 3
        + [vmem] * 2,
        out_specs=[anywhere] * 2 + [vmem] * 4,
        scratch_shapes=[
            pltpu.VMEM((wide, width), bf16),
            pltpu.VMEM((wide, width), bf16),
            pltpu.VMEM(bundle, f32),
            pltpu.VMEM((count, wide), bf16),
            pltpu.VMEM((blocks, count, width), bf16),
            pltpu.VMEM((count, wide), f32),
            pltpu.VMEM((count, wide), bf16),
            pltpu.SemaphoreType.DMA((3 * blocks,)),
            pltpu.SemaphoreType.DMA((blocks + 1,)),
        ],
        compiler_params=pltpu.CompilerParams(vmem_limit_bytes=60 * 1024 * 1024),
        cost_estimate=pl.CostEstimate(
            flops=1_600_000_000, bytes_accessed=9_000_000, transcendentals=1000
        ),
        name="dense",
    )(
        core[None],
        labels[None, :],
        pooled,
        proj_u,
        proj_v,
        cross_bias[None, :],
        head[None, :],
    )


def keep_kernel(core_ref, left_ref, latent_ref, dlatent_ref, extra_ref, keep_ref):
    width = latent_ref.shape[1]
    right = jnp.where(core_ref[0] == 0, latent_ref[...], dlatent_ref[...])
    for c in range(keep_ref.shape[0]):
        keep_ref[c, :width, :] = lax.dot_general(
            left_ref[:, c * width : (c + 1) * width],
            right,
            (((0,), (0,)), ((), ())),
            preferred_element_type=jnp.float32,
        )
        keep_ref[c, width : width + 8, :] = extra_ref[c]


def kept(core, left, latent, dlatent, extra):
    blocks, _, width = extra.shape
    vmem = pl.BlockSpec(memory_space=pltpu.VMEM)
    return pl.pallas_call(
        keep_kernel,
        out_shape=jax.ShapeDtypeStruct((blocks, width + 8, width), jnp.float32),
        in_specs=[pl.BlockSpec(memory_space=pltpu.SMEM)] + [vmem] * 4,
        out_specs=vmem,
        compiler_params=pltpu.CompilerParams(vmem_limit_bytes=16 * 1024 * 1024),
        cost_estimate=pl.CostEstimate(
            flops=300_000_000, bytes_accessed=4_000_000, transcendentals=0
        ),
        name="kept",
    )(core[None], left, latent, dlatent, extra)


def payload_kernel(
    slot_ref, evict_ref, miss_ref, accum_ref, cache_any, out_ref, taken, place, cache, sems
):
    owners, per = taken.shape[0], out_ref.shape[0] // taken.shape[0]
    width = out_ref.shape[1]
    listed = slot_ref.shape[0]
    step = cache.shape[0] // 4
    loads = []
    for part in range(4):
        rows = pl.ds(part * step, step)
        loads.append(pltpu.make_async_copy(cache_any.at[rows], cache.at[rows], sems.at[part]))
        loads[-1].start()
    lane = lax.broadcasted_iota(jnp.int32, (1, width), 1)
    base = jnp.where((lane >= per) & (lane < 2 * per), -1.0, 0.0)
    for o in range(owners):
        taken[o] = 0
        out_ref[o * per : o * per + per - 1, :] = jnp.zeros((per - 1, width), jnp.float32)
        out_ref[o * per + per - 1 : (o + 1) * per, :] = base

    def leave(i, _):
        owner = evict_ref[0, i]
        rank = taken[owner]
        taken[owner] = rank + 1
        place[i] = owner * per + rank
        spot = pl.ds(owner * per + per - 1, 1)
        meta = jnp.where(lane == rank, accum_ref[slot_ref[i]], out_ref[spot, :])
        row = evict_ref[1, i].astype(jnp.float32)
        out_ref[spot, :] = jnp.where(lane == per + rank, row, meta)
        return 0

    lax.fori_loop(0, listed, leave, 0, unroll=8)
    for o in range(owners):
        taken[o] = 0

    def ask(i, _):
        owner = miss_ref[0, i]
        rank = taken[owner]
        taken[owner] = rank + 1
        spot = pl.ds(owner * per + per - 1, 1)
        row = miss_ref[1, i].astype(jnp.float32)
        out_ref[spot, :] = jnp.where(lane == 2 * per + rank, row, out_ref[spot, :])
        return 0

    lax.fori_loop(0, listed, ask, 0, unroll=8)
    for load in loads:
        load.wait()

    def move(i, _):
        out_ref[pl.ds(place[i], 1), :] = cache[pl.ds(slot_ref[i], 1), :]
        return 0

    lax.fori_loop(0, listed, move, 0, unroll=8)


def payload(evict_slot, evict_dest, miss_dest, cache_accum, cache_rows, owners, per):
    smem = pl.BlockSpec(memory_space=pltpu.SMEM)
    return pl.pallas_call(
        payload_kernel,
        out_shape=jax.ShapeDtypeStruct((owners * per, cache_rows.shape[1]), jnp.float32),
        in_specs=[smem] * 4 + [pl.BlockSpec(memory_space=pl.ANY)],
        out_specs=pl.BlockSpec(memory_space=pltpu.VMEM),
        scratch_shapes=[
            pltpu.SMEM((owners,), jnp.int32),
            pltpu.SMEM(evict_slot.shape, jnp.int32),
            pltpu.VMEM(cache_rows.shape, jnp.float32),
            pltpu.SemaphoreType.DMA((4,)),
        ],
        compiler_params=pltpu.CompilerParams(vmem_limit_bytes=60 * 1024 * 1024),
        cost_estimate=pl.CostEstimate(flops=100_000, bytes_accessed=1_500_000, transcendentals=0),
        name="payload",
    )(evict_slot, evict_dest.T, miss_dest.T, cache_accum, cache_rows)


def update_kernel(
    slots_ref,
    evict_ref,
    place_ref,
    cache_ref,
    accum_ref,
    latent_ref,
    dlatent_ref,
    dlogit_ref,
    u_ref,
    v_ref,
    bias_ref,
    head_ref,
    back_ref,
    rows_ref,
    accum_out,
):
    f32, bf16 = jnp.float32, jnp.bfloat16
    (cells, width), count = cache_ref.shape, latent_ref.shape[0]
    feats = u_ref.shape[0] // width
    looks = slots_ref.shape[0] // feats
    across = (((1,), (1,)), ((), ()))
    latent, dlatent = latent_ref[...], dlatent_ref[...]
    dlogit = jnp.transpose(dlogit_ref[...])
    cell = lax.broadcasted_iota(jnp.int32, (cells, count), 0)
    grad = jnp.zeros((cells, width), f32)
    for f in range(feats):
        counts = jnp.zeros((cells, count), f32)
        for look in range(looks):
            at = f * looks + look
            counts = counts + jnp.where(cell == slots_ref[at : at + 1, :], 1.0, 0.0)
        cut = slice(f * width, (f + 1) * width)
        moved = lax.dot_general(latent, u_ref[cut, :], across, preferred_element_type=f32)
        moved = moved + bias_ref[:, cut]
        through = lax.dot_general(dlatent, v_ref[cut, :], across, preferred_element_type=f32)
        dpooled = (dlogit * head_ref[:, cut] * (moved + 1.0) + through).astype(bf16)
        grad = grad + jnp.dot(counts.astype(bf16), dpooled, preferred_element_type=f32)
    mean = jnp.sum(grad * grad, axis=1, keepdims=True) / width
    accum = jnp.transpose(accum_ref[...]) + mean
    rows_ref[...] = cache_ref[...] - ETA * grad * lax.rsqrt(accum)
    accum_out[...] = jnp.transpose(accum)

    def refill(i, _):
        rows_ref[pl.ds(evict_ref[i], 1), :] = back_ref[pl.ds(place_ref[i], 1), :]
        return 0

    lax.fori_loop(0, evict_ref.shape[0], refill, 0, unroll=8)


def updated(slot_ids, evict_slot, place, cache_rows, cache_accum, saved, params, back):
    cells = cache_rows.shape[0]
    smem = pl.BlockSpec(memory_space=pltpu.SMEM)
    vmem = pl.BlockSpec(memory_space=pltpu.VMEM)
    return pl.pallas_call(
        update_kernel,
        out_shape=(
            jax.ShapeDtypeStruct(cache_rows.shape, jnp.float32),
            jax.ShapeDtypeStruct((1, cells), jnp.float32),
        ),
        in_specs=[vmem, smem, smem] + [vmem] * 10,
        out_specs=(vmem, vmem),
        compiler_params=pltpu.CompilerParams(vmem_limit_bytes=60 * 1024 * 1024),
        cost_estimate=pl.CostEstimate(
            flops=1_100_000_000, bytes_accessed=4_000_000, transcendentals=1000
        ),
        name="update",
    )(
        slot_ids.T,
        evict_slot,
        place,
        cache_rows,
        cache_accum[None, :],
        *saved,
        *params,
        back,
    )


def reply_kernel(
    ids_ref,
    sums_ref,
    got_ref,
    table_any,
    accum_any,
    reply_ref,
    table_out,
    accum_out,
    table,
    accum,
    sems,
):
    owners, per = sums_ref.shape
    cap = per - 2
    width = got_ref.shape[1]
    step = table.shape[0] // 4
    loads = [pltpu.make_async_copy(accum_any, accum, sems.at[4])]
    stores = [pltpu.make_async_copy(accum, accum_out, sems.at[4])]
    for part in range(4):
        rows = pl.ds(part * step, step)
        loads.append(pltpu.make_async_copy(table_any.at[rows], table.at[rows], sems.at[part]))
        stores.append(pltpu.make_async_copy(table.at[rows], table_out.at[rows], sems.at[part]))
    for load in loads:
        load.start()
    for load in loads:
        load.wait()

    def store(s, _):
        for r in range(cap):
            row = ids_ref[s, per + r]

            @pl.when(row >= 0)
            def _():
                table[pl.ds(row, 1), :] = got_ref[pl.ds(s * per + r, 1), :]
                accum[row] = sums_ref[s, r]

        return 0

    lax.fori_loop(0, owners, store, 0, unroll=2)
    for copy in stores:
        copy.start()
    lane = lax.broadcasted_iota(jnp.int32, (1, width), 1)

    def answer(s, _):
        meta = jnp.zeros((1, width), jnp.float32)
        for r in range(cap):
            row = ids_ref[s, 2 * per + r]
            reply_ref[pl.ds(s * per + r, 1), :] = table[pl.ds(row, 1), :]
            meta = jnp.where(lane == r, accum[row], meta)
        reply_ref[pl.ds(s * per + cap, 1), :] = jnp.zeros((1, width), jnp.float32)
        reply_ref[pl.ds(s * per + per - 1, 1), :] = meta
        return 0

    lax.fori_loop(0, owners, answer, 0, unroll=4)
    for copy in stores:
        copy.wait()


def replied(got, table_rows, table_accum):
    owners, per, width = got.shape
    smem = pl.BlockSpec(memory_space=pltpu.SMEM)
    vmem = pl.BlockSpec(memory_space=pltpu.VMEM)
    anywhere = pl.BlockSpec(memory_space=pl.ANY)
    meta = got[:, per - 1, : 3 * per]
    return pl.pallas_call(
        reply_kernel,
        out_shape=(
            jax.ShapeDtypeStruct((owners * per, width), jnp.float32),
            jax.ShapeDtypeStruct(table_rows.shape, jnp.float32),
            jax.ShapeDtypeStruct(table_accum.shape, jnp.float32),
        ),
        in_specs=[smem, smem, vmem, anywhere, anywhere],
        out_specs=(vmem, anywhere, anywhere),
        scratch_shapes=[
            pltpu.VMEM(table_rows.shape, jnp.float32),
            pltpu.SMEM(table_accum.shape, jnp.float32),
            pltpu.SemaphoreType.DMA((5,)),
        ],
        compiler_params=pltpu.CompilerParams(vmem_limit_bytes=60 * 1024 * 1024),
        cost_estimate=pl.CostEstimate(flops=100_000, bytes_accessed=3_000_000, transcendentals=0),
        name="reply",
    )(meta.astype(jnp.int32), meta[:, :per], got.reshape(owners * per, width), table_rows, table_accum)


def scaled(index, half_any, proj_ref, half, stage, in_sems, out_sems):
    blocks, width = half.shape[0], half.shape[2]
    loads = []
    for c in range(blocks):
        loads.append(pltpu.make_async_copy(half_any.at[c], half.at[c], in_sems.at[c]))
        loads[-1].start()
    squares = jnp.zeros((width, width), jnp.float32)
    for c in range(blocks):
        loads[c].wait()
        block = half[c, :width, :]
        squares = squares + block * block
    total = jnp.sum(jnp.sum(squares, axis=0, keepdims=True), axis=1, keepdims=True)
    scale = lax.rsqrt(total / (blocks * width * width) + EPS)
    copies = []
    for c in range(blocks):
        stage[c] = half[c, :width, :] * scale
        copies.append(
            pltpu.make_async_copy(
                stage.at[c], proj_ref.at[index, pl.ds(c * width, width), :], out_sems.at[c]
            )
        )
        copies[-1].start()
    return copies


def own_kernel(core_ref, half_any, proj_ref, half, stage, in_sems, out_sems):
    for copy in scaled(core_ref[0], half_any, proj_ref, half, stage, in_sems, out_sems):
        copy.wait()


def other_kernel(
    core_ref,
    proj_in,
    own_ref,
    half_any,
    proj_ref,
    vec_ref,
    loss_ref,
    half,
    stage,
    in_sems,
    out_sems,
):
    core = core_ref[0]
    copies = scaled(1 - core, half_any, proj_ref, half, stage, in_sems, out_sems)
    blocks, width = half.shape[0], half.shape[2]
    mine = core == 0
    own = [own_ref[c, 0:1, :] for c in range(blocks)]
    far = [half[c, width : width + 1, :] for c in range(blocks)]
    for index in (0, 1):
        rows = [jnp.where(mine, *((a, b) if index == 0 else (b, a))) for a, b in zip(own, far)]
        squares = sum(row * row for row in rows)
        total = jnp.sum(squares, axis=1, keepdims=True)
        scale = lax.rsqrt(total / (blocks * width) + EPS)
        for c in range(blocks):
            vec_ref[index : index + 1, c * width : (c + 1) * width] = rows[c] * scale
    loss_ref[...] = jnp.where(
        mine, half[0, width + 1 : width + 2, :128], own_ref[0, 1:2, :128]
    )
    for copy in copies:
        copy.wait()


def normalized(core, own, other):
    blocks, depth, width = own.shape
    wide = blocks * width
    smem = pl.BlockSpec(memory_space=pltpu.SMEM)
    vmem = pl.BlockSpec(memory_space=pltpu.VMEM)
    anywhere = pl.BlockSpec(memory_space=pl.ANY)
    scratch = [
        pltpu.VMEM((blocks, depth, width), jnp.float32),
        pltpu.VMEM((blocks, width, width), jnp.float32),
        pltpu.SemaphoreType.DMA((blocks,)),
        pltpu.SemaphoreType.DMA((blocks,)),
    ]
    proj = jax.ShapeDtypeStruct((2, wide, width), jnp.float32)
    limit = pltpu.CompilerParams(vmem_limit_bytes=16 * 1024 * 1024)
    half = pl.pallas_call(
        own_kernel,
        out_shape=proj,
        in_specs=[smem, anywhere],
        out_specs=anywhere,
        scratch_shapes=scratch,
        compiler_params=limit,
        name="scale_own",
    )(core[None], own)
    return pl.pallas_call(
        other_kernel,
        out_shape=(
            proj,
            jax.ShapeDtypeStruct((2, wide), jnp.float32),
            jax.ShapeDtypeStruct((1, 128), jnp.float32),
        ),
        in_specs=[smem, anywhere, vmem, anywhere],
        out_specs=(anywhere, vmem, vmem),
        scratch_shapes=scratch,
        input_output_aliases={1: 0},
        compiler_params=limit,
        name="scale_other",
    )(core[None], half, own[:, width:, :], other)


def shards(
    slot_ids,
    labels,
    cache_rows,
    cache_accum,
    table_rows,
    table_accum,
    miss_dest,
    evict_slot,
    evict_dest,
    proj_u,
    proj_v,
    cross_bias,
    head,
):
    owners = 32
    per = 8
    width = cache_rows.shape[1]
    cells = cache_rows.shape[0]
    spots = owners * per
    core = lax.axis_index("table") % 2

    sent = payload(
        evict_slot, evict_dest, miss_dest, cache_accum, cache_rows, owners, per
    ).reshape(owners, per, width)
    sent, slots_late = lax.optimization_barrier((sent, slot_ids))
    got = lax.all_to_all(sent, "table", split_axis=0, concat_axis=0, tiled=True)
    feats = proj_u.shape[0] // width
    pooled = pool(slots_late, cache_rows, feats)

    pooled, got = lax.optimization_barrier((pooled, got))
    reply, table_new, accum_table = replied(got, table_rows, table_accum)
    reply, pooled = lax.optimization_barrier((reply, pooled))
    back = lax.all_to_all(
        reply.reshape(owners, per, width), "table", split_axis=0, concat_axis=0, tiled=True
    )

    count = slot_ids.shape[0]
    send, left, latent, dlatent, dlogit, extra = dense(
        core, labels, pooled, proj_u, proj_v, cross_bias, head
    )

    blocks = feats
    depth = width
    send, back = lax.optimization_barrier((send, back))
    held = kept(core, left, latent, dlatent, extra) + swap_cores(send)
    held = exchange(held, first_groups())
    held = jnp.sum(held, axis=0)
    fine = depth // 16
    pieces16 = jnp.concatenate(
        [
            held[:depth].reshape(16, fine, width),
            jnp.broadcast_to(held[None, depth:], (16, 8, width)),
        ],
        axis=1,
    )
    held = exchange(pieces16, second_groups())
    place = miss_dest[:, 0] * per + ranks(miss_dest[:, 0])
    rows_new, accum_new = updated(
        slot_ids,
        evict_slot,
        place,
        cache_rows,
        cache_accum,
        (latent, dlatent, dlogit),
        (proj_u, proj_v, cross_bias[None, :], head[None, :]),
        back.reshape(spots, width),
    )
    fetched_accum = picked(back[:, per - 1, :per].reshape(-1), place)
    filled = evict_slot[:, None] == jnp.arange(cells, dtype=jnp.int32)[None, :]
    filled_sum = jnp.sum(jnp.where(filled, fetched_accum[:, None], 0.0), axis=0)
    accum_new = jnp.where(jnp.any(filled, axis=0), filled_sum, accum_new.reshape(cells))
    held, rows_new, accum_new = lax.optimization_barrier((held, rows_new, accum_new))
    summed16 = jnp.sum(held, axis=0)
    extras = summed16[fine:]
    spread = jnp.broadcast_to(summed16[None, :fine], (16, fine, width))
    held = exchange(spread, second_groups())
    whole = jnp.concatenate([held.reshape(depth, width), extras], axis=0)
    whole = exchange(jnp.broadcast_to(whole[None], (blocks, depth + 8, width)), first_groups())
    clipped_proj, clipped_vecs, loss_row = normalized(core, whole, swap_cores(whole))
    loss = loss_row[0, 0] / (count * 256)
    return (rows_new, accum_new, table_new, accum_table, clipped_proj, clipped_vecs, loss)


def solution(mesh):
    split = P(AXES)
    rows = P(AXES, None)
    return jax.shard_map(
        shards,
        mesh=mesh,
        in_specs=(
            rows,
            split,
            rows,
            split,
            rows,
            split,
            rows,
            split,
            rows,
            P(),
            P(),
            P(),
            P(),
        ),
        out_specs=(rows, split, rows, split, P(), P(), P()),
        check_vma=False,
    )
```

```python
import jax
import jax.numpy as jnp
from jax import lax
from jax.experimental import pallas as pl
from jax.experimental.pallas import tpu as pltpu
from jax.sharding import PartitionSpec as P

EPS = 1e-06
ETA = 0.05
AXES = ("trainer", "table")


def device_at(y, x, z, core):
    return (((y // 2 * 4 + x) * 2 + y % 2) * 8 + z % 8) * 2 + core


def plane_groups():
    return [
        [device_at(y, x, 2 * pair + core + b, core) for y in range(4) for x in range(4) for b in (0, 1)]
        for core in range(2)
        for pair in range(4)
    ]


def shift_z(value, step):
    there = [
        (device_at(y, x, z, core), device_at(y, x, z + step, core))
        for y in range(4)
        for x in range(4)
        for z in range(8)
        for core in range(2)
    ]
    return lax.ppermute(value, AXES, there)


def swap_cores(value):
    return lax.ppermute(value, AXES, [(i, i ^ 1) for i in range(256)])


def exchange(value, groups):
    return lax.all_to_all(
        value, AXES, split_axis=0, concat_axis=0, tiled=True, axis_index_groups=groups
    )


def ranks(owner):
    listed = owner.shape[0]
    order = jnp.arange(listed, dtype=jnp.int32)
    earlier = (owner[:, None] == owner[None, :]) & (order[None, :] < order[:, None])
    return jnp.sum(earlier.astype(jnp.int32), axis=1)


def meta_row(columns, width):
    block = jnp.concatenate(columns, axis=1)
    return jnp.pad(block, ((0, 0), (0, width - block.shape[1])))[:, None, :]


def picked(values, index):
    hit = index[:, None] == jnp.arange(values.shape[0], dtype=jnp.int32)[None, :]
    return jnp.sum(jnp.where(hit, values[None, :], 0.0), axis=1)


def cross(value, bit):
    split = value.reshape(value.shape[0] // (2 * bit), 2, bit, *value.shape[1:])
    there = [(i, i ^ bit) for i in range(256)]
    came = lax.ppermute(split[:, 1], AXES, there)
    return jnp.stack([split[:, 0], came], axis=1).reshape(value.shape)


def put_blocks(ref, c, grad):
    half = grad.shape[1] // 2
    rows = grad.shape[0] // 4
    for q in range(4):
        part = grad[q * rows : (q + 1) * rows, :]
        ref[4 * c + q, :rows, :] = part[:, :half]
        ref[4 * c + q, rows : 2 * rows, :] = part[:, half:]


def dense_kernel(
    core_ref,
    slots_ref,
    labels_ref,
    cache_any,
    u_any,
    v_any,
    bias_ref,
    head_ref,
    send_out,
    left_out,
    latent_ref,
    dlatent_ref,
    dlogit_ref,
    extra_ref,
    cache,
    u_ref,
    v_ref,
    send_ref,
    left,
    high,
    mid,
    low,
    pooled,
    shifted,
    dlift,
    in_sems,
    out_sems,
):
    f32, bf16 = jnp.float32, jnp.bfloat16
    count, (cells, width) = slots_ref.shape[1], cache.shape
    feats = u_ref.shape[0] // width
    looks = slots_ref.shape[0] // feats
    cuts = [slice(c * width, (c + 1) * width) for c in range(feats)]
    loads = []
    for source, target in ((cache_any, cache), (v_any, v_ref), (u_any, u_ref)):
        step = target.shape[0] // 4
        for part in range(4):
            rows = pl.ds(part * step, step)
            loads.append(
                pltpu.make_async_copy(source.at[rows], target.at[rows], in_sems.at[len(loads)])
            )
            loads[-1].start()
    slots = jnp.transpose(slots_ref[...])
    lane = lax.broadcasted_iota(jnp.int32, (count, cells), 1)

    def counted(f):
        counts = jnp.zeros((count, cells), f32)
        for look in range(looks):
            at = f * looks + look
            counts = counts + jnp.where(lane == slots[:, at : at + 1], 1.0, 0.0)
        return counts.astype(bf16)

    counts = counted(0)
    step = cells // 4
    for part in range(4):
        loads[part].wait()
        rows = cache[part * step : (part + 1) * step, :]
        first = rows.astype(bf16)
        rest = rows - first.astype(f32)
        second = rest.astype(bf16)
        high[part * step : (part + 1) * step, :] = first
        mid[part * step : (part + 1) * step, :] = second
        low[part * step : (part + 1) * step, :] = (rest - second.astype(f32)).astype(bf16)
    for f in range(feats):
        if f > 0:
            counts = counted(f)
        total = jnp.dot(counts, low[...], preferred_element_type=f32)
        total = total + jnp.dot(counts, mid[...], preferred_element_type=f32)
        total = total + jnp.dot(counts, high[...], preferred_element_type=f32)
        pooled[:, cuts[f]] = total.astype(bf16)

    for load in loads[4:]:
        load.wait()
    latent = jnp.dot(pooled[...], v_ref[...], preferred_element_type=f32).astype(bf16)
    latent_ref[...] = latent
    across = (((1,), (1,)), ((), ()))
    logit_wide = jnp.zeros((count, width), f32)
    for cut in cuts:
        moved = lax.dot_general(latent, u_ref[cut, :], across, preferred_element_type=f32)
        moved = moved + bias_ref[:, cut]
        shifted[:, cut] = moved
        part = pooled[:, cut].astype(f32)
        logit_wide = logit_wide + (part * moved + part) * head_ref[:, cut]
    logit = jnp.sum(logit_wide, axis=1, keepdims=True)
    target = jnp.transpose(labels_ref[...]).astype(f32)
    small = jnp.exp(-jnp.abs(logit))
    losses = jnp.maximum(logit, 0.0) + jnp.log1p(small) - target * logit
    loss = jnp.sum(losses, axis=0, keepdims=True)
    dlogit = jnp.where(logit >= 0, 1.0, small) / (1.0 + small) - target
    dlogit_ref[...] = jnp.transpose(dlogit)

    mine = core_ref[0] == 0
    half = width // 2
    lane1 = lax.broadcasted_iota(jnp.int32, (1, half), 1)
    loss_row = jnp.where(lane1 == 0, loss, 0.0)
    back = jnp.zeros((count, width), f32)
    for c, cut in enumerate(cuts):
        part = pooled[:, cut].astype(f32)
        lift = dlogit * head_ref[:, cut] * part
        crossed = part * shifted[:, cut] + part
        dbias = jnp.sum(lift, axis=0, keepdims=True)
        dhead = jnp.sum(dlogit * crossed, axis=0, keepdims=True)
        lift = lift.astype(bf16)
        dlift[:, cut] = lift
        back = back + jnp.dot(lift, u_ref[cut, :], preferred_element_type=f32)
        for ref, row in (
            (extra_ref, jnp.where(mine, dbias, dhead)),
            (send_ref, jnp.where(mine, dhead, dbias)),
        ):
            top = ref.shape[1] - 8
            for q in range(4):
                at = 4 * c + q
                ref[at, top : top + 8, :] = jnp.zeros((8, half), f32)
                ref[at, top + 1 : top + 2, :] = loss_row
                if q % 2 == 0:
                    ref[at, top : top + 1, :] = row[:, q // 2 * half : (q // 2 + 1) * half]
        left[:, cut] = jnp.where(mine, lift, pooled[:, cut])
    dlatent = back.astype(bf16)
    dlatent_ref[...] = dlatent
    copies = [pltpu.make_async_copy(left, left_out, out_sems.at[feats])]
    copies[0].start()
    right = jnp.where(mine, dlatent, latent)
    for c, cut in enumerate(cuts):
        grad = lax.dot_general(
            jnp.where(mine, pooled[:, cut], dlift[:, cut]),
            right,
            (((0,), (0,)), ((), ())),
            preferred_element_type=f32,
        )
        put_blocks(send_ref, c, grad)
        four = pl.ds(4 * c, 4)
        copies.append(
            pltpu.make_async_copy(send_ref.at[four], send_out.at[four], out_sems.at[c])
        )
        copies[-1].start()
    for copy in copies:
        copy.wait()


def dense(core, slot_ids, labels, cache_rows, proj_u, proj_v, cross_bias, head):
    count, (cells, width) = slot_ids.shape[0], cache_rows.shape
    wide = proj_u.shape[0]
    blocks = wide // width
    f32, bf16 = jnp.float32, jnp.bfloat16
    vmem = pl.BlockSpec(memory_space=pltpu.VMEM)
    anywhere = pl.BlockSpec(memory_space=pl.ANY)
    bundle = (4 * blocks, width // 2 + 8, width // 2)
    return pl.pallas_call(
        dense_kernel,
        out_shape=(
            jax.ShapeDtypeStruct(bundle, f32),
            jax.ShapeDtypeStruct((count, wide), bf16),
            jax.ShapeDtypeStruct((count, width), bf16),
            jax.ShapeDtypeStruct((count, width), bf16),
            jax.ShapeDtypeStruct((1, count), f32),
            jax.ShapeDtypeStruct((4 * blocks, 8, width // 2), f32),
        ),
        in_specs=[pl.BlockSpec(memory_space=pltpu.SMEM)]
        + [vmem] * 2
        + [anywhere] * 3
        + [vmem] * 2,
        out_specs=[anywhere] * 2 + [vmem] * 4,
        scratch_shapes=[
            pltpu.VMEM((cells, width), f32),
            pltpu.VMEM((wide, width), bf16),
            pltpu.VMEM((wide, width), bf16),
            pltpu.VMEM(bundle, f32),
            pltpu.VMEM((count, wide), bf16),
        ]
        + [pltpu.VMEM((cells, width), bf16)] * 3
        + [
            pltpu.VMEM((count, wide), bf16),
            pltpu.VMEM((count, wide), f32),
            pltpu.VMEM((count, wide), bf16),
            pltpu.SemaphoreType.DMA((12,)),
            pltpu.SemaphoreType.DMA((blocks + 1,)),
        ],
        compiler_params=pltpu.CompilerParams(vmem_limit_bytes=60 * 1024 * 1024),
        cost_estimate=pl.CostEstimate(
            flops=5_000_000_000, bytes_accessed=9_000_000, transcendentals=1000
        ),
        name="dense",
    )(
        core[None],
        slot_ids.T,
        labels[None, :],
        cache_rows,
        proj_u,
        proj_v,
        cross_bias[None, :],
        head[None, :],
    )


def keep_kernel(core_ref, left_ref, latent_ref, dlatent_ref, extra_ref, keep_ref):
    width = latent_ref.shape[1]
    right = jnp.where(core_ref[0] == 0, latent_ref[...], dlatent_ref[...])
    for c in range(keep_ref.shape[0] // 4):
        grad = lax.dot_general(
            left_ref[:, c * width : (c + 1) * width],
            right,
            (((0,), (0,)), ((), ())),
            preferred_element_type=jnp.float32,
        )
        put_blocks(keep_ref, c, grad)
    keep_ref[:, width // 2 :, :] = extra_ref[...]


def kept(core, left, latent, dlatent, extra):
    blocks, _, half = extra.shape
    vmem = pl.BlockSpec(memory_space=pltpu.VMEM)
    return pl.pallas_call(
        keep_kernel,
        out_shape=jax.ShapeDtypeStruct((blocks, half + 8, half), jnp.float32),
        in_specs=[pl.BlockSpec(memory_space=pltpu.SMEM)] + [vmem] * 4,
        out_specs=vmem,
        compiler_params=pltpu.CompilerParams(vmem_limit_bytes=16 * 1024 * 1024),
        cost_estimate=pl.CostEstimate(
            flops=300_000_000, bytes_accessed=4_000_000, transcendentals=0
        ),
        name="kept",
    )(core[None], left, latent, dlatent, extra)


def payload_kernel(
    slot_ref, evict_ref, miss_ref, accum_ref, cache_any, out_ref, taken, place, cache, sems
):
    owners, per = taken.shape[0], out_ref.shape[0] // taken.shape[0]
    width = out_ref.shape[1]
    listed = slot_ref.shape[0]
    step = cache.shape[0] // 4
    loads = []
    for part in range(4):
        rows = pl.ds(part * step, step)
        loads.append(pltpu.make_async_copy(cache_any.at[rows], cache.at[rows], sems.at[part]))
        loads[-1].start()
    lane = lax.broadcasted_iota(jnp.int32, (1, width), 1)
    base = jnp.where((lane >= per) & (lane < 2 * per), -1.0, 0.0)
    for o in range(owners):
        taken[o] = 0
        out_ref[o * per : o * per + per - 1, :] = jnp.zeros((per - 1, width), jnp.float32)
        out_ref[o * per + per - 1 : (o + 1) * per, :] = base

    def leave(i, _):
        owner = evict_ref[0, i]
        rank = taken[owner]
        taken[owner] = rank + 1
        place[i] = owner * per + rank
        spot = pl.ds(owner * per + per - 1, 1)
        meta = jnp.where(lane == rank, accum_ref[slot_ref[i]], out_ref[spot, :])
        row = evict_ref[1, i].astype(jnp.float32)
        out_ref[spot, :] = jnp.where(lane == per + rank, row, meta)
        return 0

    lax.fori_loop(0, listed, leave, 0, unroll=8)
    for o in range(owners):
        taken[o] = 0

    def ask(i, _):
        owner = miss_ref[0, i]
        rank = taken[owner]
        taken[owner] = rank + 1
        spot = pl.ds(owner * per + per - 1, 1)
        row = miss_ref[1, i].astype(jnp.float32)
        out_ref[spot, :] = jnp.where(lane == 2 * per + rank, row, out_ref[spot, :])
        return 0

    lax.fori_loop(0, listed, ask, 0, unroll=8)
    for load in loads:
        load.wait()

    def move(i, _):
        out_ref[pl.ds(place[i], 1), :] = cache[pl.ds(slot_ref[i], 1), :]
        return 0

    lax.fori_loop(0, listed, move, 0, unroll=8)


def payload(evict_slot, evict_dest, miss_dest, cache_accum, cache_rows, owners, per):
    smem = pl.BlockSpec(memory_space=pltpu.SMEM)
    return pl.pallas_call(
        payload_kernel,
        out_shape=jax.ShapeDtypeStruct((owners * per, cache_rows.shape[1]), jnp.float32),
        in_specs=[smem] * 4 + [pl.BlockSpec(memory_space=pl.ANY)],
        out_specs=pl.BlockSpec(memory_space=pltpu.VMEM),
        scratch_shapes=[
            pltpu.SMEM((owners,), jnp.int32),
            pltpu.SMEM(evict_slot.shape, jnp.int32),
            pltpu.VMEM(cache_rows.shape, jnp.float32),
            pltpu.SemaphoreType.DMA((4,)),
        ],
        compiler_params=pltpu.CompilerParams(vmem_limit_bytes=60 * 1024 * 1024),
        cost_estimate=pl.CostEstimate(flops=100_000, bytes_accessed=1_500_000, transcendentals=0),
        name="payload",
    )(evict_slot, evict_dest.T, miss_dest.T, cache_accum, cache_rows)


def update_kernel(
    slots_ref,
    cache_ref,
    accum_ref,
    latent_ref,
    dlatent_ref,
    dlogit_ref,
    u_ref,
    v_ref,
    bias_ref,
    head_ref,
    rows_ref,
    accum_out,
):
    f32, bf16 = jnp.float32, jnp.bfloat16
    (cells, width), count = cache_ref.shape, latent_ref.shape[0]
    feats = u_ref.shape[0] // width
    looks = slots_ref.shape[0] // feats
    across = (((1,), (1,)), ((), ()))
    latent, dlatent = latent_ref[...], dlatent_ref[...]
    dlogit = jnp.transpose(dlogit_ref[...])
    cell = lax.broadcasted_iota(jnp.int32, (cells, count), 0)
    grad = jnp.zeros((cells, width), f32)
    for f in range(feats):
        counts = jnp.zeros((cells, count), f32)
        for look in range(looks):
            at = f * looks + look
            counts = counts + jnp.where(cell == slots_ref[at : at + 1, :], 1.0, 0.0)
        cut = slice(f * width, (f + 1) * width)
        moved = lax.dot_general(latent, u_ref[cut, :], across, preferred_element_type=f32)
        moved = moved + bias_ref[:, cut]
        through = lax.dot_general(dlatent, v_ref[cut, :], across, preferred_element_type=f32)
        dpooled = (dlogit * head_ref[:, cut] * (moved + 1.0) + through).astype(bf16)
        grad = grad + jnp.dot(counts.astype(bf16), dpooled, preferred_element_type=f32)
    mean = jnp.sum(grad * grad, axis=1, keepdims=True) / width
    accum = jnp.transpose(accum_ref[...]) + mean
    rows_ref[...] = cache_ref[...] - ETA * grad * lax.rsqrt(accum)
    accum_out[...] = jnp.transpose(accum)


def refill_kernel(evict_ref, place_ref, back_ref, old_ref, rows_ref):
    rows_ref[...] = old_ref[...]

    def refill(i, _):
        rows_ref[pl.ds(evict_ref[i], 1), :] = back_ref[pl.ds(place_ref[i], 1), :]
        return 0

    lax.fori_loop(0, evict_ref.shape[0], refill, 0, unroll=8)


def updated(slot_ids, cache_rows, cache_accum, saved, params):
    cells = cache_rows.shape[0]
    vmem = pl.BlockSpec(memory_space=pltpu.VMEM)
    return pl.pallas_call(
        update_kernel,
        out_shape=(
            jax.ShapeDtypeStruct(cache_rows.shape, jnp.float32),
            jax.ShapeDtypeStruct((1, cells), jnp.float32),
        ),
        in_specs=[vmem] * 10,
        out_specs=(vmem, vmem),
        compiler_params=pltpu.CompilerParams(vmem_limit_bytes=60 * 1024 * 1024),
        cost_estimate=pl.CostEstimate(
            flops=1_100_000_000, bytes_accessed=4_000_000, transcendentals=1000
        ),
        name="update",
    )(slot_ids.T, cache_rows, cache_accum[None, :], *saved, *params)


def refilled(evict_slot, place, back, rows):
    smem = pl.BlockSpec(memory_space=pltpu.SMEM)
    vmem = pl.BlockSpec(memory_space=pltpu.VMEM)
    return pl.pallas_call(
        refill_kernel,
        out_shape=jax.ShapeDtypeStruct(rows.shape, jnp.float32),
        in_specs=[smem, smem, vmem, vmem],
        out_specs=vmem,
        compiler_params=pltpu.CompilerParams(vmem_limit_bytes=60 * 1024 * 1024),
        cost_estimate=pl.CostEstimate(flops=100_000, bytes_accessed=2_000_000, transcendentals=0),
        name="refill",
    )(evict_slot, place, back, rows)


def scaled(index, half_any, proj_ref, half, stage, in_sems, out_sems):
    chunks, width = stage.shape[0], stage.shape[2]
    edge, rows = width // 2, width // 4
    loads = []
    for c in range(chunks):
        four = pl.ds(4 * c, 4)
        loads.append(pltpu.make_async_copy(half_any.at[four], half.at[four], in_sems.at[c]))
        loads[-1].start()
    squares = jnp.zeros((edge, edge), jnp.float32)
    for c in range(chunks):
        loads[c].wait()
        for q in range(4):
            block = half[4 * c + q, :edge, :]
            squares = squares + block * block
    total = jnp.sum(jnp.sum(squares, axis=0, keepdims=True), axis=1, keepdims=True)
    scale = lax.rsqrt(total / (chunks * width * width) + EPS)
    copies = []
    for c in range(chunks):
        for q in range(4):
            at = slice(q * rows, (q + 1) * rows)
            stage[c, at, :edge] = half[4 * c + q, :rows, :] * scale
            stage[c, at, edge:] = half[4 * c + q, rows:edge, :] * scale
        copies.append(
            pltpu.make_async_copy(
                stage.at[c], proj_ref.at[index, pl.ds(c * width, width), :], out_sems.at[c]
            )
        )
        copies[-1].start()
    return copies


def own_kernel(core_ref, half_any, proj_ref, half, stage, in_sems, out_sems):
    for copy in scaled(core_ref[0], half_any, proj_ref, half, stage, in_sems, out_sems):
        copy.wait()


def other_kernel(
    core_ref,
    proj_in,
    own_ref,
    half_any,
    proj_ref,
    vec_ref,
    loss_ref,
    half,
    stage,
    in_sems,
    out_sems,
):
    core = core_ref[0]
    copies = scaled(1 - core, half_any, proj_ref, half, stage, in_sems, out_sems)
    edge = half.shape[2]
    tiles = vec_ref.shape[1] // edge
    mine = core == 0
    own = [own_ref[2 * t, 0:1, :] for t in range(tiles)]
    far = [half[2 * t, edge : edge + 1, :] for t in range(tiles)]
    for index in (0, 1):
        rows = [jnp.where(mine, *((a, b) if index == 0 else (b, a))) for a, b in zip(own, far)]
        squares = sum(row * row for row in rows)
        total = jnp.sum(squares, axis=1, keepdims=True)
        scale = lax.rsqrt(total / (tiles * edge) + EPS)
        for t in range(tiles):
            vec_ref[index : index + 1, t * edge : (t + 1) * edge] = rows[t] * scale
    loss_ref[...] = jnp.where(mine, half[0, edge + 1 : edge + 2, :], own_ref[0, 1:2, :])
    for copy in copies:
        copy.wait()


def normalized(core, own, other):
    blocks, depth, edge = own.shape
    chunks, width = blocks // 4, 2 * edge
    wide = chunks * width
    smem = pl.BlockSpec(memory_space=pltpu.SMEM)
    vmem = pl.BlockSpec(memory_space=pltpu.VMEM)
    anywhere = pl.BlockSpec(memory_space=pl.ANY)
    scratch = [
        pltpu.VMEM(own.shape, jnp.float32),
        pltpu.VMEM((chunks, width, width), jnp.float32),
        pltpu.SemaphoreType.DMA((chunks,)),
        pltpu.SemaphoreType.DMA((chunks,)),
    ]
    proj = jax.ShapeDtypeStruct((2, wide, width), jnp.float32)
    limit = pltpu.CompilerParams(vmem_limit_bytes=16 * 1024 * 1024)
    half = pl.pallas_call(
        own_kernel,
        out_shape=proj,
        in_specs=[smem, anywhere],
        out_specs=anywhere,
        scratch_shapes=scratch,
        compiler_params=limit,
        name="scale_own",
    )(core[None], own)
    return pl.pallas_call(
        other_kernel,
        out_shape=(
            proj,
            jax.ShapeDtypeStruct((2, wide), jnp.float32),
            jax.ShapeDtypeStruct((1, 128), jnp.float32),
        ),
        in_specs=[smem, anywhere, vmem, anywhere],
        out_specs=(anywhere, vmem, vmem),
        scratch_shapes=scratch,
        input_output_aliases={1: 0},
        compiler_params=limit,
        name="scale_other",
    )(core[None], half, own[:, edge:, :], other)


def shards(
    slot_ids,
    labels,
    cache_rows,
    cache_accum,
    table_rows,
    table_accum,
    miss_dest,
    evict_slot,
    evict_dest,
    proj_u,
    proj_v,
    cross_bias,
    head,
):
    owners = 32
    per = 8
    cap = 6
    width = cache_rows.shape[1]
    owned = table_rows.shape[0]
    cells = cache_rows.shape[0]
    spots = owners * per
    core = lax.axis_index("table") % 2

    me = lax.axis_index("table")
    sent = payload(
        evict_slot, evict_dest, miss_dest, cache_accum, cache_rows, owners, per
    ).reshape(owners, per, width)
    sent, slots_late = lax.optimization_barrier((sent, slot_ids))
    got = lax.all_to_all(sent, "table", split_axis=0, concat_axis=0, tiled=True)

    count = slot_ids.shape[0]
    feats = proj_u.shape[0] // width
    send, left, latent, dlatent, dlogit, extra = dense(
        core, slots_late, labels, cache_rows, proj_u, proj_v, cross_bias, head
    )

    send, got = lax.optimization_barrier((send, got))
    held = kept(core, left, latent, dlatent, extra) + swap_cores(send)
    held, got = lax.optimization_barrier((held, got))

    got_meta = got[:, per - 1, :]
    got_id = got_meta[:, per : per + cap].astype(jnp.int32)
    flat = got_id.reshape(-1)
    table_new = table_rows.at[jnp.where(flat < 0, owned, flat)].set(
        got[:, :cap, :].reshape(-1, width), mode="drop"
    )
    stored = flat[:, None] == jnp.arange(owned, dtype=jnp.int32)[None, :]
    stored_sum = jnp.sum(jnp.where(stored, got_meta[:, :cap].reshape(-1)[:, None], 0.0), axis=0)
    accum_table = jnp.where(jnp.any(stored, axis=0), stored_sum, table_accum)
    order = jnp.arange(owners, dtype=jnp.int32)
    turned = (order ^ me)[:, None] == order[None, :]
    asked = jnp.sum(
        jnp.where(turned[:, :, None], got_meta[None, :, 2 * per : 3 * per], 0.0), axis=1
    )
    asked = asked.astype(jnp.int32).reshape(-1)
    is_meta = (jnp.arange(per) == per - 1)[None, :, None]
    reply_rows = jnp.take(table_new, asked, axis=0, mode="clip").reshape(owners, per, width)
    reply_accum = picked(accum_table, asked).reshape(owners, per)
    back = jnp.where(is_meta, meta_row([reply_accum], width), reply_rows)

    held = exchange(held, plane_groups())
    back = cross(cross(cross(back, 1), 16), 2)
    rows_new, accum_new = updated(
        slot_ids,
        cache_rows,
        cache_accum,
        (latent, dlatent, dlogit),
        (proj_u, proj_v, cross_bias[None, :], head[None, :]),
    )
    held, back, rows_new, accum_new = lax.optimization_barrier(
        (held, back, rows_new, accum_new)
    )
    held = jnp.sum(held, axis=0)
    held = (held + shift_z(held, 4)) + (shift_z(held, 2) + shift_z(held, -2))
    whole = jnp.broadcast_to(held[None], (4 * feats, *held.shape))
    whole, back = lax.optimization_barrier((whole, back))
    whole = exchange(whole, plane_groups())
    back = cross(cross(back, 4), 8)
    in_place = (miss_dest[:, 0] ^ me) * per + ranks(miss_dest[:, 0])
    rows_new = refilled(evict_slot, in_place, back.reshape(spots, width), rows_new)
    fetched_accum = picked(back[:, per - 1, :per].reshape(-1), in_place)
    filled = evict_slot[:, None] == jnp.arange(cells, dtype=jnp.int32)[None, :]
    filled_sum = jnp.sum(jnp.where(filled, fetched_accum[:, None], 0.0), axis=0)
    accum_new = jnp.where(jnp.any(filled, axis=0), filled_sum, accum_new.reshape(cells))
    whole, rows_new, accum_new = lax.optimization_barrier((whole, rows_new, accum_new))
    clipped_proj, clipped_vecs, loss_row = normalized(core, whole, swap_cores(whole))
    loss = loss_row[0, 0] / (count * 256)
    return (rows_new, accum_new, table_new, accum_table, clipped_proj, clipped_vecs, loss)


def solution(mesh):
    split = P(AXES)
    rows = P(AXES, None)
    return jax.shard_map(
        shards,
        mesh=mesh,
        in_specs=(
            rows,
            split,
            rows,
            split,
            rows,
            split,
            rows,
            split,
            rows,
            P(),
            P(),
            P(),
            P(),
        ),
        out_specs=(rows, split, rows, split, P(), P(), P()),
        check_vma=False,
    )
```

```python
import jax
import jax.numpy as jnp
from jax import lax
from jax.experimental import pallas as pl
from jax.experimental.pallas import tpu as pltpu
from jax.sharding import PartitionSpec as P

EPS = 1e-06
ETA = 0.05
AXES = ("trainer", "table")


def device_at(y, x, z, core):
    return (((y // 2 * 4 + x) * 2 + y % 2) * 8 + z % 8) * 2 + core


def plane_groups():
    return [
        [device_at(y, x, 2 * pair + core + b, core) for y in range(4) for x in range(4) for b in (0, 1)]
        for core in range(2)
        for pair in range(4)
    ]


def shift_z(value, step):
    there = [
        (device_at(y, x, z, core), device_at(y, x, z + step, core))
        for y in range(4)
        for x in range(4)
        for z in range(8)
        for core in range(2)
    ]
    return lax.ppermute(value, AXES, there)


def swap_cores(value):
    return lax.ppermute(value, AXES, [(i, i ^ 1) for i in range(256)])


def exchange(value, groups):
    return lax.all_to_all(
        value, AXES, split_axis=0, concat_axis=0, tiled=True, axis_index_groups=groups
    )


def ranks(owner):
    listed = owner.shape[0]
    order = jnp.arange(listed, dtype=jnp.int32)
    earlier = (owner[:, None] == owner[None, :]) & (order[None, :] < order[:, None])
    return jnp.sum(earlier.astype(jnp.int32), axis=1)


def picked(values, index):
    hit = index[:, None] == jnp.arange(values.shape[0], dtype=jnp.int32)[None, :]
    return jnp.sum(jnp.where(hit, values[None, :], 0.0), axis=1)


def cross(value, bit):
    split = value.reshape(value.shape[0] // (2 * bit), 2, bit, *value.shape[1:])
    there = [(i, i ^ bit) for i in range(256)]
    came = lax.ppermute(split[:, 1], AXES, there)
    return jnp.stack([split[:, 0], came], axis=1).reshape(value.shape)


def put_blocks(ref, c, grad):
    half = grad.shape[1] // 2
    rows = grad.shape[0] // 4
    for q in range(4):
        part = grad[q * rows : (q + 1) * rows, :]
        ref[4 * c + q, :rows, :] = part[:, :half]
        ref[4 * c + q, rows : 2 * rows, :] = part[:, half:]


def dense_kernel(
    core_ref,
    slots_ref,
    labels_ref,
    cache_any,
    u_any,
    v_any,
    bias_ref,
    head_ref,
    send_out,
    left_out,
    latent_ref,
    dlatent_ref,
    dlogit_ref,
    extra_ref,
    cache,
    u_ref,
    v_ref,
    send_ref,
    left,
    high,
    mid,
    low,
    pooled,
    shifted,
    dlift,
    in_sems,
    out_sems,
):
    f32, bf16 = jnp.float32, jnp.bfloat16
    count, (cells, width) = slots_ref.shape[1], cache.shape
    feats = u_ref.shape[0] // width
    looks = slots_ref.shape[0] // feats
    cuts = [slice(c * width, (c + 1) * width) for c in range(feats)]
    loads = []
    for source, target in ((cache_any, cache), (v_any, v_ref), (u_any, u_ref)):
        step = target.shape[0] // 4
        for part in range(4):
            rows = pl.ds(part * step, step)
            loads.append(
                pltpu.make_async_copy(source.at[rows], target.at[rows], in_sems.at[len(loads)])
            )
            loads[-1].start()
    slots = jnp.transpose(slots_ref[...])
    lane = lax.broadcasted_iota(jnp.int32, (count, cells), 1)

    def counted(f):
        counts = jnp.zeros((count, cells), f32)
        for look in range(looks):
            at = f * looks + look
            counts = counts + jnp.where(lane == slots[:, at : at + 1], 1.0, 0.0)
        return counts.astype(bf16)

    counts = counted(0)
    step = cells // 4
    for part in range(4):
        loads[part].wait()
        rows = cache[part * step : (part + 1) * step, :]
        first = rows.astype(bf16)
        rest = rows - first.astype(f32)
        second = rest.astype(bf16)
        high[part * step : (part + 1) * step, :] = first
        mid[part * step : (part + 1) * step, :] = second
        low[part * step : (part + 1) * step, :] = (rest - second.astype(f32)).astype(bf16)
    for f in range(feats):
        if f > 0:
            counts = counted(f)
        total = jnp.dot(counts, low[...], preferred_element_type=f32)
        total = total + jnp.dot(counts, mid[...], preferred_element_type=f32)
        total = total + jnp.dot(counts, high[...], preferred_element_type=f32)
        pooled[:, cuts[f]] = total.astype(bf16)

    for load in loads[4:]:
        load.wait()
    latent = jnp.dot(pooled[...], v_ref[...], preferred_element_type=f32).astype(bf16)
    latent_ref[...] = latent
    across = (((1,), (1,)), ((), ()))
    logit_wide = jnp.zeros((count, width), f32)
    for cut in cuts:
        moved = lax.dot_general(latent, u_ref[cut, :], across, preferred_element_type=f32)
        moved = moved + bias_ref[:, cut]
        shifted[:, cut] = moved
        part = pooled[:, cut].astype(f32)
        logit_wide = logit_wide + (part * moved + part) * head_ref[:, cut]
    logit = jnp.sum(logit_wide, axis=1, keepdims=True)
    target = jnp.transpose(labels_ref[...]).astype(f32)
    small = jnp.exp(-jnp.abs(logit))
    losses = jnp.maximum(logit, 0.0) + jnp.log1p(small) - target * logit
    loss = jnp.sum(losses, axis=0, keepdims=True)
    dlogit = jnp.where(logit >= 0, 1.0, small) / (1.0 + small) - target
    dlogit_ref[...] = jnp.transpose(dlogit)

    mine = core_ref[0] == 0
    half = width // 2
    lane1 = lax.broadcasted_iota(jnp.int32, (1, half), 1)
    loss_row = jnp.where(lane1 == 0, loss, 0.0)
    back = jnp.zeros((count, width), f32)
    for c, cut in enumerate(cuts):
        part = pooled[:, cut].astype(f32)
        lift = dlogit * head_ref[:, cut] * part
        crossed = part * shifted[:, cut] + part
        dbias = jnp.sum(lift, axis=0, keepdims=True)
        dhead = jnp.sum(dlogit * crossed, axis=0, keepdims=True)
        lift = lift.astype(bf16)
        dlift[:, cut] = lift
        back = back + jnp.dot(lift, u_ref[cut, :], preferred_element_type=f32)
        for ref, row in (
            (extra_ref, jnp.where(mine, dbias, dhead)),
            (send_ref, jnp.where(mine, dhead, dbias)),
        ):
            top = ref.shape[1] - 8
            for q in range(4):
                at = 4 * c + q
                ref[at, top : top + 8, :] = jnp.zeros((8, half), f32)
                ref[at, top + 1 : top + 2, :] = loss_row
                if q % 2 == 0:
                    ref[at, top : top + 1, :] = row[:, q // 2 * half : (q // 2 + 1) * half]
        left[:, cut] = jnp.where(mine, lift, pooled[:, cut])
    dlatent = back.astype(bf16)
    dlatent_ref[...] = dlatent
    copies = [pltpu.make_async_copy(left, left_out, out_sems.at[feats])]
    copies[0].start()
    right = jnp.where(mine, dlatent, latent)
    for c, cut in enumerate(cuts):
        grad = lax.dot_general(
            jnp.where(mine, pooled[:, cut], dlift[:, cut]),
            right,
            (((0,), (0,)), ((), ())),
            preferred_element_type=f32,
        )
        put_blocks(send_ref, c, grad)
        four = pl.ds(4 * c, 4)
        copies.append(
            pltpu.make_async_copy(send_ref.at[four], send_out.at[four], out_sems.at[c])
        )
        copies[-1].start()
    for copy in copies:
        copy.wait()


def dense(core, slot_ids, labels, cache_rows, proj_u, proj_v, cross_bias, head):
    count, (cells, width) = slot_ids.shape[0], cache_rows.shape
    wide = proj_u.shape[0]
    blocks = wide // width
    f32, bf16 = jnp.float32, jnp.bfloat16
    vmem = pl.BlockSpec(memory_space=pltpu.VMEM)
    anywhere = pl.BlockSpec(memory_space=pl.ANY)
    bundle = (4 * blocks, width // 2 + 8, width // 2)
    return pl.pallas_call(
        dense_kernel,
        out_shape=(
            jax.ShapeDtypeStruct(bundle, f32),
            jax.ShapeDtypeStruct((count, wide), bf16),
            jax.ShapeDtypeStruct((count, width), bf16),
            jax.ShapeDtypeStruct((count, width), bf16),
            jax.ShapeDtypeStruct((1, count), f32),
            jax.ShapeDtypeStruct((4 * blocks, 8, width // 2), f32),
        ),
        in_specs=[pl.BlockSpec(memory_space=pltpu.SMEM)]
        + [vmem] * 2
        + [anywhere] * 3
        + [vmem] * 2,
        out_specs=[anywhere] * 2 + [vmem] * 4,
        scratch_shapes=[
            pltpu.VMEM((cells, width), f32),
            pltpu.VMEM((wide, width), bf16),
            pltpu.VMEM((wide, width), bf16),
            pltpu.VMEM(bundle, f32),
            pltpu.VMEM((count, wide), bf16),
        ]
        + [pltpu.VMEM((cells, width), bf16)] * 3
        + [
            pltpu.VMEM((count, wide), bf16),
            pltpu.VMEM((count, wide), f32),
            pltpu.VMEM((count, wide), bf16),
            pltpu.SemaphoreType.DMA((12,)),
            pltpu.SemaphoreType.DMA((blocks + 1,)),
        ],
        compiler_params=pltpu.CompilerParams(vmem_limit_bytes=60 * 1024 * 1024),
        cost_estimate=pl.CostEstimate(
            flops=5_000_000_000, bytes_accessed=9_000_000, transcendentals=1000
        ),
        name="dense",
    )(
        core[None],
        slot_ids.T,
        labels[None, :],
        cache_rows,
        proj_u,
        proj_v,
        cross_bias[None, :],
        head[None, :],
    )


def keep_kernel(core_ref, left_ref, latent_ref, dlatent_ref, extra_ref, keep_ref):
    width = latent_ref.shape[1]
    right = jnp.where(core_ref[0] == 0, latent_ref[...], dlatent_ref[...])
    for c in range(keep_ref.shape[0] // 4):
        grad = lax.dot_general(
            left_ref[:, c * width : (c + 1) * width],
            right,
            (((0,), (0,)), ((), ())),
            preferred_element_type=jnp.float32,
        )
        put_blocks(keep_ref, c, grad)
    keep_ref[:, width // 2 :, :] = extra_ref[...]


def kept(core, left, latent, dlatent, extra):
    blocks, _, half = extra.shape
    vmem = pl.BlockSpec(memory_space=pltpu.VMEM)
    return pl.pallas_call(
        keep_kernel,
        out_shape=jax.ShapeDtypeStruct((blocks, half + 8, half), jnp.float32),
        in_specs=[pl.BlockSpec(memory_space=pltpu.SMEM)] + [vmem] * 4,
        out_specs=vmem,
        compiler_params=pltpu.CompilerParams(vmem_limit_bytes=16 * 1024 * 1024),
        cost_estimate=pl.CostEstimate(
            flops=300_000_000, bytes_accessed=4_000_000, transcendentals=0
        ),
        name="kept",
    )(core[None], left, latent, dlatent, extra)


def payload_kernel(
    slot_ref, evict_ref, miss_ref, accum_ref, cache_any, out_ref, taken, place, cache, sems
):
    owners, per = taken.shape[0], out_ref.shape[0] // taken.shape[0]
    width = out_ref.shape[1]
    listed = slot_ref.shape[0]
    step = cache.shape[0] // 4
    loads = []
    for part in range(4):
        rows = pl.ds(part * step, step)
        loads.append(pltpu.make_async_copy(cache_any.at[rows], cache.at[rows], sems.at[part]))
        loads[-1].start()
    lane = lax.broadcasted_iota(jnp.int32, (1, width), 1)
    base = jnp.where((lane >= per) & (lane < 2 * per), -1.0, 0.0)
    for o in range(owners):
        taken[o] = 0
        out_ref[o * per : o * per + per - 1, :] = jnp.zeros((per - 1, width), jnp.float32)
        out_ref[o * per + per - 1 : (o + 1) * per, :] = base

    def leave(i, _):
        owner = evict_ref[0, i]
        rank = taken[owner]
        taken[owner] = rank + 1
        place[i] = owner * per + rank
        spot = pl.ds(owner * per + per - 1, 1)
        meta = jnp.where(lane == rank, accum_ref[slot_ref[i]], out_ref[spot, :])
        row = evict_ref[1, i].astype(jnp.float32)
        out_ref[spot, :] = jnp.where(lane == per + rank, row, meta)
        return 0

    lax.fori_loop(0, listed, leave, 0, unroll=8)
    for o in range(owners):
        taken[o] = 0

    def ask(i, _):
        owner = miss_ref[0, i]
        rank = taken[owner]
        taken[owner] = rank + 1
        spot = pl.ds(owner * per + per - 1, 1)
        row = miss_ref[1, i].astype(jnp.float32)
        out_ref[spot, :] = jnp.where(lane == 2 * per + rank, row, out_ref[spot, :])
        return 0

    lax.fori_loop(0, listed, ask, 0, unroll=8)
    for load in loads:
        load.wait()

    def move(i, _):
        out_ref[pl.ds(place[i], 1), :] = cache[pl.ds(slot_ref[i], 1), :]
        return 0

    lax.fori_loop(0, listed, move, 0, unroll=8)


def payload(evict_slot, evict_dest, miss_dest, cache_accum, cache_rows, owners, per):
    smem = pl.BlockSpec(memory_space=pltpu.SMEM)
    return pl.pallas_call(
        payload_kernel,
        out_shape=jax.ShapeDtypeStruct((owners * per, cache_rows.shape[1]), jnp.float32),
        in_specs=[smem] * 4 + [pl.BlockSpec(memory_space=pl.ANY)],
        out_specs=pl.BlockSpec(memory_space=pltpu.VMEM),
        scratch_shapes=[
            pltpu.SMEM((owners,), jnp.int32),
            pltpu.SMEM(evict_slot.shape, jnp.int32),
            pltpu.VMEM(cache_rows.shape, jnp.float32),
            pltpu.SemaphoreType.DMA((4,)),
        ],
        compiler_params=pltpu.CompilerParams(vmem_limit_bytes=60 * 1024 * 1024),
        cost_estimate=pl.CostEstimate(flops=100_000, bytes_accessed=1_500_000, transcendentals=0),
        name="payload",
    )(evict_slot, evict_dest.T, miss_dest.T, cache_accum, cache_rows)


def update_kernel(
    slots_ref,
    cache_ref,
    accum_ref,
    latent_ref,
    dlatent_ref,
    dlogit_ref,
    u_ref,
    v_ref,
    bias_ref,
    head_ref,
    rows_ref,
    accum_out,
):
    f32, bf16 = jnp.float32, jnp.bfloat16
    (cells, width), count = cache_ref.shape, latent_ref.shape[0]
    feats = u_ref.shape[0] // width
    looks = slots_ref.shape[0] // feats
    across = (((1,), (1,)), ((), ()))
    latent, dlatent = latent_ref[...], dlatent_ref[...]
    dlogit = jnp.transpose(dlogit_ref[...])
    cell = lax.broadcasted_iota(jnp.int32, (cells, count), 0)
    grad = jnp.zeros((cells, width), f32)
    for f in range(feats):
        counts = jnp.zeros((cells, count), f32)
        for look in range(looks):
            at = f * looks + look
            counts = counts + jnp.where(cell == slots_ref[at : at + 1, :], 1.0, 0.0)
        cut = slice(f * width, (f + 1) * width)
        moved = lax.dot_general(latent, u_ref[cut, :], across, preferred_element_type=f32)
        moved = moved + bias_ref[:, cut]
        through = lax.dot_general(dlatent, v_ref[cut, :], across, preferred_element_type=f32)
        dpooled = (dlogit * head_ref[:, cut] * (moved + 1.0) + through).astype(bf16)
        grad = grad + jnp.dot(counts.astype(bf16), dpooled, preferred_element_type=f32)
    mean = jnp.sum(grad * grad, axis=1, keepdims=True) / width
    accum = jnp.transpose(accum_ref[...]) + mean
    rows_ref[...] = cache_ref[...] - ETA * grad * lax.rsqrt(accum)
    accum_out[...] = jnp.transpose(accum)


def refill_kernel(evict_ref, place_ref, back_ref, old_ref, rows_ref):
    rows_ref[...] = old_ref[...]

    def refill(i, _):
        rows_ref[pl.ds(evict_ref[i], 1), :] = back_ref[pl.ds(place_ref[i], 1), :]
        return 0

    lax.fori_loop(0, evict_ref.shape[0], refill, 0, unroll=8)


def updated(slot_ids, cache_rows, cache_accum, saved, params):
    cells = cache_rows.shape[0]
    vmem = pl.BlockSpec(memory_space=pltpu.VMEM)
    return pl.pallas_call(
        update_kernel,
        out_shape=(
            jax.ShapeDtypeStruct(cache_rows.shape, jnp.float32),
            jax.ShapeDtypeStruct((1, cells), jnp.float32),
        ),
        in_specs=[vmem] * 10,
        out_specs=(vmem, vmem),
        compiler_params=pltpu.CompilerParams(vmem_limit_bytes=60 * 1024 * 1024),
        cost_estimate=pl.CostEstimate(
            flops=1_100_000_000, bytes_accessed=4_000_000, transcendentals=1000
        ),
        name="update",
    )(slot_ids.T, cache_rows, cache_accum[None, :], *saved, *params)


def refilled(evict_slot, place, back, rows):
    smem = pl.BlockSpec(memory_space=pltpu.SMEM)
    vmem = pl.BlockSpec(memory_space=pltpu.VMEM)
    return pl.pallas_call(
        refill_kernel,
        out_shape=jax.ShapeDtypeStruct(rows.shape, jnp.float32),
        in_specs=[smem, smem, vmem, vmem],
        out_specs=vmem,
        compiler_params=pltpu.CompilerParams(vmem_limit_bytes=60 * 1024 * 1024),
        cost_estimate=pl.CostEstimate(flops=100_000, bytes_accessed=2_000_000, transcendentals=0),
        name="refill",
    )(evict_slot, place, back, rows)


def reply_kernel(
    me_ref,
    ids_ref,
    sums_ref,
    got_ref,
    table_any,
    accum_any,
    reply_ref,
    table_out,
    accum_out,
    table,
    accum,
    sems,
):
    owners, per = sums_ref.shape
    cap = per - 2
    width = got_ref.shape[1]
    step = table.shape[0] // 4
    loads = [pltpu.make_async_copy(accum_any, accum, sems.at[4])]
    stores = [pltpu.make_async_copy(accum, accum_out, sems.at[4])]
    for part in range(4):
        rows = pl.ds(part * step, step)
        loads.append(pltpu.make_async_copy(table_any.at[rows], table.at[rows], sems.at[part]))
        stores.append(pltpu.make_async_copy(table.at[rows], table_out.at[rows], sems.at[part]))
    for load in loads:
        load.start()
    for load in loads:
        load.wait()

    def store(s, _):
        for r in range(cap):
            row = ids_ref[s, per + r]

            @pl.when(row >= 0)
            def _():
                table[pl.ds(row, 1), :] = got_ref[pl.ds(s * per + r, 1), :]
                accum[row] = sums_ref[s, r]

        return 0

    lax.fori_loop(0, owners, store, 0, unroll=2)
    for copy in stores:
        copy.start()
    lane = lax.broadcasted_iota(jnp.int32, (1, width), 1)

    def answer(s, _):
        block = (s ^ me_ref[0]) * per
        meta = jnp.zeros((1, width), jnp.float32)
        for r in range(cap):
            row = ids_ref[s, 2 * per + r]
            reply_ref[pl.ds(block + r, 1), :] = table[pl.ds(row, 1), :]
            meta = jnp.where(lane == r, accum[row], meta)
        reply_ref[pl.ds(block + cap, 1), :] = jnp.zeros((1, width), jnp.float32)
        reply_ref[pl.ds(block + per - 1, 1), :] = meta
        return 0

    lax.fori_loop(0, owners, answer, 0, unroll=4)
    for copy in stores:
        copy.wait()


def replied(me, got, table_rows, table_accum):
    owners, per, width = got.shape
    smem = pl.BlockSpec(memory_space=pltpu.SMEM)
    vmem = pl.BlockSpec(memory_space=pltpu.VMEM)
    anywhere = pl.BlockSpec(memory_space=pl.ANY)
    meta = got[:, per - 1, : 3 * per]
    return pl.pallas_call(
        reply_kernel,
        out_shape=(
            jax.ShapeDtypeStruct((owners * per, width), jnp.float32),
            jax.ShapeDtypeStruct(table_rows.shape, jnp.float32),
            jax.ShapeDtypeStruct(table_accum.shape, jnp.float32),
        ),
        in_specs=[smem, smem, smem, vmem, anywhere, anywhere],
        out_specs=(vmem, anywhere, anywhere),
        scratch_shapes=[
            pltpu.VMEM(table_rows.shape, jnp.float32),
            pltpu.SMEM(table_accum.shape, jnp.float32),
            pltpu.SemaphoreType.DMA((5,)),
        ],
        compiler_params=pltpu.CompilerParams(vmem_limit_bytes=60 * 1024 * 1024),
        cost_estimate=pl.CostEstimate(flops=100_000, bytes_accessed=3_000_000, transcendentals=0),
        name="reply",
    )(
        me[None],
        meta.astype(jnp.int32),
        meta[:, :per],
        got.reshape(owners * per, width),
        table_rows,
        table_accum,
    )


def scaled(index, half_any, proj_ref, half, stage, in_sems, out_sems):
    chunks, width = stage.shape[0], stage.shape[2]
    edge, rows = width // 2, width // 4
    loads = []
    for c in range(chunks):
        four = pl.ds(4 * c, 4)
        loads.append(pltpu.make_async_copy(half_any.at[four], half.at[four], in_sems.at[c]))
        loads[-1].start()
    squares = jnp.zeros((edge, edge), jnp.float32)
    for c in range(chunks):
        loads[c].wait()
        for q in range(4):
            block = half[4 * c + q, :edge, :]
            squares = squares + block * block
    total = jnp.sum(jnp.sum(squares, axis=0, keepdims=True), axis=1, keepdims=True)
    scale = lax.rsqrt(total / (chunks * width * width) + EPS)
    copies = []
    for c in range(chunks):
        for q in range(4):
            at = slice(q * rows, (q + 1) * rows)
            stage[c, at, :edge] = half[4 * c + q, :rows, :] * scale
            stage[c, at, edge:] = half[4 * c + q, rows:edge, :] * scale
        copies.append(
            pltpu.make_async_copy(
                stage.at[c], proj_ref.at[index, pl.ds(c * width, width), :], out_sems.at[c]
            )
        )
        copies[-1].start()
    return copies


def own_kernel(core_ref, half_any, proj_ref, half, stage, in_sems, out_sems):
    for copy in scaled(core_ref[0], half_any, proj_ref, half, stage, in_sems, out_sems):
        copy.wait()


def other_kernel(
    core_ref,
    proj_in,
    own_ref,
    half_any,
    proj_ref,
    vec_ref,
    loss_ref,
    half,
    stage,
    in_sems,
    out_sems,
):
    core = core_ref[0]
    copies = scaled(1 - core, half_any, proj_ref, half, stage, in_sems, out_sems)
    edge = half.shape[2]
    tiles = vec_ref.shape[1] // edge
    mine = core == 0
    own = [own_ref[2 * t, 0:1, :] for t in range(tiles)]
    far = [half[2 * t, edge : edge + 1, :] for t in range(tiles)]
    for index in (0, 1):
        rows = [jnp.where(mine, *((a, b) if index == 0 else (b, a))) for a, b in zip(own, far)]
        squares = sum(row * row for row in rows)
        total = jnp.sum(squares, axis=1, keepdims=True)
        scale = lax.rsqrt(total / (tiles * edge) + EPS)
        for t in range(tiles):
            vec_ref[index : index + 1, t * edge : (t + 1) * edge] = rows[t] * scale
    loss_ref[...] = jnp.where(mine, half[0, edge + 1 : edge + 2, :], own_ref[0, 1:2, :])
    for copy in copies:
        copy.wait()


def normalized(core, own, other):
    blocks, depth, edge = own.shape
    chunks, width = blocks // 4, 2 * edge
    wide = chunks * width
    smem = pl.BlockSpec(memory_space=pltpu.SMEM)
    vmem = pl.BlockSpec(memory_space=pltpu.VMEM)
    anywhere = pl.BlockSpec(memory_space=pl.ANY)
    scratch = [
        pltpu.VMEM(own.shape, jnp.float32),
        pltpu.VMEM((chunks, width, width), jnp.float32),
        pltpu.SemaphoreType.DMA((chunks,)),
        pltpu.SemaphoreType.DMA((chunks,)),
    ]
    proj = jax.ShapeDtypeStruct((2, wide, width), jnp.float32)
    limit = pltpu.CompilerParams(vmem_limit_bytes=16 * 1024 * 1024)
    half = pl.pallas_call(
        own_kernel,
        out_shape=proj,
        in_specs=[smem, anywhere],
        out_specs=anywhere,
        scratch_shapes=scratch,
        compiler_params=limit,
        name="scale_own",
    )(core[None], own)
    return pl.pallas_call(
        other_kernel,
        out_shape=(
            proj,
            jax.ShapeDtypeStruct((2, wide), jnp.float32),
            jax.ShapeDtypeStruct((1, 128), jnp.float32),
        ),
        in_specs=[smem, anywhere, vmem, anywhere],
        out_specs=(anywhere, vmem, vmem),
        scratch_shapes=scratch,
        input_output_aliases={1: 0},
        compiler_params=limit,
        name="scale_other",
    )(core[None], half, own[:, edge:, :], other)


def shards(
    slot_ids,
    labels,
    cache_rows,
    cache_accum,
    table_rows,
    table_accum,
    miss_dest,
    evict_slot,
    evict_dest,
    proj_u,
    proj_v,
    cross_bias,
    head,
):
    owners = 32
    per = 8
    width = cache_rows.shape[1]
    cells = cache_rows.shape[0]
    spots = owners * per
    core = lax.axis_index("table") % 2

    me = lax.axis_index("table")
    sent = payload(
        evict_slot, evict_dest, miss_dest, cache_accum, cache_rows, owners, per
    ).reshape(owners, per, width)
    sent, slots_late = lax.optimization_barrier((sent, slot_ids))
    got = lax.all_to_all(sent, "table", split_axis=0, concat_axis=0, tiled=True)

    count = slot_ids.shape[0]
    feats = proj_u.shape[0] // width
    send, left, latent, dlatent, dlogit, extra = dense(
        core, slots_late, labels, cache_rows, proj_u, proj_v, cross_bias, head
    )

    send, got = lax.optimization_barrier((send, got))
    held = kept(core, left, latent, dlatent, extra) + swap_cores(send)
    held, got = lax.optimization_barrier((held, got))

    reply, table_new, accum_table = replied(me, got, table_rows, table_accum)
    back = reply.reshape(owners, per, width)

    held = exchange(held, plane_groups())
    back = cross(cross(cross(back, 1), 16), 2)
    rows_new, accum_new = updated(
        slot_ids,
        cache_rows,
        cache_accum,
        (latent, dlatent, dlogit),
        (proj_u, proj_v, cross_bias[None, :], head[None, :]),
    )
    held, back, rows_new, accum_new = lax.optimization_barrier(
        (held, back, rows_new, accum_new)
    )
    held = jnp.sum(held, axis=0)
    held = (held + shift_z(held, 4)) + (shift_z(held, 2) + shift_z(held, -2))
    back = cross(back, 4)
    held, back = lax.optimization_barrier((held, back))
    whole = jnp.broadcast_to(held[None], (4 * feats, *held.shape))
    whole = exchange(whole, plane_groups())
    back = cross(back, 8)
    in_place = (miss_dest[:, 0] ^ me) * per + ranks(miss_dest[:, 0])
    rows_new = refilled(evict_slot, in_place, back.reshape(spots, width), rows_new)
    fetched_accum = picked(back[:, per - 1, :per].reshape(-1), in_place)
    filled = evict_slot[:, None] == jnp.arange(cells, dtype=jnp.int32)[None, :]
    filled_sum = jnp.sum(jnp.where(filled, fetched_accum[:, None], 0.0), axis=0)
    accum_new = jnp.where(jnp.any(filled, axis=0), filled_sum, accum_new.reshape(cells))
    whole, rows_new, accum_new = lax.optimization_barrier((whole, rows_new, accum_new))
    clipped_proj, clipped_vecs, loss_row = normalized(core, whole, swap_cores(whole))
    loss = loss_row[0, 0] / (count * 256)
    return (rows_new, accum_new, table_new, accum_table, clipped_proj, clipped_vecs, loss)


def solution(mesh):
    split = P(AXES)
    rows = P(AXES, None)
    return jax.shard_map(
        shards,
        mesh=mesh,
        in_specs=(
            rows,
            split,
            rows,
            split,
            rows,
            split,
            rows,
            split,
            rows,
            P(),
            P(),
            P(),
            P(),
        ),
        out_specs=(rows, split, rows, split, P(), P(), P()),
        check_vma=False,
    )
```

```python
import jax
import jax.numpy as jnp
from jax import lax
from jax.experimental import pallas as pl
from jax.experimental.pallas import tpu as pltpu
from jax.sharding import PartitionSpec as P

EPS = 1e-06
ETA = 0.05
AXES = ("trainer", "table")


def device_at(y, x, z, core):
    return (((y // 2 * 4 + x) * 2 + y % 2) * 8 + z % 8) * 2 + core


def plane_groups():
    return [
        [device_at(y, x, 2 * pair + core + b, core) for y in range(4) for x in range(4) for b in (0, 1)]
        for core in range(2)
        for pair in range(4)
    ]


def shift_z(value, step):
    there = [
        (device_at(y, x, z, core), device_at(y, x, z + step, core))
        for y in range(4)
        for x in range(4)
        for z in range(8)
        for core in range(2)
    ]
    return lax.ppermute(value, AXES, there)


def swap_cores(value):
    return lax.ppermute(value, AXES, [(i, i ^ 1) for i in range(256)])


def exchange(value, groups):
    return lax.all_to_all(
        value, AXES, split_axis=0, concat_axis=0, tiled=True, axis_index_groups=groups
    )


def ranks(owner):
    listed = owner.shape[0]
    order = jnp.arange(listed, dtype=jnp.int32)
    earlier = (owner[:, None] == owner[None, :]) & (order[None, :] < order[:, None])
    return jnp.sum(earlier.astype(jnp.int32), axis=1)


def picked(values, index):
    hit = index[:, None] == jnp.arange(values.shape[0], dtype=jnp.int32)[None, :]
    return jnp.sum(jnp.where(hit, values[None, :], 0.0), axis=1)


def cross(value, bit):
    split = value.reshape(value.shape[0] // (2 * bit), 2, bit, *value.shape[1:])
    there = [(i, i ^ bit) for i in range(256)]
    came = lax.ppermute(split[:, 1], AXES, there)
    return jnp.stack([split[:, 0], came], axis=1).reshape(value.shape)


def put_blocks(ref, c, grad):
    half = grad.shape[1] // 2
    rows = grad.shape[0] // 4
    for q in range(4):
        part = grad[q * rows : (q + 1) * rows, :]
        ref[4 * c + q, :rows, :] = part[:, :half]
        ref[4 * c + q, rows : 2 * rows, :] = part[:, half:]


def dense_kernel(
    core_ref,
    slots_ref,
    labels_ref,
    cache_any,
    u_any,
    v_any,
    bias_ref,
    head_ref,
    send_out,
    left_out,
    latent_ref,
    dlatent_ref,
    dlogit_ref,
    extra_ref,
    cache,
    u_ref,
    v_ref,
    send_ref,
    left,
    high,
    mid,
    low,
    pooled,
    shifted,
    dlift,
    in_sems,
    out_sems,
):
    f32, bf16 = jnp.float32, jnp.bfloat16
    count, (cells, width) = slots_ref.shape[1], cache.shape
    feats = u_ref.shape[0] // width
    looks = slots_ref.shape[0] // feats
    cuts = [slice(c * width, (c + 1) * width) for c in range(feats)]
    loads = []
    for source, target in ((cache_any, cache), (v_any, v_ref), (u_any, u_ref)):
        step = target.shape[0] // 4
        for part in range(4):
            rows = pl.ds(part * step, step)
            loads.append(
                pltpu.make_async_copy(source.at[rows], target.at[rows], in_sems.at[len(loads)])
            )
            loads[-1].start()
    slots = jnp.transpose(slots_ref[...])
    lane = lax.broadcasted_iota(jnp.int32, (count, cells), 1)

    def counted(f):
        counts = jnp.zeros((count, cells), f32)
        for look in range(looks):
            at = f * looks + look
            counts = counts + jnp.where(lane == slots[:, at : at + 1], 1.0, 0.0)
        return counts.astype(bf16)

    counts = counted(0)
    step = cells // 4
    for part in range(4):
        loads[part].wait()
        rows = cache[part * step : (part + 1) * step, :]
        first = rows.astype(bf16)
        rest = rows - first.astype(f32)
        second = rest.astype(bf16)
        high[part * step : (part + 1) * step, :] = first
        mid[part * step : (part + 1) * step, :] = second
        low[part * step : (part + 1) * step, :] = (rest - second.astype(f32)).astype(bf16)
    for f in range(feats):
        if f > 0:
            counts = counted(f)
        total = jnp.dot(counts, low[...], preferred_element_type=f32)
        total = total + jnp.dot(counts, mid[...], preferred_element_type=f32)
        total = total + jnp.dot(counts, high[...], preferred_element_type=f32)
        pooled[:, cuts[f]] = total.astype(bf16)

    for load in loads[4:]:
        load.wait()
    latent = jnp.dot(pooled[...], v_ref[...], preferred_element_type=f32).astype(bf16)
    latent_ref[...] = latent
    across = (((1,), (1,)), ((), ()))
    logit_wide = jnp.zeros((count, width), f32)
    for cut in cuts:
        moved = lax.dot_general(latent, u_ref[cut, :], across, preferred_element_type=f32)
        moved = moved + bias_ref[:, cut]
        shifted[:, cut] = moved
        part = pooled[:, cut].astype(f32)
        logit_wide = logit_wide + (part * moved + part) * head_ref[:, cut]
    logit = jnp.sum(logit_wide, axis=1, keepdims=True)
    target = jnp.transpose(labels_ref[...]).astype(f32)
    small = jnp.exp(-jnp.abs(logit))
    losses = jnp.maximum(logit, 0.0) + jnp.log1p(small) - target * logit
    loss = jnp.sum(losses, axis=0, keepdims=True)
    dlogit = jnp.where(logit >= 0, 1.0, small) / (1.0 + small) - target
    dlogit_ref[...] = jnp.transpose(dlogit)

    mine = core_ref[0] == 0
    half = width // 2
    lane1 = lax.broadcasted_iota(jnp.int32, (1, half), 1)
    loss_row = jnp.where(lane1 == 0, loss, 0.0)
    back = jnp.zeros((count, width), f32)
    for c, cut in enumerate(cuts):
        part = pooled[:, cut].astype(f32)
        lift = dlogit * head_ref[:, cut] * part
        crossed = part * shifted[:, cut] + part
        dbias = jnp.sum(lift, axis=0, keepdims=True)
        dhead = jnp.sum(dlogit * crossed, axis=0, keepdims=True)
        lift = lift.astype(bf16)
        dlift[:, cut] = lift
        back = back + jnp.dot(lift, u_ref[cut, :], preferred_element_type=f32)
        for ref, row in (
            (extra_ref, jnp.where(mine, dbias, dhead)),
            (send_ref, jnp.where(mine, dhead, dbias)),
        ):
            top = ref.shape[1] - 8
            for q in range(4):
                at = 4 * c + q
                ref[at, top : top + 8, :] = jnp.zeros((8, half), f32)
                ref[at, top + 1 : top + 2, :] = loss_row
                if q % 2 == 0:
                    ref[at, top : top + 1, :] = row[:, q // 2 * half : (q // 2 + 1) * half]
        left[:, cut] = jnp.where(mine, lift, pooled[:, cut])
    dlatent = back.astype(bf16)
    dlatent_ref[...] = dlatent
    copies = [pltpu.make_async_copy(left, left_out, out_sems.at[feats])]
    copies[0].start()
    right = jnp.where(mine, dlatent, latent)
    for c, cut in enumerate(cuts):
        grad = lax.dot_general(
            jnp.where(mine, pooled[:, cut], dlift[:, cut]),
            right,
            (((0,), (0,)), ((), ())),
            preferred_element_type=f32,
        )
        put_blocks(send_ref, c, grad)
        four = pl.ds(4 * c, 4)
        copies.append(
            pltpu.make_async_copy(send_ref.at[four], send_out.at[four], out_sems.at[c])
        )
        copies[-1].start()
    for copy in copies:
        copy.wait()


def dense(core, slot_ids, labels, cache_rows, proj_u, proj_v, cross_bias, head):
    count, (cells, width) = slot_ids.shape[0], cache_rows.shape
    wide = proj_u.shape[0]
    blocks = wide // width
    f32, bf16 = jnp.float32, jnp.bfloat16
    vmem = pl.BlockSpec(memory_space=pltpu.VMEM)
    anywhere = pl.BlockSpec(memory_space=pl.ANY)
    bundle = (4 * blocks, width // 2 + 8, width // 2)
    return pl.pallas_call(
        dense_kernel,
        out_shape=(
            jax.ShapeDtypeStruct(bundle, f32),
            jax.ShapeDtypeStruct((count, wide), bf16),
            jax.ShapeDtypeStruct((count, width), bf16),
            jax.ShapeDtypeStruct((count, width), bf16),
            jax.ShapeDtypeStruct((1, count), f32),
            jax.ShapeDtypeStruct((4 * blocks, 8, width // 2), f32),
        ),
        in_specs=[pl.BlockSpec(memory_space=pltpu.SMEM)]
        + [vmem] * 2
        + [anywhere] * 3
        + [vmem] * 2,
        out_specs=[anywhere] * 2 + [vmem] * 4,
        scratch_shapes=[
            pltpu.VMEM((cells, width), f32),
            pltpu.VMEM((wide, width), bf16),
            pltpu.VMEM((wide, width), bf16),
            pltpu.VMEM(bundle, f32),
            pltpu.VMEM((count, wide), bf16),
        ]
        + [pltpu.VMEM((cells, width), bf16)] * 3
        + [
            pltpu.VMEM((count, wide), bf16),
            pltpu.VMEM((count, wide), f32),
            pltpu.VMEM((count, wide), bf16),
            pltpu.SemaphoreType.DMA((12,)),
            pltpu.SemaphoreType.DMA((blocks + 1,)),
        ],
        compiler_params=pltpu.CompilerParams(vmem_limit_bytes=60 * 1024 * 1024),
        cost_estimate=pl.CostEstimate(
            flops=5_000_000_000, bytes_accessed=9_000_000, transcendentals=1000
        ),
        name="dense",
    )(
        core[None],
        slot_ids.T,
        labels[None, :],
        cache_rows,
        proj_u,
        proj_v,
        cross_bias[None, :],
        head[None, :],
    )


def keep_kernel(core_ref, left_ref, latent_ref, dlatent_ref, extra_ref, keep_ref):
    width = latent_ref.shape[1]
    right = jnp.where(core_ref[0] == 0, latent_ref[...], dlatent_ref[...])
    for c in range(keep_ref.shape[0] // 4):
        grad = lax.dot_general(
            left_ref[:, c * width : (c + 1) * width],
            right,
            (((0,), (0,)), ((), ())),
            preferred_element_type=jnp.float32,
        )
        put_blocks(keep_ref, c, grad)
    keep_ref[:, width // 2 :, :] = extra_ref[...]


def kept(core, left, latent, dlatent, extra):
    blocks, _, half = extra.shape
    vmem = pl.BlockSpec(memory_space=pltpu.VMEM)
    return pl.pallas_call(
        keep_kernel,
        out_shape=jax.ShapeDtypeStruct((blocks, half + 8, half), jnp.float32),
        in_specs=[pl.BlockSpec(memory_space=pltpu.SMEM)] + [vmem] * 4,
        out_specs=vmem,
        compiler_params=pltpu.CompilerParams(vmem_limit_bytes=16 * 1024 * 1024),
        cost_estimate=pl.CostEstimate(
            flops=300_000_000, bytes_accessed=4_000_000, transcendentals=0
        ),
        name="kept",
    )(core[None], left, latent, dlatent, extra)


def payload_kernel(
    slot_ref, evict_ref, miss_ref, accum_ref, cache_any, out_ref, taken, place, cache, sems
):
    owners, per = taken.shape[0], out_ref.shape[0] // taken.shape[0]
    width = out_ref.shape[1]
    listed = slot_ref.shape[0]
    step = cache.shape[0] // 4
    loads = []
    for part in range(4):
        rows = pl.ds(part * step, step)
        loads.append(pltpu.make_async_copy(cache_any.at[rows], cache.at[rows], sems.at[part]))
        loads[-1].start()
    lane = lax.broadcasted_iota(jnp.int32, (1, width), 1)
    base = jnp.where((lane >= per) & (lane < 2 * per), -1.0, 0.0)
    for o in range(owners):
        taken[o] = 0
        out_ref[o * per : o * per + per - 1, :] = jnp.zeros((per - 1, width), jnp.float32)
        out_ref[o * per + per - 1 : (o + 1) * per, :] = base

    def leave(i, _):
        owner = evict_ref[0, i]
        rank = taken[owner]
        taken[owner] = rank + 1
        place[i] = owner * per + rank
        spot = pl.ds(owner * per + per - 1, 1)
        meta = jnp.where(lane == rank, accum_ref[slot_ref[i]], out_ref[spot, :])
        row = evict_ref[1, i].astype(jnp.float32)
        out_ref[spot, :] = jnp.where(lane == per + rank, row, meta)
        return 0

    lax.fori_loop(0, listed, leave, 0, unroll=8)
    for o in range(owners):
        taken[o] = 0

    def ask(i, _):
        owner = miss_ref[0, i]
        rank = taken[owner]
        taken[owner] = rank + 1
        spot = pl.ds(owner * per + per - 1, 1)
        row = miss_ref[1, i].astype(jnp.float32)
        out_ref[spot, :] = jnp.where(lane == 2 * per + rank, row, out_ref[spot, :])
        return 0

    lax.fori_loop(0, listed, ask, 0, unroll=8)
    for load in loads:
        load.wait()

    def move(i, _):
        out_ref[pl.ds(place[i], 1), :] = cache[pl.ds(slot_ref[i], 1), :]
        return 0

    lax.fori_loop(0, listed, move, 0, unroll=8)


def payload(evict_slot, evict_dest, miss_dest, cache_accum, cache_rows, owners, per):
    smem = pl.BlockSpec(memory_space=pltpu.SMEM)
    return pl.pallas_call(
        payload_kernel,
        out_shape=jax.ShapeDtypeStruct((owners * per, cache_rows.shape[1]), jnp.float32),
        in_specs=[smem] * 4 + [pl.BlockSpec(memory_space=pl.ANY)],
        out_specs=pl.BlockSpec(memory_space=pltpu.VMEM),
        scratch_shapes=[
            pltpu.SMEM((owners,), jnp.int32),
            pltpu.SMEM(evict_slot.shape, jnp.int32),
            pltpu.VMEM(cache_rows.shape, jnp.float32),
            pltpu.SemaphoreType.DMA((4,)),
        ],
        compiler_params=pltpu.CompilerParams(vmem_limit_bytes=60 * 1024 * 1024),
        cost_estimate=pl.CostEstimate(flops=100_000, bytes_accessed=1_500_000, transcendentals=0),
        name="payload",
    )(evict_slot, evict_dest.T, miss_dest.T, cache_accum, cache_rows)


def update_kernel(
    slots_ref,
    cache_ref,
    accum_ref,
    latent_ref,
    dlatent_ref,
    dlogit_ref,
    u_ref,
    v_ref,
    bias_ref,
    head_ref,
    rows_ref,
    accum_out,
):
    f32, bf16 = jnp.float32, jnp.bfloat16
    (cells, width), count = cache_ref.shape, latent_ref.shape[0]
    feats = u_ref.shape[0] // width
    looks = slots_ref.shape[0] // feats
    across = (((1,), (1,)), ((), ()))
    latent, dlatent = latent_ref[...], dlatent_ref[...]
    dlogit = jnp.transpose(dlogit_ref[...])
    cell = lax.broadcasted_iota(jnp.int32, (cells, count), 0)
    grad = jnp.zeros((cells, width), f32)
    for f in range(feats):
        counts = jnp.zeros((cells, count), f32)
        for look in range(looks):
            at = f * looks + look
            counts = counts + jnp.where(cell == slots_ref[at : at + 1, :], 1.0, 0.0)
        cut = slice(f * width, (f + 1) * width)
        moved = lax.dot_general(latent, u_ref[cut, :], across, preferred_element_type=f32)
        moved = moved + bias_ref[:, cut]
        through = lax.dot_general(dlatent, v_ref[cut, :], across, preferred_element_type=f32)
        dpooled = (dlogit * head_ref[:, cut] * (moved + 1.0) + through).astype(bf16)
        grad = grad + jnp.dot(counts.astype(bf16), dpooled, preferred_element_type=f32)
    mean = jnp.sum(grad * grad, axis=1, keepdims=True) / width
    accum = jnp.transpose(accum_ref[...]) + mean
    rows_ref[...] = cache_ref[...] - ETA * grad * lax.rsqrt(accum)
    accum_out[...] = jnp.transpose(accum)


def refill_kernel(evict_ref, place_ref, back_ref, old_ref, rows_ref):
    rows_ref[...] = old_ref[...]

    def refill(i, _):
        rows_ref[pl.ds(evict_ref[i], 1), :] = back_ref[pl.ds(place_ref[i], 1), :]
        return 0

    lax.fori_loop(0, evict_ref.shape[0], refill, 0, unroll=8)


def updated(slot_ids, cache_rows, cache_accum, saved, params):
    cells = cache_rows.shape[0]
    vmem = pl.BlockSpec(memory_space=pltpu.VMEM)
    return pl.pallas_call(
        update_kernel,
        out_shape=(
            jax.ShapeDtypeStruct(cache_rows.shape, jnp.float32),
            jax.ShapeDtypeStruct((1, cells), jnp.float32),
        ),
        in_specs=[vmem] * 10,
        out_specs=(vmem, vmem),
        compiler_params=pltpu.CompilerParams(vmem_limit_bytes=60 * 1024 * 1024),
        cost_estimate=pl.CostEstimate(
            flops=1_100_000_000, bytes_accessed=4_000_000, transcendentals=1000
        ),
        name="update",
    )(slot_ids.T, cache_rows, cache_accum[None, :], *saved, *params)


def refilled(evict_slot, place, back, rows):
    smem = pl.BlockSpec(memory_space=pltpu.SMEM)
    vmem = pl.BlockSpec(memory_space=pltpu.VMEM)
    return pl.pallas_call(
        refill_kernel,
        out_shape=jax.ShapeDtypeStruct(rows.shape, jnp.float32),
        in_specs=[smem, smem, vmem, vmem],
        out_specs=vmem,
        compiler_params=pltpu.CompilerParams(vmem_limit_bytes=60 * 1024 * 1024),
        cost_estimate=pl.CostEstimate(flops=100_000, bytes_accessed=2_000_000, transcendentals=0),
        name="refill",
    )(evict_slot, place, back, rows)


def reply_kernel(
    me_ref,
    ids_ref,
    sums_ref,
    got_ref,
    table_any,
    accum_any,
    reply_ref,
    table_out,
    accum_out,
    table,
    accum,
    sems,
):
    owners, per = sums_ref.shape
    cap = per - 2
    width = got_ref.shape[1]
    step = table.shape[0] // 4
    loads = [pltpu.make_async_copy(accum_any, accum, sems.at[4])]
    stores = [pltpu.make_async_copy(accum, accum_out, sems.at[4])]
    for part in range(4):
        rows = pl.ds(part * step, step)
        loads.append(pltpu.make_async_copy(table_any.at[rows], table.at[rows], sems.at[part]))
        stores.append(pltpu.make_async_copy(table.at[rows], table_out.at[rows], sems.at[part]))
    for load in loads:
        load.start()
    for load in loads:
        load.wait()

    def store(s, _):
        for r in range(cap):
            row = ids_ref[s, per + r]

            @pl.when(row >= 0)
            def _():
                table[pl.ds(row, 1), :] = got_ref[pl.ds(s * per + r, 1), :]
                accum[row] = sums_ref[s, r]

        return 0

    lax.fori_loop(0, owners, store, 0, unroll=2)
    for copy in stores:
        copy.start()
    lane = lax.broadcasted_iota(jnp.int32, (1, width), 1)

    def answer(s, _):
        block = (s ^ me_ref[0]) * per
        meta = jnp.zeros((1, width), jnp.float32)
        for r in range(cap):
            row = ids_ref[s, 2 * per + r]
            reply_ref[pl.ds(block + r, 1), :] = table[pl.ds(row, 1), :]
            meta = jnp.where(lane == r, accum[row], meta)
        reply_ref[pl.ds(block + cap, 1), :] = jnp.zeros((1, width), jnp.float32)
        reply_ref[pl.ds(block + per - 1, 1), :] = meta
        return 0

    lax.fori_loop(0, owners, answer, 0, unroll=4)
    for copy in stores:
        copy.wait()


def replied(me, got, table_rows, table_accum):
    owners, per, width = got.shape
    smem = pl.BlockSpec(memory_space=pltpu.SMEM)
    vmem = pl.BlockSpec(memory_space=pltpu.VMEM)
    anywhere = pl.BlockSpec(memory_space=pl.ANY)
    meta = got[:, per - 1, : 3 * per]
    return pl.pallas_call(
        reply_kernel,
        out_shape=(
            jax.ShapeDtypeStruct((owners * per, width), jnp.float32),
            jax.ShapeDtypeStruct(table_rows.shape, jnp.float32),
            jax.ShapeDtypeStruct(table_accum.shape, jnp.float32),
        ),
        in_specs=[smem, smem, smem, vmem, anywhere, anywhere],
        out_specs=(vmem, anywhere, anywhere),
        scratch_shapes=[
            pltpu.VMEM(table_rows.shape, jnp.float32),
            pltpu.SMEM(table_accum.shape, jnp.float32),
            pltpu.SemaphoreType.DMA((5,)),
        ],
        compiler_params=pltpu.CompilerParams(vmem_limit_bytes=60 * 1024 * 1024),
        cost_estimate=pl.CostEstimate(flops=100_000, bytes_accessed=3_000_000, transcendentals=0),
        name="reply",
    )(
        me[None],
        meta.astype(jnp.int32),
        meta[:, :per],
        got.reshape(owners * per, width),
        table_rows,
        table_accum,
    )


def scaled(index, half_any, proj_ref, half, stage, in_sems, out_sems):
    chunks, width = stage.shape[0], stage.shape[2]
    edge, rows = width // 2, width // 4
    loads = []
    for c in range(chunks):
        four = pl.ds(4 * c, 4)
        loads.append(pltpu.make_async_copy(half_any.at[four], half.at[four], in_sems.at[c]))
        loads[-1].start()
    squares = jnp.zeros((edge, edge), jnp.float32)
    for c in range(chunks):
        loads[c].wait()
        for q in range(4):
            block = half[4 * c + q, :edge, :]
            squares = squares + block * block
    total = jnp.sum(jnp.sum(squares, axis=0, keepdims=True), axis=1, keepdims=True)
    scale = lax.rsqrt(total / (chunks * width * width) + EPS)
    copies = []
    for c in range(chunks):
        for q in range(4):
            at = slice(q * rows, (q + 1) * rows)
            stage[c, at, :edge] = half[4 * c + q, :rows, :] * scale
            stage[c, at, edge:] = half[4 * c + q, rows:edge, :] * scale
        copies.append(
            pltpu.make_async_copy(
                stage.at[c], proj_ref.at[index, pl.ds(c * width, width), :], out_sems.at[c]
            )
        )
        copies[-1].start()
    return copies


def own_kernel(core_ref, half_any, proj_ref, half, stage, in_sems, out_sems):
    for copy in scaled(core_ref[0], half_any, proj_ref, half, stage, in_sems, out_sems):
        copy.wait()


def other_kernel(
    core_ref,
    proj_in,
    own_ref,
    half_any,
    proj_ref,
    vec_ref,
    loss_ref,
    half,
    stage,
    in_sems,
    out_sems,
):
    core = core_ref[0]
    copies = scaled(1 - core, half_any, proj_ref, half, stage, in_sems, out_sems)
    edge = half.shape[2]
    tiles = vec_ref.shape[1] // edge
    mine = core == 0
    own = [own_ref[2 * t, 0:1, :] for t in range(tiles)]
    far = [half[2 * t, edge : edge + 1, :] for t in range(tiles)]
    for index in (0, 1):
        rows = [jnp.where(mine, *((a, b) if index == 0 else (b, a))) for a, b in zip(own, far)]
        squares = sum(row * row for row in rows)
        total = jnp.sum(squares, axis=1, keepdims=True)
        scale = lax.rsqrt(total / (tiles * edge) + EPS)
        for t in range(tiles):
            vec_ref[index : index + 1, t * edge : (t + 1) * edge] = rows[t] * scale
    loss_ref[...] = jnp.where(mine, half[0, edge + 1 : edge + 2, :], own_ref[0, 1:2, :])
    for copy in copies:
        copy.wait()


def normalized(core, own, other):
    blocks, depth, edge = own.shape
    chunks, width = blocks // 4, 2 * edge
    wide = chunks * width
    smem = pl.BlockSpec(memory_space=pltpu.SMEM)
    vmem = pl.BlockSpec(memory_space=pltpu.VMEM)
    anywhere = pl.BlockSpec(memory_space=pl.ANY)
    scratch = [
        pltpu.VMEM(own.shape, jnp.float32),
        pltpu.VMEM((chunks, width, width), jnp.float32),
        pltpu.SemaphoreType.DMA((chunks,)),
        pltpu.SemaphoreType.DMA((chunks,)),
    ]
    proj = jax.ShapeDtypeStruct((2, wide, width), jnp.float32)
    limit = pltpu.CompilerParams(vmem_limit_bytes=16 * 1024 * 1024)
    half = pl.pallas_call(
        own_kernel,
        out_shape=proj,
        in_specs=[smem, anywhere],
        out_specs=anywhere,
        scratch_shapes=scratch,
        compiler_params=limit,
        name="scale_own",
    )(core[None], own)
    return pl.pallas_call(
        other_kernel,
        out_shape=(
            proj,
            jax.ShapeDtypeStruct((2, wide), jnp.float32),
            jax.ShapeDtypeStruct((1, 128), jnp.float32),
        ),
        in_specs=[smem, anywhere, vmem, anywhere],
        out_specs=(anywhere, vmem, vmem),
        scratch_shapes=scratch,
        input_output_aliases={1: 0},
        compiler_params=limit,
        name="scale_other",
    )(core[None], half, own[:, edge:, :], other)


def shards(
    slot_ids,
    labels,
    cache_rows,
    cache_accum,
    table_rows,
    table_accum,
    miss_dest,
    evict_slot,
    evict_dest,
    proj_u,
    proj_v,
    cross_bias,
    head,
):
    owners = 32
    per = 8
    width = cache_rows.shape[1]
    cells = cache_rows.shape[0]
    spots = owners * per
    core = lax.axis_index("table") % 2

    me = lax.axis_index("table")
    sent = payload(
        evict_slot, evict_dest, miss_dest, cache_accum, cache_rows, owners, per
    ).reshape(owners, per, width)
    sent, slots_late = lax.optimization_barrier((sent, slot_ids))
    got = lax.all_to_all(sent, "table", split_axis=0, concat_axis=0, tiled=True)

    count = slot_ids.shape[0]
    feats = proj_u.shape[0] // width
    send, left, latent, dlatent, dlogit, extra = dense(
        core, slots_late, labels, cache_rows, proj_u, proj_v, cross_bias, head
    )

    send, got = lax.optimization_barrier((send, got))
    held = kept(core, left, latent, dlatent, extra) + swap_cores(send)
    held, got = lax.optimization_barrier((held, got))

    reply, table_new, accum_table = replied(me, got, table_rows, table_accum)
    back = reply.reshape(owners, per, width)

    held = exchange(held, plane_groups())
    back = cross(cross(back, 1), 8)
    rows_new, accum_new = updated(
        slot_ids,
        cache_rows,
        cache_accum,
        (latent, dlatent, dlogit),
        (proj_u, proj_v, cross_bias[None, :], head[None, :]),
    )
    held, back, rows_new, accum_new = lax.optimization_barrier(
        (held, back, rows_new, accum_new)
    )
    held = jnp.sum(held, axis=0)
    held = (held + shift_z(held, 4)) + (shift_z(held, 2) + shift_z(held, -2))
    back = cross(cross(back, 16), 2)
    held, back = lax.optimization_barrier((held, back))
    whole = jnp.broadcast_to(held[None], (4 * feats, *held.shape))
    whole = exchange(whole, plane_groups())
    back = cross(back, 4)
    in_place = (miss_dest[:, 0] ^ me) * per + ranks(miss_dest[:, 0])
    rows_new = refilled(evict_slot, in_place, back.reshape(spots, width), rows_new)
    fetched_accum = picked(back[:, per - 1, :per].reshape(-1), in_place)
    filled = evict_slot[:, None] == jnp.arange(cells, dtype=jnp.int32)[None, :]
    filled_sum = jnp.sum(jnp.where(filled, fetched_accum[:, None], 0.0), axis=0)
    accum_new = jnp.where(jnp.any(filled, axis=0), filled_sum, accum_new.reshape(cells))
    whole, rows_new, accum_new = lax.optimization_barrier((whole, rows_new, accum_new))
    clipped_proj, clipped_vecs, loss_row = normalized(core, whole, swap_cores(whole))
    loss = loss_row[0, 0] / (count * 256)
    return (rows_new, accum_new, table_new, accum_table, clipped_proj, clipped_vecs, loss)


def solution(mesh):
    split = P(AXES)
    rows = P(AXES, None)
    return jax.shard_map(
        shards,
        mesh=mesh,
        in_specs=(
            rows,
            split,
            rows,
            split,
            rows,
            split,
            rows,
            split,
            rows,
            P(),
            P(),
            P(),
            P(),
        ),
        out_specs=(rows, split, rows, split, P(), P(), P()),
        check_vma=False,
    )
```

```python
import jax
import jax.numpy as jnp
from jax import lax
from jax.experimental import pallas as pl
from jax.experimental.pallas import tpu as pltpu
from jax.sharding import PartitionSpec as P

EPS = 1e-06
ETA = 0.05
AXES = ("trainer", "table")


def device_at(y, x, z, core):
    return (((y // 2 * 4 + x) * 2 + y % 2) * 8 + z % 8) * 2 + core


def plane_groups():
    return [
        [device_at(y, x, 2 * pair + core + b, core) for y in range(4) for x in range(4) for b in (0, 1)]
        for core in range(2)
        for pair in range(4)
    ]


def shift_z(value, step):
    there = [
        (device_at(y, x, z, core), device_at(y, x, z + step, core))
        for y in range(4)
        for x in range(4)
        for z in range(8)
        for core in range(2)
    ]
    return lax.ppermute(value, AXES, there)


def swap_cores(value):
    return lax.ppermute(value, AXES, [(i, i ^ 1) for i in range(256)])


def exchange(value, groups):
    return lax.all_to_all(
        value, AXES, split_axis=0, concat_axis=0, tiled=True, axis_index_groups=groups
    )


def ranks(owner):
    listed = owner.shape[0]
    order = jnp.arange(listed, dtype=jnp.int32)
    earlier = (owner[:, None] == owner[None, :]) & (order[None, :] < order[:, None])
    return jnp.sum(earlier.astype(jnp.int32), axis=1)


def picked(values, index):
    hit = index[:, None] == jnp.arange(values.shape[0], dtype=jnp.int32)[None, :]
    return jnp.sum(jnp.where(hit, values[None, :], 0.0), axis=1)


def cross_two(value, high, low):
    split = value.reshape(value.shape[0] // (2 * high), 2, high // (2 * low), 2, low, *value.shape[1:])
    rows = []
    for first in (0, 1):
        row = []
        for second in (0, 1):
            bits = first * high + second * low
            part = split[:, first, :, second]
            if bits:
                part = lax.ppermute(part, AXES, [(i, i ^ bits) for i in range(256)])
            row.append(part)
        rows.append(jnp.stack(row, axis=2))
    return jnp.stack(rows, axis=1).reshape(value.shape)


def cross(value, bit):
    split = value.reshape(value.shape[0] // (2 * bit), 2, bit, *value.shape[1:])
    there = [(i, i ^ bit) for i in range(256)]
    came = lax.ppermute(split[:, 1], AXES, there)
    return jnp.stack([split[:, 0], came], axis=1).reshape(value.shape)


def put_blocks(ref, c, grad):
    half = grad.shape[1] // 2
    rows = grad.shape[0] // 4
    for q in range(4):
        part = grad[q * rows : (q + 1) * rows, :]
        ref[4 * c + q, :rows, :] = part[:, :half]
        ref[4 * c + q, rows : 2 * rows, :] = part[:, half:]


def dense_kernel(
    core_ref,
    slots_ref,
    labels_ref,
    cache_any,
    u_any,
    v_any,
    bias_ref,
    head_ref,
    send_out,
    left_out,
    latent_ref,
    dlatent_ref,
    dlogit_ref,
    extra_ref,
    cache,
    u_ref,
    v_ref,
    send_ref,
    left,
    high,
    mid,
    low,
    pooled,
    shifted,
    dlift,
    in_sems,
    out_sems,
):
    f32, bf16 = jnp.float32, jnp.bfloat16
    count, (cells, width) = slots_ref.shape[1], cache.shape
    feats = u_ref.shape[0] // width
    looks = slots_ref.shape[0] // feats
    cuts = [slice(c * width, (c + 1) * width) for c in range(feats)]
    loads = []
    for source, target in ((cache_any, cache), (v_any, v_ref), (u_any, u_ref)):
        step = target.shape[0] // 4
        for part in range(4):
            rows = pl.ds(part * step, step)
            loads.append(
                pltpu.make_async_copy(source.at[rows], target.at[rows], in_sems.at[len(loads)])
            )
            loads[-1].start()
    slots = jnp.transpose(slots_ref[...])
    lanes = 128
    lane = lax.broadcasted_iota(jnp.int32, (count, lanes), 1)
    one = jnp.ones((count, lanes), bf16)

    def counted(f):
        keys = []
        for at in range(f * looks, (f + 1) * looks):
            slot = slots[:, at : at + 1]
            key = jnp.where(lane == slot % lanes, slot // lanes, -1)
            keys.append(key.astype(f32).astype(bf16))
        tiles = []
        for tile in range(cells // lanes):
            this = jnp.full((count, lanes), tile, bf16)
            tiles.append(sum(jnp.where(key == this, one, 0 * one) for key in keys))
        return jnp.concatenate(tiles, axis=1)

    counts = counted(0)
    step = cells // 4
    for part in range(4):
        loads[part].wait()
        rows = cache[part * step : (part + 1) * step, :]
        first = rows.astype(bf16)
        rest = rows - first.astype(f32)
        second = rest.astype(bf16)
        high[part * step : (part + 1) * step, :] = first
        mid[part * step : (part + 1) * step, :] = second
        low[part * step : (part + 1) * step, :] = (rest - second.astype(f32)).astype(bf16)
    for f in range(feats):
        if f > 0:
            counts = counted(f)
        total = jnp.dot(counts, low[...], preferred_element_type=f32)
        total = total + jnp.dot(counts, mid[...], preferred_element_type=f32)
        total = total + jnp.dot(counts, high[...], preferred_element_type=f32)
        pooled[:, cuts[f]] = total.astype(bf16)

    for load in loads[4:]:
        load.wait()
    latent = jnp.dot(pooled[...], v_ref[...], preferred_element_type=f32).astype(bf16)
    latent_ref[...] = latent
    across = (((1,), (1,)), ((), ()))
    logit_wide = jnp.zeros((count, width), f32)
    for cut in cuts:
        moved = lax.dot_general(latent, u_ref[cut, :], across, preferred_element_type=f32)
        moved = moved + bias_ref[:, cut]
        shifted[:, cut] = moved
        part = pooled[:, cut].astype(f32)
        logit_wide = logit_wide + (part * moved + part) * head_ref[:, cut]
    logit = jnp.sum(logit_wide, axis=1, keepdims=True)
    target = jnp.transpose(labels_ref[...]).astype(f32)
    small = jnp.exp(-jnp.abs(logit))
    losses = jnp.maximum(logit, 0.0) + jnp.log1p(small) - target * logit
    loss = jnp.sum(losses, axis=0, keepdims=True)
    dlogit = jnp.where(logit >= 0, 1.0, small) / (1.0 + small) - target
    dlogit_ref[...] = jnp.transpose(dlogit)

    mine = core_ref[0] == 0
    half = width // 2
    lane1 = lax.broadcasted_iota(jnp.int32, (1, half), 1)
    loss_row = jnp.where(lane1 == 0, loss, 0.0)
    back = jnp.zeros((count, width), f32)
    for c, cut in enumerate(cuts):
        part = pooled[:, cut].astype(f32)
        lift = dlogit * head_ref[:, cut] * part
        crossed = part * shifted[:, cut] + part
        dbias = jnp.sum(lift, axis=0, keepdims=True)
        dhead = jnp.sum(dlogit * crossed, axis=0, keepdims=True)
        lift = lift.astype(bf16)
        dlift[:, cut] = lift
        back = back + jnp.dot(lift, u_ref[cut, :], preferred_element_type=f32)
        for ref, row in (
            (extra_ref, jnp.where(mine, dbias, dhead)),
            (send_ref, jnp.where(mine, dhead, dbias)),
        ):
            top = ref.shape[1] - 8
            for q in range(4):
                at = 4 * c + q
                ref[at, top : top + 8, :] = jnp.zeros((8, half), f32)
                ref[at, top + 1 : top + 2, :] = loss_row
                if q % 2 == 0:
                    ref[at, top : top + 1, :] = row[:, q // 2 * half : (q // 2 + 1) * half]
        left[:, cut] = jnp.where(mine, lift, pooled[:, cut])
    dlatent = back.astype(bf16)
    dlatent_ref[...] = dlatent
    copies = [pltpu.make_async_copy(left, left_out, out_sems.at[feats])]
    copies[0].start()
    right = jnp.where(mine, dlatent, latent)
    for c, cut in enumerate(cuts):
        grad = lax.dot_general(
            jnp.where(mine, pooled[:, cut], dlift[:, cut]),
            right,
            (((0,), (0,)), ((), ())),
            preferred_element_type=f32,
        )
        put_blocks(send_ref, c, grad)
        four = pl.ds(4 * c, 4)
        copies.append(
            pltpu.make_async_copy(send_ref.at[four], send_out.at[four], out_sems.at[c])
        )
        copies[-1].start()
    for copy in copies:
        copy.wait()


def dense(core, slot_ids, labels, cache_rows, proj_u, proj_v, cross_bias, head):
    count, (cells, width) = slot_ids.shape[0], cache_rows.shape
    wide = proj_u.shape[0]
    blocks = wide // width
    f32, bf16 = jnp.float32, jnp.bfloat16
    vmem = pl.BlockSpec(memory_space=pltpu.VMEM)
    anywhere = pl.BlockSpec(memory_space=pl.ANY)
    bundle = (4 * blocks, width // 2 + 8, width // 2)
    return pl.pallas_call(
        dense_kernel,
        out_shape=(
            jax.ShapeDtypeStruct(bundle, f32),
            jax.ShapeDtypeStruct((count, wide), bf16),
            jax.ShapeDtypeStruct((count, width), bf16),
            jax.ShapeDtypeStruct((count, width), bf16),
            jax.ShapeDtypeStruct((1, count), f32),
            jax.ShapeDtypeStruct((4 * blocks, 8, width // 2), f32),
        ),
        in_specs=[pl.BlockSpec(memory_space=pltpu.SMEM)]
        + [vmem] * 2
        + [anywhere] * 3
        + [vmem] * 2,
        out_specs=[anywhere] * 2 + [vmem] * 4,
        scratch_shapes=[
            pltpu.VMEM((cells, width), f32),
            pltpu.VMEM((wide, width), bf16),
            pltpu.VMEM((wide, width), bf16),
            pltpu.VMEM(bundle, f32),
            pltpu.VMEM((count, wide), bf16),
        ]
        + [pltpu.VMEM((cells, width), bf16)] * 3
        + [
            pltpu.VMEM((count, wide), bf16),
            pltpu.VMEM((count, wide), f32),
            pltpu.VMEM((count, wide), bf16),
            pltpu.SemaphoreType.DMA((12,)),
            pltpu.SemaphoreType.DMA((blocks + 1,)),
        ],
        compiler_params=pltpu.CompilerParams(vmem_limit_bytes=60 * 1024 * 1024),
        cost_estimate=pl.CostEstimate(
            flops=5_000_000_000, bytes_accessed=9_000_000, transcendentals=1000
        ),
        name="dense",
    )(
        core[None],
        slot_ids.T,
        labels[None, :],
        cache_rows,
        proj_u,
        proj_v,
        cross_bias[None, :],
        head[None, :],
    )


def keep_kernel(core_ref, left_ref, latent_ref, dlatent_ref, extra_ref, keep_ref):
    width = latent_ref.shape[1]
    right = jnp.where(core_ref[0] == 0, latent_ref[...], dlatent_ref[...])
    for c in range(keep_ref.shape[0] // 4):
        grad = lax.dot_general(
            left_ref[:, c * width : (c + 1) * width],
            right,
            (((0,), (0,)), ((), ())),
            preferred_element_type=jnp.float32,
        )
        put_blocks(keep_ref, c, grad)
    keep_ref[:, width // 2 :, :] = extra_ref[...]


def kept(core, left, latent, dlatent, extra):
    blocks, _, half = extra.shape
    vmem = pl.BlockSpec(memory_space=pltpu.VMEM)
    return pl.pallas_call(
        keep_kernel,
        out_shape=jax.ShapeDtypeStruct((blocks, half + 8, half), jnp.float32),
        in_specs=[pl.BlockSpec(memory_space=pltpu.SMEM)] + [vmem] * 4,
        out_specs=vmem,
        compiler_params=pltpu.CompilerParams(vmem_limit_bytes=16 * 1024 * 1024),
        cost_estimate=pl.CostEstimate(
            flops=300_000_000, bytes_accessed=4_000_000, transcendentals=0
        ),
        name="kept",
    )(core[None], left, latent, dlatent, extra)


def payload_kernel(
    slot_ref, evict_ref, miss_ref, accum_ref, cache_any, out_ref, taken, place, cache, sems
):
    owners, per = taken.shape[0], out_ref.shape[0] // taken.shape[0]
    width = out_ref.shape[1]
    listed = slot_ref.shape[0]
    step = cache.shape[0] // 4
    loads = []
    for part in range(4):
        rows = pl.ds(part * step, step)
        loads.append(pltpu.make_async_copy(cache_any.at[rows], cache.at[rows], sems.at[part]))
        loads[-1].start()
    lane = lax.broadcasted_iota(jnp.int32, (1, width), 1)
    base = jnp.where((lane >= per) & (lane < 2 * per), -1.0, 0.0)
    for o in range(owners):
        taken[o] = 0
        out_ref[o * per : o * per + per - 1, :] = jnp.zeros((per - 1, width), jnp.float32)
        out_ref[o * per + per - 1 : (o + 1) * per, :] = base

    def leave(i, _):
        owner = evict_ref[0, i]
        rank = taken[owner]
        taken[owner] = rank + 1
        place[i] = owner * per + rank
        spot = pl.ds(owner * per + per - 1, 1)
        meta = jnp.where(lane == rank, accum_ref[slot_ref[i]], out_ref[spot, :])
        row = evict_ref[1, i].astype(jnp.float32)
        out_ref[spot, :] = jnp.where(lane == per + rank, row, meta)
        return 0

    lax.fori_loop(0, listed, leave, 0, unroll=8)
    for o in range(owners):
        taken[o] = 0

    def ask(i, _):
        owner = miss_ref[0, i]
        rank = taken[owner]
        taken[owner] = rank + 1
        spot = pl.ds(owner * per + per - 1, 1)
        row = miss_ref[1, i].astype(jnp.float32)
        out_ref[spot, :] = jnp.where(lane == 2 * per + rank, row, out_ref[spot, :])
        return 0

    lax.fori_loop(0, listed, ask, 0, unroll=8)
    for load in loads:
        load.wait()

    def move(i, _):
        out_ref[pl.ds(place[i], 1), :] = cache[pl.ds(slot_ref[i], 1), :]
        return 0

    lax.fori_loop(0, listed, move, 0, unroll=8)


def payload(evict_slot, evict_dest, miss_dest, cache_accum, cache_rows, owners, per):
    smem = pl.BlockSpec(memory_space=pltpu.SMEM)
    return pl.pallas_call(
        payload_kernel,
        out_shape=jax.ShapeDtypeStruct((owners * per, cache_rows.shape[1]), jnp.float32),
        in_specs=[smem] * 4 + [pl.BlockSpec(memory_space=pl.ANY)],
        out_specs=pl.BlockSpec(memory_space=pltpu.VMEM),
        scratch_shapes=[
            pltpu.SMEM((owners,), jnp.int32),
            pltpu.SMEM(evict_slot.shape, jnp.int32),
            pltpu.VMEM(cache_rows.shape, jnp.float32),
            pltpu.SemaphoreType.DMA((4,)),
        ],
        compiler_params=pltpu.CompilerParams(vmem_limit_bytes=60 * 1024 * 1024),
        cost_estimate=pl.CostEstimate(flops=100_000, bytes_accessed=1_500_000, transcendentals=0),
        name="payload",
    )(evict_slot, evict_dest.T, miss_dest.T, cache_accum, cache_rows)


def update_kernel(
    slots_ref,
    cache_ref,
    accum_ref,
    latent_ref,
    dlatent_ref,
    dlogit_ref,
    u_ref,
    v_ref,
    bias_ref,
    head_ref,
    rows_ref,
    accum_out,
):
    f32, bf16 = jnp.float32, jnp.bfloat16
    (cells, width), count = cache_ref.shape, latent_ref.shape[0]
    feats = u_ref.shape[0] // width
    looks = slots_ref.shape[0] // feats
    across = (((1,), (1,)), ((), ()))
    latent, dlatent = latent_ref[...], dlatent_ref[...]
    dlogit = jnp.transpose(dlogit_ref[...])
    cell = lax.broadcasted_iota(jnp.int32, (cells, count), 0)
    grad = jnp.zeros((cells, width), f32)
    for f in range(feats):
        counts = jnp.zeros((cells, count), f32)
        for look in range(looks):
            at = f * looks + look
            counts = counts + jnp.where(cell == slots_ref[at : at + 1, :], 1.0, 0.0)
        cut = slice(f * width, (f + 1) * width)
        moved = lax.dot_general(latent, u_ref[cut, :], across, preferred_element_type=f32)
        moved = moved + bias_ref[:, cut]
        through = lax.dot_general(dlatent, v_ref[cut, :], across, preferred_element_type=f32)
        dpooled = (dlogit * head_ref[:, cut] * (moved + 1.0) + through).astype(bf16)
        grad = grad + jnp.dot(counts.astype(bf16), dpooled, preferred_element_type=f32)
    mean = jnp.sum(grad * grad, axis=1, keepdims=True) / width
    accum = jnp.transpose(accum_ref[...]) + mean
    rows_ref[...] = cache_ref[...] - ETA * grad * lax.rsqrt(accum)
    accum_out[...] = jnp.transpose(accum)


def refill_kernel(evict_ref, place_ref, back_ref, old_ref, rows_ref):
    rows_ref[...] = old_ref[...]

    def refill(i, _):
        rows_ref[pl.ds(evict_ref[i], 1), :] = back_ref[pl.ds(place_ref[i], 1), :]
        return 0

    lax.fori_loop(0, evict_ref.shape[0], refill, 0, unroll=8)


def updated(slot_ids, cache_rows, cache_accum, saved, params):
    cells = cache_rows.shape[0]
    vmem = pl.BlockSpec(memory_space=pltpu.VMEM)
    return pl.pallas_call(
        update_kernel,
        out_shape=(
            jax.ShapeDtypeStruct(cache_rows.shape, jnp.float32),
            jax.ShapeDtypeStruct((1, cells), jnp.float32),
        ),
        in_specs=[vmem] * 10,
        out_specs=(vmem, vmem),
        compiler_params=pltpu.CompilerParams(vmem_limit_bytes=60 * 1024 * 1024),
        cost_estimate=pl.CostEstimate(
            flops=1_100_000_000, bytes_accessed=4_000_000, transcendentals=1000
        ),
        name="update",
    )(slot_ids.T, cache_rows, cache_accum[None, :], *saved, *params)


def refilled(evict_slot, place, back, rows):
    smem = pl.BlockSpec(memory_space=pltpu.SMEM)
    vmem = pl.BlockSpec(memory_space=pltpu.VMEM)
    return pl.pallas_call(
        refill_kernel,
        out_shape=jax.ShapeDtypeStruct(rows.shape, jnp.float32),
        in_specs=[smem, smem, vmem, vmem],
        out_specs=vmem,
        compiler_params=pltpu.CompilerParams(vmem_limit_bytes=60 * 1024 * 1024),
        cost_estimate=pl.CostEstimate(flops=100_000, bytes_accessed=2_000_000, transcendentals=0),
        name="refill",
    )(evict_slot, place, back, rows)


def reply_kernel(
    me_ref,
    ids_ref,
    sums_ref,
    got_ref,
    table_any,
    accum_any,
    reply_ref,
    table_out,
    accum_out,
    table,
    accum,
    sems,
):
    owners, per = sums_ref.shape
    cap = per - 2
    width = got_ref.shape[1]
    step = table.shape[0] // 4
    loads = [pltpu.make_async_copy(accum_any, accum, sems.at[4])]
    stores = [pltpu.make_async_copy(accum, accum_out, sems.at[4])]
    for part in range(4):
        rows = pl.ds(part * step, step)
        loads.append(pltpu.make_async_copy(table_any.at[rows], table.at[rows], sems.at[part]))
        stores.append(pltpu.make_async_copy(table.at[rows], table_out.at[rows], sems.at[part]))
    for load in loads:
        load.start()
    for load in loads:
        load.wait()

    def store(s, _):
        for r in range(cap):
            row = ids_ref[s, per + r]

            @pl.when(row >= 0)
            def _():
                table[pl.ds(row, 1), :] = got_ref[pl.ds(s * per + r, 1), :]
                accum[row] = sums_ref[s, r]

        return 0

    lax.fori_loop(0, owners, store, 0, unroll=2)
    for copy in stores:
        copy.start()
    lane = lax.broadcasted_iota(jnp.int32, (1, width), 1)

    def answer(s, _):
        block = (s ^ me_ref[0]) * per
        meta = jnp.zeros((1, width), jnp.float32)
        for r in range(cap):
            row = ids_ref[s, 2 * per + r]
            reply_ref[pl.ds(block + r, 1), :] = table[pl.ds(row, 1), :]
            meta = jnp.where(lane == r, accum[row], meta)
        reply_ref[pl.ds(block + cap, 1), :] = jnp.zeros((1, width), jnp.float32)
        reply_ref[pl.ds(block + per - 1, 1), :] = meta
        return 0

    lax.fori_loop(0, owners, answer, 0, unroll=4)
    for copy in stores:
        copy.wait()


def replied(me, got, table_rows, table_accum):
    owners, per, width = got.shape
    smem = pl.BlockSpec(memory_space=pltpu.SMEM)
    vmem = pl.BlockSpec(memory_space=pltpu.VMEM)
    anywhere = pl.BlockSpec(memory_space=pl.ANY)
    meta = got[:, per - 1, : 3 * per]
    return pl.pallas_call(
        reply_kernel,
        out_shape=(
            jax.ShapeDtypeStruct((owners * per, width), jnp.float32),
            jax.ShapeDtypeStruct(table_rows.shape, jnp.float32),
            jax.ShapeDtypeStruct(table_accum.shape, jnp.float32),
        ),
        in_specs=[smem, smem, smem, vmem, anywhere, anywhere],
        out_specs=(vmem, anywhere, anywhere),
        scratch_shapes=[
            pltpu.VMEM(table_rows.shape, jnp.float32),
            pltpu.SMEM(table_accum.shape, jnp.float32),
            pltpu.SemaphoreType.DMA((5,)),
        ],
        compiler_params=pltpu.CompilerParams(vmem_limit_bytes=60 * 1024 * 1024),
        cost_estimate=pl.CostEstimate(flops=100_000, bytes_accessed=3_000_000, transcendentals=0),
        name="reply",
    )(
        me[None],
        meta.astype(jnp.int32),
        meta[:, :per],
        got.reshape(owners * per, width),
        table_rows,
        table_accum,
    )


def scaled(index, half, proj_ref, stage, out_sems):
    chunks, width = stage.shape[0], stage.shape[2]
    edge, rows = width // 2, width // 4
    squares = jnp.zeros((edge, edge), jnp.float32)
    for c in range(chunks):
        for q in range(4):
            block = half[4 * c + q, :edge, :]
            squares = squares + block * block
    total = jnp.sum(jnp.sum(squares, axis=0, keepdims=True), axis=1, keepdims=True)
    scale = lax.rsqrt(total / (chunks * width * width) + EPS)
    copies = []
    for c in range(chunks):
        for q in range(4):
            at = slice(q * rows, (q + 1) * rows)
            stage[c, at, :edge] = half[4 * c + q, :rows, :] * scale
            stage[c, at, edge:] = half[4 * c + q, rows:edge, :] * scale
        copies.append(
            pltpu.make_async_copy(
                stage.at[c], proj_ref.at[index, pl.ds(c * width, width), :], out_sems.at[c]
            )
        )
        copies[-1].start()
    return copies


def own_kernel(core_ref, half, proj_ref, stage, out_sems):
    for copy in scaled(core_ref[0], half, proj_ref, stage, out_sems):
        copy.wait()


def other_kernel(
    core_ref,
    proj_in,
    own_ref,
    half,
    proj_ref,
    vec_ref,
    loss_ref,
    stage,
    out_sems,
):
    core = core_ref[0]
    copies = scaled(1 - core, half, proj_ref, stage, out_sems)
    edge = half.shape[2]
    tiles = vec_ref.shape[1] // edge
    mine = core == 0
    own = [own_ref[2 * t, 0:1, :] for t in range(tiles)]
    far = [half[2 * t, edge : edge + 1, :] for t in range(tiles)]
    for index in (0, 1):
        rows = [jnp.where(mine, *((a, b) if index == 0 else (b, a))) for a, b in zip(own, far)]
        squares = sum(row * row for row in rows)
        total = jnp.sum(squares, axis=1, keepdims=True)
        scale = lax.rsqrt(total / (tiles * edge) + EPS)
        for t in range(tiles):
            vec_ref[index : index + 1, t * edge : (t + 1) * edge] = rows[t] * scale
    loss_ref[...] = jnp.where(mine, half[0, edge + 1 : edge + 2, :], own_ref[0, 1:2, :])
    for copy in copies:
        copy.wait()


def normalized(core, own, other):
    blocks, depth, edge = own.shape
    chunks, width = blocks // 4, 2 * edge
    wide = chunks * width
    smem = pl.BlockSpec(memory_space=pltpu.SMEM)
    vmem = pl.BlockSpec(memory_space=pltpu.VMEM)
    anywhere = pl.BlockSpec(memory_space=pl.ANY)
    scratch = [
        pltpu.VMEM((chunks, width, width), jnp.float32),
        pltpu.SemaphoreType.DMA((chunks,)),
    ]
    proj = jax.ShapeDtypeStruct((2, wide, width), jnp.float32)
    limit = pltpu.CompilerParams(vmem_limit_bytes=16 * 1024 * 1024)
    half = pl.pallas_call(
        own_kernel,
        out_shape=proj,
        in_specs=[smem, vmem],
        out_specs=anywhere,
        scratch_shapes=scratch,
        compiler_params=limit,
        name="scale_own",
    )(core[None], own)
    return pl.pallas_call(
        other_kernel,
        out_shape=(
            proj,
            jax.ShapeDtypeStruct((2, wide), jnp.float32),
            jax.ShapeDtypeStruct((1, 128), jnp.float32),
        ),
        in_specs=[smem, anywhere, vmem, vmem],
        out_specs=(anywhere, vmem, vmem),
        scratch_shapes=scratch,
        input_output_aliases={1: 0},
        compiler_params=limit,
        name="scale_other",
    )(core[None], half, own[:, edge:, :], other)


def shards(
    slot_ids,
    labels,
    cache_rows,
    cache_accum,
    table_rows,
    table_accum,
    miss_dest,
    evict_slot,
    evict_dest,
    proj_u,
    proj_v,
    cross_bias,
    head,
):
    owners = 32
    per = 8
    width = cache_rows.shape[1]
    cells = cache_rows.shape[0]
    spots = owners * per
    core = lax.axis_index("table") % 2

    me = lax.axis_index("table")
    sent = payload(
        evict_slot, evict_dest, miss_dest, cache_accum, cache_rows, owners, per
    ).reshape(owners, per, width)
    sent, slots_late = lax.optimization_barrier((sent, slot_ids))
    got = lax.all_to_all(sent, "table", split_axis=0, concat_axis=0, tiled=True)

    count = slot_ids.shape[0]
    feats = proj_u.shape[0] // width
    send, left, latent, dlatent, dlogit, extra = dense(
        core, slots_late, labels, cache_rows, proj_u, proj_v, cross_bias, head
    )

    send, got = lax.optimization_barrier((send, got))
    held = kept(core, left, latent, dlatent, extra) + swap_cores(send)
    held, got = lax.optimization_barrier((held, got))

    reply, table_new, accum_table = replied(me, got, table_rows, table_accum)
    back = reply.reshape(owners, per, width)

    held = exchange(held, plane_groups())
    back = cross_two(cross(back, 1), 16, 8)
    rows_new, accum_new = updated(
        slot_ids,
        cache_rows,
        cache_accum,
        (latent, dlatent, dlogit),
        (proj_u, proj_v, cross_bias[None, :], head[None, :]),
    )
    held, back, rows_new, accum_new = lax.optimization_barrier(
        (held, back, rows_new, accum_new)
    )
    held = jnp.sum(held, axis=0)
    held = (held + shift_z(held, 4)) + (shift_z(held, 2) + shift_z(held, -2))
    back = cross(cross(back, 2), 4)
    held, back = lax.optimization_barrier((held, back))
    whole = jnp.broadcast_to(held[None], (4 * feats, *held.shape))
    whole = exchange(whole, plane_groups())
    in_place = (miss_dest[:, 0] ^ me) * per + ranks(miss_dest[:, 0])
    rows_new = refilled(evict_slot, in_place, back.reshape(spots, width), rows_new)
    fetched_accum = picked(back[:, per - 1, :per].reshape(-1), in_place)
    filled = evict_slot[:, None] == jnp.arange(cells, dtype=jnp.int32)[None, :]
    filled_sum = jnp.sum(jnp.where(filled, fetched_accum[:, None], 0.0), axis=0)
    accum_new = jnp.where(jnp.any(filled, axis=0), filled_sum, accum_new.reshape(cells))
    whole, rows_new, accum_new = lax.optimization_barrier((whole, rows_new, accum_new))
    clipped_proj, clipped_vecs, loss_row = normalized(core, whole, swap_cores(whole))
    loss = loss_row[0, 0] / (count * 256)
    return (rows_new, accum_new, table_new, accum_table, clipped_proj, clipped_vecs, loss)


def solution(mesh):
    split = P(AXES)
    rows = P(AXES, None)
    return jax.shard_map(
        shards,
        mesh=mesh,
        in_specs=(
            rows,
            split,
            rows,
            split,
            rows,
            split,
            rows,
            split,
            rows,
            P(),
            P(),
            P(),
            P(),
        ),
        out_specs=(rows, split, rows, split, P(), P(), P()),
        check_vma=False,
    )
```

```python
import jax
import jax.numpy as jnp
from jax import lax
from jax.experimental import pallas as pl
from jax.experimental.pallas import tpu as pltpu
from jax.sharding import PartitionSpec as P

EPS = 1e-06
ETA = 0.05
AXES = ("trainer", "table")


def device_at(y, x, z, core):
    return (((y // 2 * 4 + x) * 2 + y % 2) * 8 + z % 8) * 2 + core


def plane_groups():
    return [
        [device_at(y, x, 2 * pair + core + b, core) for y in range(4) for x in range(4) for b in (0, 1)]
        for core in range(2)
        for pair in range(4)
    ]


def shift_z(value, step):
    there = [
        (device_at(y, x, z, core), device_at(y, x, z + step, core))
        for y in range(4)
        for x in range(4)
        for z in range(8)
        for core in range(2)
    ]
    return lax.ppermute(value, AXES, there)


def swap_cores(value):
    return lax.ppermute(value, AXES, [(i, i ^ 1) for i in range(256)])


def exchange(value, groups):
    return lax.all_to_all(
        value, AXES, split_axis=0, concat_axis=0, tiled=True, axis_index_groups=groups
    )


def ranks(owner):
    listed = owner.shape[0]
    order = jnp.arange(listed, dtype=jnp.int32)
    earlier = (owner[:, None] == owner[None, :]) & (order[None, :] < order[:, None])
    return jnp.sum(earlier.astype(jnp.int32), axis=1)


def picked(values, index):
    hit = index[:, None] == jnp.arange(values.shape[0], dtype=jnp.int32)[None, :]
    return jnp.sum(jnp.where(hit, values[None, :], 0.0), axis=1)


def cross(value, bit):
    split = value.reshape(value.shape[0] // (2 * bit), 2, bit, *value.shape[1:])
    there = [(i, i ^ bit) for i in range(256)]
    came = lax.ppermute(split[:, 1], AXES, there)
    return jnp.stack([split[:, 0], came], axis=1).reshape(value.shape)


def put_blocks(ref, c, grad):
    half = grad.shape[1] // 2
    rows = grad.shape[0] // 4
    for q in range(4):
        part = grad[q * rows : (q + 1) * rows, :]
        ref[4 * c + q, :rows, :] = part[:, :half]
        ref[4 * c + q, rows : 2 * rows, :] = part[:, half:]


def dense_kernel(
    core_ref,
    slots_ref,
    labels_ref,
    cache_any,
    u_any,
    v_any,
    bias_ref,
    head_ref,
    send_out,
    left_out,
    latent_ref,
    dlatent_ref,
    dlogit_ref,
    extra_ref,
    cache,
    u_ref,
    v_ref,
    send_ref,
    left,
    high,
    mid,
    low,
    pooled,
    shifted,
    dlift,
    in_sems,
    out_sems,
):
    f32, bf16 = jnp.float32, jnp.bfloat16
    count, (cells, width) = slots_ref.shape[1], cache.shape
    feats = u_ref.shape[0] // width
    looks = slots_ref.shape[0] // feats
    cuts = [slice(c * width, (c + 1) * width) for c in range(feats)]
    loads = []
    for source, target in ((cache_any, cache), (v_any, v_ref), (u_any, u_ref)):
        step = target.shape[0] // 4
        for part in range(4):
            rows = pl.ds(part * step, step)
            loads.append(
                pltpu.make_async_copy(source.at[rows], target.at[rows], in_sems.at[len(loads)])
            )
            loads[-1].start()
    slots = jnp.transpose(slots_ref[...])
    lanes = 128
    lane = lax.broadcasted_iota(jnp.int32, (count, lanes), 1)
    one = jnp.ones((count, lanes), bf16)

    def counted(f):
        keys = []
        for at in range(f * looks, (f + 1) * looks):
            slot = slots[:, at : at + 1]
            key = jnp.where(lane == slot % lanes, slot // lanes, -1)
            keys.append(key.astype(f32).astype(bf16))
        tiles = []
        for tile in range(cells // lanes):
            this = jnp.full((count, lanes), tile, bf16)
            tiles.append(sum(jnp.where(key == this, one, 0 * one) for key in keys))
        return jnp.concatenate(tiles, axis=1)

    counts = counted(0)
    step = cells // 4
    for part in range(4):
        loads[part].wait()
        rows = cache[part * step : (part + 1) * step, :]
        first = rows.astype(bf16)
        rest = rows - first.astype(f32)
        second = rest.astype(bf16)
        high[part * step : (part + 1) * step, :] = first
        mid[part * step : (part + 1) * step, :] = second
        low[part * step : (part + 1) * step, :] = (rest - second.astype(f32)).astype(bf16)
    for f in range(feats):
        if f > 0:
            counts = counted(f)
        total = jnp.dot(counts, low[...], preferred_element_type=f32)
        total = total + jnp.dot(counts, mid[...], preferred_element_type=f32)
        total = total + jnp.dot(counts, high[...], preferred_element_type=f32)
        pooled[:, cuts[f]] = total.astype(bf16)

    for load in loads[4:]:
        load.wait()
    latent = jnp.dot(pooled[...], v_ref[...], preferred_element_type=f32).astype(bf16)
    latent_ref[...] = latent
    across = (((1,), (1,)), ((), ()))
    logit_wide = jnp.zeros((count, width), f32)
    for cut in cuts:
        moved = lax.dot_general(latent, u_ref[cut, :], across, preferred_element_type=f32)
        moved = moved + bias_ref[:, cut]
        shifted[:, cut] = moved
        part = pooled[:, cut].astype(f32)
        logit_wide = logit_wide + (part * moved + part) * head_ref[:, cut]
    logit = jnp.sum(logit_wide, axis=1, keepdims=True)
    target = jnp.transpose(labels_ref[...]).astype(f32)
    small = jnp.exp(-jnp.abs(logit))
    losses = jnp.maximum(logit, 0.0) + jnp.log1p(small) - target * logit
    loss = jnp.sum(losses, axis=0, keepdims=True)
    dlogit = jnp.where(logit >= 0, 1.0, small) / (1.0 + small) - target
    dlogit_ref[...] = jnp.transpose(dlogit)

    mine = core_ref[0] == 0
    half = width // 2
    lane1 = lax.broadcasted_iota(jnp.int32, (1, half), 1)
    loss_row = jnp.where(lane1 == 0, loss, 0.0)
    back = jnp.zeros((count, width), f32)
    for c, cut in enumerate(cuts):
        part = pooled[:, cut].astype(f32)
        lift = dlogit * head_ref[:, cut] * part
        crossed = part * shifted[:, cut] + part
        dbias = jnp.sum(lift, axis=0, keepdims=True)
        dhead = jnp.sum(dlogit * crossed, axis=0, keepdims=True)
        lift = lift.astype(bf16)
        dlift[:, cut] = lift
        back = back + jnp.dot(lift, u_ref[cut, :], preferred_element_type=f32)
        for ref, row in (
            (extra_ref, jnp.where(mine, dbias, dhead)),
            (send_ref, jnp.where(mine, dhead, dbias)),
        ):
            top = ref.shape[1] - 8
            for q in range(4):
                at = 4 * c + q
                ref[at, top : top + 8, :] = jnp.zeros((8, half), f32)
                ref[at, top + 1 : top + 2, :] = loss_row
                if q % 2 == 0:
                    ref[at, top : top + 1, :] = row[:, q // 2 * half : (q // 2 + 1) * half]
        left[:, cut] = jnp.where(mine, lift, pooled[:, cut])
    dlatent = back.astype(bf16)
    dlatent_ref[...] = dlatent
    copies = [pltpu.make_async_copy(left, left_out, out_sems.at[feats])]
    copies[0].start()
    right = jnp.where(mine, dlatent, latent)
    for c, cut in enumerate(cuts):
        grad = lax.dot_general(
            jnp.where(mine, pooled[:, cut], dlift[:, cut]),
            right,
            (((0,), (0,)), ((), ())),
            preferred_element_type=f32,
        )
        put_blocks(send_ref, c, grad)
        four = pl.ds(4 * c, 4)
        copies.append(
            pltpu.make_async_copy(send_ref.at[four], send_out.at[four], out_sems.at[c])
        )
        copies[-1].start()
    for copy in copies:
        copy.wait()


def dense(core, slot_ids, labels, cache_rows, proj_u, proj_v, cross_bias, head):
    count, (cells, width) = slot_ids.shape[0], cache_rows.shape
    wide = proj_u.shape[0]
    blocks = wide // width
    f32, bf16 = jnp.float32, jnp.bfloat16
    vmem = pl.BlockSpec(memory_space=pltpu.VMEM)
    anywhere = pl.BlockSpec(memory_space=pl.ANY)
    bundle = (4 * blocks, width // 2 + 8, width // 2)
    return pl.pallas_call(
        dense_kernel,
        out_shape=(
            jax.ShapeDtypeStruct(bundle, f32),
            jax.ShapeDtypeStruct((count, wide), bf16),
            jax.ShapeDtypeStruct((count, width), bf16),
            jax.ShapeDtypeStruct((count, width), bf16),
            jax.ShapeDtypeStruct((1, count), f32),
            jax.ShapeDtypeStruct((4 * blocks, 8, width // 2), f32),
        ),
        in_specs=[pl.BlockSpec(memory_space=pltpu.SMEM)]
        + [vmem] * 2
        + [anywhere] * 3
        + [vmem] * 2,
        out_specs=[anywhere] * 2 + [vmem] * 4,
        scratch_shapes=[
            pltpu.VMEM((cells, width), f32),
            pltpu.VMEM((wide, width), bf16),
            pltpu.VMEM((wide, width), bf16),
            pltpu.VMEM(bundle, f32),
            pltpu.VMEM((count, wide), bf16),
        ]
        + [pltpu.VMEM((cells, width), bf16)] * 3
        + [
            pltpu.VMEM((count, wide), bf16),
            pltpu.VMEM((count, wide), f32),
            pltpu.VMEM((count, wide), bf16),
            pltpu.SemaphoreType.DMA((12,)),
            pltpu.SemaphoreType.DMA((blocks + 1,)),
        ],
        compiler_params=pltpu.CompilerParams(vmem_limit_bytes=60 * 1024 * 1024),
        cost_estimate=pl.CostEstimate(
            flops=5_000_000_000, bytes_accessed=9_000_000, transcendentals=1000
        ),
        name="dense",
    )(
        core[None],
        slot_ids.T,
        labels[None, :],
        cache_rows,
        proj_u,
        proj_v,
        cross_bias[None, :],
        head[None, :],
    )


def keep_kernel(core_ref, left_ref, latent_ref, dlatent_ref, extra_ref, keep_ref):
    width = latent_ref.shape[1]
    right = jnp.where(core_ref[0] == 0, latent_ref[...], dlatent_ref[...])
    for c in range(keep_ref.shape[0] // 4):
        grad = lax.dot_general(
            left_ref[:, c * width : (c + 1) * width],
            right,
            (((0,), (0,)), ((), ())),
            preferred_element_type=jnp.float32,
        )
        put_blocks(keep_ref, c, grad)
    keep_ref[:, width // 2 :, :] = extra_ref[...]


def kept(core, left, latent, dlatent, extra):
    blocks, _, half = extra.shape
    vmem = pl.BlockSpec(memory_space=pltpu.VMEM)
    return pl.pallas_call(
        keep_kernel,
        out_shape=jax.ShapeDtypeStruct((blocks, half + 8, half), jnp.float32),
        in_specs=[pl.BlockSpec(memory_space=pltpu.SMEM)] + [vmem] * 4,
        out_specs=vmem,
        compiler_params=pltpu.CompilerParams(vmem_limit_bytes=16 * 1024 * 1024),
        cost_estimate=pl.CostEstimate(
            flops=300_000_000, bytes_accessed=4_000_000, transcendentals=0
        ),
        name="kept",
    )(core[None], left, latent, dlatent, extra)


def payload_kernel(
    slot_ref, evict_ref, miss_ref, accum_ref, cache_any, out_ref, taken, place, cache, sems
):
    owners, per = taken.shape[0], out_ref.shape[0] // taken.shape[0]
    width = out_ref.shape[1]
    listed = slot_ref.shape[0]
    step = cache.shape[0] // 4
    loads = []
    for part in range(4):
        rows = pl.ds(part * step, step)
        loads.append(pltpu.make_async_copy(cache_any.at[rows], cache.at[rows], sems.at[part]))
        loads[-1].start()
    lane = lax.broadcasted_iota(jnp.int32, (1, width), 1)
    base = jnp.where((lane >= per) & (lane < 2 * per), -1.0, 0.0)
    for o in range(owners):
        taken[o] = 0
        out_ref[o * per : o * per + per - 1, :] = jnp.zeros((per - 1, width), jnp.float32)
        out_ref[o * per + per - 1 : (o + 1) * per, :] = base

    def leave(i, _):
        owner = evict_ref[0, i]
        rank = taken[owner]
        taken[owner] = rank + 1
        place[i] = owner * per + rank
        spot = pl.ds(owner * per + per - 1, 1)
        meta = jnp.where(lane == rank, accum_ref[slot_ref[i]], out_ref[spot, :])
        row = evict_ref[1, i].astype(jnp.float32)
        out_ref[spot, :] = jnp.where(lane == per + rank, row, meta)
        return 0

    lax.fori_loop(0, listed, leave, 0, unroll=8)
    for o in range(owners):
        taken[o] = 0

    def ask(i, _):
        owner = miss_ref[0, i]
        rank = taken[owner]
        taken[owner] = rank + 1
        spot = pl.ds(owner * per + per - 1, 1)
        row = miss_ref[1, i].astype(jnp.float32)
        out_ref[spot, :] = jnp.where(lane == 2 * per + rank, row, out_ref[spot, :])
        return 0

    lax.fori_loop(0, listed, ask, 0, unroll=8)
    for load in loads:
        load.wait()

    def move(i, _):
        out_ref[pl.ds(place[i], 1), :] = cache[pl.ds(slot_ref[i], 1), :]
        return 0

    lax.fori_loop(0, listed, move, 0, unroll=8)


def payload(evict_slot, evict_dest, miss_dest, cache_accum, cache_rows, owners, per):
    smem = pl.BlockSpec(memory_space=pltpu.SMEM)
    return pl.pallas_call(
        payload_kernel,
        out_shape=jax.ShapeDtypeStruct((owners * per, cache_rows.shape[1]), jnp.float32),
        in_specs=[smem] * 4 + [pl.BlockSpec(memory_space=pl.ANY)],
        out_specs=pl.BlockSpec(memory_space=pltpu.VMEM),
        scratch_shapes=[
            pltpu.SMEM((owners,), jnp.int32),
            pltpu.SMEM(evict_slot.shape, jnp.int32),
            pltpu.VMEM(cache_rows.shape, jnp.float32),
            pltpu.SemaphoreType.DMA((4,)),
        ],
        compiler_params=pltpu.CompilerParams(vmem_limit_bytes=60 * 1024 * 1024),
        cost_estimate=pl.CostEstimate(flops=100_000, bytes_accessed=1_500_000, transcendentals=0),
        name="payload",
    )(evict_slot, evict_dest.T, miss_dest.T, cache_accum, cache_rows)


def update_kernel(
    slots_ref,
    cache_ref,
    accum_ref,
    latent_ref,
    dlatent_ref,
    dlogit_ref,
    u_ref,
    v_ref,
    bias_ref,
    head_ref,
    rows_ref,
    accum_out,
):
    f32, bf16 = jnp.float32, jnp.bfloat16
    (cells, width), count = cache_ref.shape, latent_ref.shape[0]
    feats = u_ref.shape[0] // width
    looks = slots_ref.shape[0] // feats
    across = (((1,), (1,)), ((), ()))
    latent, dlatent = latent_ref[...], dlatent_ref[...]
    dlogit = jnp.transpose(dlogit_ref[...])
    cell = lax.broadcasted_iota(jnp.int32, (cells, count), 0)
    grad = jnp.zeros((cells, width), f32)
    for f in range(feats):
        counts = jnp.zeros((cells, count), f32)
        for look in range(looks):
            at = f * looks + look
            counts = counts + jnp.where(cell == slots_ref[at : at + 1, :], 1.0, 0.0)
        cut = slice(f * width, (f + 1) * width)
        moved = lax.dot_general(latent, u_ref[cut, :], across, preferred_element_type=f32)
        moved = moved + bias_ref[:, cut]
        through = lax.dot_general(dlatent, v_ref[cut, :], across, preferred_element_type=f32)
        dpooled = (dlogit * head_ref[:, cut] * (moved + 1.0) + through).astype(bf16)
        grad = grad + jnp.dot(counts.astype(bf16), dpooled, preferred_element_type=f32)
    mean = jnp.sum(grad * grad, axis=1, keepdims=True) / width
    accum = jnp.transpose(accum_ref[...]) + mean
    rows_ref[...] = cache_ref[...] - ETA * grad * lax.rsqrt(accum)
    accum_out[...] = jnp.transpose(accum)


def refill_kernel(evict_ref, place_ref, back_ref, old_ref, rows_ref):
    rows_ref[...] = old_ref[...]

    def refill(i, _):
        rows_ref[pl.ds(evict_ref[i], 1), :] = back_ref[pl.ds(place_ref[i], 1), :]
        return 0

    lax.fori_loop(0, evict_ref.shape[0], refill, 0, unroll=8)


def updated(slot_ids, cache_rows, cache_accum, saved, params):
    cells = cache_rows.shape[0]
    vmem = pl.BlockSpec(memory_space=pltpu.VMEM)
    return pl.pallas_call(
        update_kernel,
        out_shape=(
            jax.ShapeDtypeStruct(cache_rows.shape, jnp.float32),
            jax.ShapeDtypeStruct((1, cells), jnp.float32),
        ),
        in_specs=[vmem] * 10,
        out_specs=(vmem, vmem),
        compiler_params=pltpu.CompilerParams(vmem_limit_bytes=60 * 1024 * 1024),
        cost_estimate=pl.CostEstimate(
            flops=1_100_000_000, bytes_accessed=4_000_000, transcendentals=1000
        ),
        name="update",
    )(slot_ids.T, cache_rows, cache_accum[None, :], *saved, *params)


def refilled(evict_slot, place, back, rows):
    smem = pl.BlockSpec(memory_space=pltpu.SMEM)
    vmem = pl.BlockSpec(memory_space=pltpu.VMEM)
    return pl.pallas_call(
        refill_kernel,
        out_shape=jax.ShapeDtypeStruct(rows.shape, jnp.float32),
        in_specs=[smem, smem, vmem, vmem],
        out_specs=vmem,
        compiler_params=pltpu.CompilerParams(vmem_limit_bytes=60 * 1024 * 1024),
        cost_estimate=pl.CostEstimate(flops=100_000, bytes_accessed=2_000_000, transcendentals=0),
        name="refill",
    )(evict_slot, place, back, rows)


def reply_kernel(
    me_ref,
    ids_ref,
    sums_ref,
    got_ref,
    table_any,
    accum_any,
    reply_ref,
    table_out,
    accum_out,
    table,
    accum,
    sems,
):
    owners, per = sums_ref.shape
    cap = per - 2
    width = got_ref.shape[1]
    step = table.shape[0] // 4
    loads = [pltpu.make_async_copy(accum_any, accum, sems.at[4])]
    stores = [pltpu.make_async_copy(accum, accum_out, sems.at[4])]
    for part in range(4):
        rows = pl.ds(part * step, step)
        loads.append(pltpu.make_async_copy(table_any.at[rows], table.at[rows], sems.at[part]))
        stores.append(pltpu.make_async_copy(table.at[rows], table_out.at[rows], sems.at[part]))
    for load in loads:
        load.start()
    for load in loads:
        load.wait()

    def store(s, _):
        for r in range(cap):
            row = ids_ref[s, per + r]

            @pl.when(row >= 0)
            def _():
                table[pl.ds(row, 1), :] = got_ref[pl.ds(s * per + r, 1), :]
                accum[row] = sums_ref[s, r]

        return 0

    lax.fori_loop(0, owners, store, 0, unroll=2)
    for copy in stores:
        copy.start()
    lane = lax.broadcasted_iota(jnp.int32, (1, width), 1)

    def answer(s, _):
        block = (s ^ me_ref[0]) * per
        meta = jnp.zeros((1, width), jnp.float32)
        for r in range(cap):
            row = ids_ref[s, 2 * per + r]
            reply_ref[pl.ds(block + r, 1), :] = table[pl.ds(row, 1), :]
            meta = jnp.where(lane == r, accum[row], meta)
        reply_ref[pl.ds(block + cap, 1), :] = jnp.zeros((1, width), jnp.float32)
        reply_ref[pl.ds(block + per - 1, 1), :] = meta
        return 0

    lax.fori_loop(0, owners, answer, 0, unroll=4)
    for copy in stores:
        copy.wait()


def replied(me, got, table_rows, table_accum):
    owners, per, width = got.shape
    smem = pl.BlockSpec(memory_space=pltpu.SMEM)
    vmem = pl.BlockSpec(memory_space=pltpu.VMEM)
    anywhere = pl.BlockSpec(memory_space=pl.ANY)
    meta = got[:, per - 1, : 3 * per]
    return pl.pallas_call(
        reply_kernel,
        out_shape=(
            jax.ShapeDtypeStruct((owners * per, width), jnp.float32),
            jax.ShapeDtypeStruct(table_rows.shape, jnp.float32),
            jax.ShapeDtypeStruct(table_accum.shape, jnp.float32),
        ),
        in_specs=[smem, smem, smem, vmem, anywhere, anywhere],
        out_specs=(vmem, anywhere, anywhere),
        scratch_shapes=[
            pltpu.VMEM(table_rows.shape, jnp.float32),
            pltpu.SMEM(table_accum.shape, jnp.float32),
            pltpu.SemaphoreType.DMA((5,)),
        ],
        compiler_params=pltpu.CompilerParams(vmem_limit_bytes=60 * 1024 * 1024),
        cost_estimate=pl.CostEstimate(flops=100_000, bytes_accessed=3_000_000, transcendentals=0),
        name="reply",
    )(
        me[None],
        meta.astype(jnp.int32),
        meta[:, :per],
        got.reshape(owners * per, width),
        table_rows,
        table_accum,
    )


def scaled(index, half, proj_ref, stage, out_sems):
    chunks, width = stage.shape[0], stage.shape[2]
    edge, rows = width // 2, width // 4
    squares = jnp.zeros((edge, edge), jnp.float32)
    for c in range(chunks):
        for q in range(4):
            block = half[4 * c + q, :edge, :]
            squares = squares + block * block
    total = jnp.sum(jnp.sum(squares, axis=0, keepdims=True), axis=1, keepdims=True)
    scale = lax.rsqrt(total / (chunks * width * width) + EPS)
    copies = []
    for c in range(chunks):
        for q in range(4):
            at = slice(q * rows, (q + 1) * rows)
            stage[c, at, :edge] = half[4 * c + q, :rows, :] * scale
            stage[c, at, edge:] = half[4 * c + q, rows:edge, :] * scale
        copies.append(
            pltpu.make_async_copy(
                stage.at[c], proj_ref.at[index, pl.ds(c * width, width), :], out_sems.at[c]
            )
        )
        copies[-1].start()
    return copies


def own_kernel(core_ref, half, proj_ref, stage, out_sems):
    for copy in scaled(core_ref[0], half, proj_ref, stage, out_sems):
        copy.wait()


def other_kernel(
    core_ref,
    proj_in,
    own_ref,
    half,
    proj_ref,
    vec_ref,
    loss_ref,
    stage,
    out_sems,
):
    core = core_ref[0]
    copies = scaled(1 - core, half, proj_ref, stage, out_sems)
    edge = half.shape[2]
    tiles = vec_ref.shape[1] // edge
    mine = core == 0
    own = [own_ref[2 * t, 0:1, :] for t in range(tiles)]
    far = [half[2 * t, edge : edge + 1, :] for t in range(tiles)]
    for index in (0, 1):
        rows = [jnp.where(mine, *((a, b) if index == 0 else (b, a))) for a, b in zip(own, far)]
        squares = sum(row * row for row in rows)
        total = jnp.sum(squares, axis=1, keepdims=True)
        scale = lax.rsqrt(total / (tiles * edge) + EPS)
        for t in range(tiles):
            vec_ref[index : index + 1, t * edge : (t + 1) * edge] = rows[t] * scale
    loss_ref[...] = jnp.where(mine, half[0, edge + 1 : edge + 2, :], own_ref[0, 1:2, :])
    for copy in copies:
        copy.wait()


def normalized(core, own, other):
    blocks, depth, edge = own.shape
    chunks, width = blocks // 4, 2 * edge
    wide = chunks * width
    smem = pl.BlockSpec(memory_space=pltpu.SMEM)
    vmem = pl.BlockSpec(memory_space=pltpu.VMEM)
    anywhere = pl.BlockSpec(memory_space=pl.ANY)
    scratch = [
        pltpu.VMEM((chunks, width, width), jnp.float32),
        pltpu.SemaphoreType.DMA((chunks,)),
    ]
    proj = jax.ShapeDtypeStruct((2, wide, width), jnp.float32)
    limit = pltpu.CompilerParams(vmem_limit_bytes=16 * 1024 * 1024)
    half = pl.pallas_call(
        own_kernel,
        out_shape=proj,
        in_specs=[smem, vmem],
        out_specs=anywhere,
        scratch_shapes=scratch,
        compiler_params=limit,
        name="scale_own",
    )(core[None], own)
    return pl.pallas_call(
        other_kernel,
        out_shape=(
            proj,
            jax.ShapeDtypeStruct((2, wide), jnp.float32),
            jax.ShapeDtypeStruct((1, 128), jnp.float32),
        ),
        in_specs=[smem, anywhere, vmem, vmem],
        out_specs=(anywhere, vmem, vmem),
        scratch_shapes=scratch,
        input_output_aliases={1: 0},
        compiler_params=limit,
        name="scale_other",
    )(core[None], half, own[:, edge:, :], other)


def shards(
    slot_ids,
    labels,
    cache_rows,
    cache_accum,
    table_rows,
    table_accum,
    miss_dest,
    evict_slot,
    evict_dest,
    proj_u,
    proj_v,
    cross_bias,
    head,
):
    owners = 32
    per = 8
    width = cache_rows.shape[1]
    cells = cache_rows.shape[0]
    spots = owners * per
    core = lax.axis_index("table") % 2

    me = lax.axis_index("table")
    sent = payload(
        evict_slot, evict_dest, miss_dest, cache_accum, cache_rows, owners, per
    ).reshape(owners, per, width)
    sent, slots_late = lax.optimization_barrier((sent, slot_ids))
    got = lax.all_to_all(sent, "table", split_axis=0, concat_axis=0, tiled=True)

    count = slot_ids.shape[0]
    feats = proj_u.shape[0] // width
    send, left, latent, dlatent, dlogit, extra = dense(
        core, slots_late, labels, cache_rows, proj_u, proj_v, cross_bias, head
    )

    send, got = lax.optimization_barrier((send, got))
    held = kept(core, left, latent, dlatent, extra) + swap_cores(send)
    held, got = lax.optimization_barrier((held, got))

    reply, table_new, accum_table = replied(me, got, table_rows, table_accum)
    back = reply.reshape(owners, per, width)

    held = exchange(held, plane_groups())
    back = cross(cross(back, 1), 8)
    rows_new, accum_new = updated(
        slot_ids,
        cache_rows,
        cache_accum,
        (latent, dlatent, dlogit),
        (proj_u, proj_v, cross_bias[None, :], head[None, :]),
    )
    held, back, rows_new, accum_new = lax.optimization_barrier(
        (held, back, rows_new, accum_new)
    )
    held = jnp.sum(held, axis=0)
    held = (held + shift_z(held, 4)) + (shift_z(held, 2) + shift_z(held, -2))
    back = cross(cross(back, 16), 2)
    held, back = lax.optimization_barrier((held, back))
    whole = jnp.broadcast_to(held[None], (4 * feats, *held.shape))
    whole = exchange(whole, plane_groups())
    back = cross(back, 4)
    in_place = (miss_dest[:, 0] ^ me) * per + ranks(miss_dest[:, 0])
    rows_new = refilled(evict_slot, in_place, back.reshape(spots, width), rows_new)
    fetched_accum = picked(back[:, per - 1, :per].reshape(-1), in_place)
    filled = evict_slot[:, None] == jnp.arange(cells, dtype=jnp.int32)[None, :]
    filled_sum = jnp.sum(jnp.where(filled, fetched_accum[:, None], 0.0), axis=0)
    accum_new = jnp.where(jnp.any(filled, axis=0), filled_sum, accum_new.reshape(cells))
    whole, rows_new, accum_new = lax.optimization_barrier((whole, rows_new, accum_new))
    clipped_proj, clipped_vecs, loss_row = normalized(core, whole, swap_cores(whole))
    loss = loss_row[0, 0] / (count * 256)
    return (rows_new, accum_new, table_new, accum_table, clipped_proj, clipped_vecs, loss)


def solution(mesh):
    split = P(AXES)
    rows = P(AXES, None)
    return jax.shard_map(
        shards,
        mesh=mesh,
        in_specs=(
            rows,
            split,
            rows,
            split,
            rows,
            split,
            rows,
            split,
            rows,
            P(),
            P(),
            P(),
            P(),
        ),
        out_specs=(rows, split, rows, split, P(), P(), P()),
        check_vma=False,
    )
```

```python
import jax
import jax.numpy as jnp
from jax import lax
from jax.experimental import pallas as pl
from jax.experimental.pallas import tpu as pltpu
from jax.sharding import PartitionSpec as P

EPS = 1e-06
ETA = 0.05
AXES = ("trainer", "table")


def device_at(y, x, z, core):
    return (((y // 2 * 4 + x) * 2 + y % 2) * 8 + z % 8) * 2 + core


def plane_groups():
    return [
        [device_at(y, x, 2 * pair + core + b, core) for y in range(4) for x in range(4) for b in (0, 1)]
        for core in range(2)
        for pair in range(4)
    ]


def shift_z(value, step):
    there = [
        (device_at(y, x, z, core), device_at(y, x, z + step, core))
        for y in range(4)
        for x in range(4)
        for z in range(8)
        for core in range(2)
    ]
    return lax.ppermute(value, AXES, there)


def swap_cores(value):
    return lax.ppermute(value, AXES, [(i, i ^ 1) for i in range(256)])


def exchange(value, groups):
    return lax.all_to_all(
        value, AXES, split_axis=0, concat_axis=0, tiled=True, axis_index_groups=groups
    )


def ranks(owner):
    listed = owner.shape[0]
    order = jnp.arange(listed, dtype=jnp.int32)
    earlier = (owner[:, None] == owner[None, :]) & (order[None, :] < order[:, None])
    return jnp.sum(earlier.astype(jnp.int32), axis=1)


def picked(values, index):
    hit = index[:, None] == jnp.arange(values.shape[0], dtype=jnp.int32)[None, :]
    return jnp.sum(jnp.where(hit, values[None, :], 0.0), axis=1)


def cross(value, bit):
    split = value.reshape(value.shape[0] // (2 * bit), 2, bit, *value.shape[1:])
    there = [(i, i ^ bit) for i in range(256)]
    came = lax.ppermute(split[:, 1], AXES, there)
    return jnp.stack([split[:, 0], came], axis=1).reshape(value.shape)


def put_blocks(ref, c, grad):
    half = grad.shape[1] // 2
    rows = grad.shape[0] // 4
    for q in range(4):
        part = grad[q * rows : (q + 1) * rows, :]
        ref[4 * c + q, :rows, :] = part[:, :half]
        ref[4 * c + q, rows : 2 * rows, :] = part[:, half:]


def dense_kernel(
    core_ref,
    slots_ref,
    labels_ref,
    cache_any,
    u_any,
    v_any,
    bias_ref,
    head_ref,
    send_out,
    left_out,
    latent_ref,
    dlatent_ref,
    dlogit_ref,
    extra_ref,
    cache,
    u_ref,
    v_ref,
    send_ref,
    left,
    high,
    mid,
    low,
    pooled,
    shifted,
    dlift,
    in_sems,
    out_sems,
):
    f32, bf16 = jnp.float32, jnp.bfloat16
    count, (cells, width) = slots_ref.shape[1], cache.shape
    feats = u_ref.shape[0] // width
    looks = slots_ref.shape[0] // feats
    cuts = [slice(c * width, (c + 1) * width) for c in range(feats)]
    loads = []
    for source, target in ((cache_any, cache), (v_any, v_ref), (u_any, u_ref)):
        step = target.shape[0] // 4
        for part in range(4):
            rows = pl.ds(part * step, step)
            loads.append(
                pltpu.make_async_copy(source.at[rows], target.at[rows], in_sems.at[len(loads)])
            )
            loads[-1].start()
    slots = jnp.transpose(slots_ref[...])
    lanes = 128
    lane = lax.broadcasted_iota(jnp.int32, (count, lanes), 1)
    one = jnp.ones((count, lanes), bf16)

    def counted(f):
        keys = []
        for at in range(f * looks, (f + 1) * looks):
            slot = slots[:, at : at + 1]
            key = jnp.where(lane == slot % lanes, slot // lanes, -1)
            keys.append(key.astype(f32).astype(bf16))
        tiles = []
        for tile in range(cells // lanes):
            this = jnp.full((count, lanes), tile, bf16)
            tiles.append(sum(jnp.where(key == this, one, 0 * one) for key in keys))
        return jnp.concatenate(tiles, axis=1)

    counts = counted(0)
    step = cells // 4
    for part in range(4):
        loads[part].wait()
        rows = cache[part * step : (part + 1) * step, :]
        first = rows.astype(bf16)
        rest = rows - first.astype(f32)
        second = rest.astype(bf16)
        high[part * step : (part + 1) * step, :] = first
        mid[part * step : (part + 1) * step, :] = second
        low[part * step : (part + 1) * step, :] = (rest - second.astype(f32)).astype(bf16)
    for f in range(feats):
        if f > 0:
            counts = counted(f)
        total = jnp.dot(counts, low[...], preferred_element_type=f32)
        total = total + jnp.dot(counts, mid[...], preferred_element_type=f32)
        total = total + jnp.dot(counts, high[...], preferred_element_type=f32)
        pooled[:, cuts[f]] = total.astype(bf16)

    for load in loads[4:]:
        load.wait()
    latent = jnp.dot(pooled[...], v_ref[...], preferred_element_type=f32).astype(bf16)
    latent_ref[...] = latent
    across = (((1,), (1,)), ((), ()))
    logit_wide = jnp.zeros((count, width), f32)
    for cut in cuts:
        moved = lax.dot_general(latent, u_ref[cut, :], across, preferred_element_type=f32)
        moved = moved + bias_ref[:, cut]
        shifted[:, cut] = moved
        part = pooled[:, cut].astype(f32)
        logit_wide = logit_wide + (part * moved + part) * head_ref[:, cut]
    logit = jnp.sum(logit_wide, axis=1, keepdims=True)
    target = jnp.transpose(labels_ref[...]).astype(f32)
    small = jnp.exp(-jnp.abs(logit))
    losses = jnp.maximum(logit, 0.0) + jnp.log1p(small) - target * logit
    loss = jnp.sum(losses, axis=0, keepdims=True)
    dlogit = jnp.where(logit >= 0, 1.0, small) / (1.0 + small) - target
    dlogit_ref[...] = jnp.transpose(dlogit)

    mine = core_ref[0] == 0
    half = width // 2
    lane1 = lax.broadcasted_iota(jnp.int32, (1, half), 1)
    loss_row = jnp.where(lane1 == 0, loss, 0.0)
    back = jnp.zeros((count, width), f32)
    for c, cut in enumerate(cuts):
        part = pooled[:, cut].astype(f32)
        lift = dlogit * head_ref[:, cut] * part
        crossed = part * shifted[:, cut] + part
        dbias = jnp.sum(lift, axis=0, keepdims=True)
        dhead = jnp.sum(dlogit * crossed, axis=0, keepdims=True)
        lift = lift.astype(bf16)
        dlift[:, cut] = lift
        back = back + jnp.dot(lift, u_ref[cut, :], preferred_element_type=f32)
        for ref, row in (
            (extra_ref, jnp.where(mine, dbias, dhead)),
            (send_ref, jnp.where(mine, dhead, dbias)),
        ):
            top = ref.shape[1] - 8
            for q in range(4):
                at = 4 * c + q
                ref[at, top : top + 8, :] = jnp.zeros((8, half), f32)
                ref[at, top + 1 : top + 2, :] = loss_row
                if q % 2 == 0:
                    ref[at, top : top + 1, :] = row[:, q // 2 * half : (q // 2 + 1) * half]
        left[:, cut] = jnp.where(mine, lift, pooled[:, cut])
    dlatent = back.astype(bf16)
    dlatent_ref[...] = dlatent
    copies = [pltpu.make_async_copy(left, left_out, out_sems.at[feats])]
    copies[0].start()
    right = jnp.where(mine, dlatent, latent)
    for c, cut in enumerate(cuts):
        grad = lax.dot_general(
            jnp.where(mine, pooled[:, cut], dlift[:, cut]),
            right,
            (((0,), (0,)), ((), ())),
            preferred_element_type=f32,
        )
        put_blocks(send_ref, c, grad)
        four = pl.ds(4 * c, 4)
        copies.append(
            pltpu.make_async_copy(send_ref.at[four], send_out.at[four], out_sems.at[c])
        )
        copies[-1].start()
    for copy in copies:
        copy.wait()


def dense(core, slot_ids, labels, cache_rows, proj_u, proj_v, cross_bias, head):
    count, (cells, width) = slot_ids.shape[0], cache_rows.shape
    wide = proj_u.shape[0]
    blocks = wide // width
    f32, bf16 = jnp.float32, jnp.bfloat16
    vmem = pl.BlockSpec(memory_space=pltpu.VMEM)
    anywhere = pl.BlockSpec(memory_space=pl.ANY)
    bundle = (4 * blocks, width // 2 + 8, width // 2)
    return pl.pallas_call(
        dense_kernel,
        out_shape=(
            jax.ShapeDtypeStruct(bundle, f32),
            jax.ShapeDtypeStruct((count, wide), bf16),
            jax.ShapeDtypeStruct((count, width), bf16),
            jax.ShapeDtypeStruct((count, width), bf16),
            jax.ShapeDtypeStruct((1, count), f32),
            jax.ShapeDtypeStruct((4 * blocks, 8, width // 2), f32),
        ),
        in_specs=[pl.BlockSpec(memory_space=pltpu.SMEM)]
        + [vmem] * 2
        + [anywhere] * 3
        + [vmem] * 2,
        out_specs=[anywhere] * 2 + [vmem] * 4,
        scratch_shapes=[
            pltpu.VMEM((cells, width), f32),
            pltpu.VMEM((wide, width), bf16),
            pltpu.VMEM((wide, width), bf16),
            pltpu.VMEM(bundle, f32),
            pltpu.VMEM((count, wide), bf16),
        ]
        + [pltpu.VMEM((cells, width), bf16)] * 3
        + [
            pltpu.VMEM((count, wide), bf16),
            pltpu.VMEM((count, wide), f32),
            pltpu.VMEM((count, wide), bf16),
            pltpu.SemaphoreType.DMA((12,)),
            pltpu.SemaphoreType.DMA((blocks + 1,)),
        ],
        compiler_params=pltpu.CompilerParams(vmem_limit_bytes=60 * 1024 * 1024),
        cost_estimate=pl.CostEstimate(
            flops=5_000_000_000, bytes_accessed=9_000_000, transcendentals=1000
        ),
        name="dense",
    )(
        core[None],
        slot_ids.T,
        labels[None, :],
        cache_rows,
        proj_u,
        proj_v,
        cross_bias[None, :],
        head[None, :],
    )


def keep_kernel(core_ref, left_ref, latent_ref, dlatent_ref, extra_ref, keep_ref):
    width = latent_ref.shape[1]
    right = jnp.where(core_ref[0] == 0, latent_ref[...], dlatent_ref[...])
    for c in range(keep_ref.shape[0] // 4):
        grad = lax.dot_general(
            left_ref[:, c * width : (c + 1) * width],
            right,
            (((0,), (0,)), ((), ())),
            preferred_element_type=jnp.float32,
        )
        put_blocks(keep_ref, c, grad)
    keep_ref[:, width // 2 :, :] = extra_ref[...]


def kept(core, left, latent, dlatent, extra):
    blocks, _, half = extra.shape
    vmem = pl.BlockSpec(memory_space=pltpu.VMEM)
    return pl.pallas_call(
        keep_kernel,
        out_shape=jax.ShapeDtypeStruct((blocks, half + 8, half), jnp.float32),
        in_specs=[pl.BlockSpec(memory_space=pltpu.SMEM)] + [vmem] * 4,
        out_specs=vmem,
        compiler_params=pltpu.CompilerParams(vmem_limit_bytes=16 * 1024 * 1024),
        cost_estimate=pl.CostEstimate(
            flops=300_000_000, bytes_accessed=4_000_000, transcendentals=0
        ),
        name="kept",
    )(core[None], left, latent, dlatent, extra)


def payload_kernel(
    slot_ref, evict_ref, miss_ref, accum_ref, cache_any, out_ref, taken, place, cache, sems
):
    owners, per = taken.shape[0], out_ref.shape[0] // taken.shape[0]
    width = out_ref.shape[1]
    listed = slot_ref.shape[0]
    step = cache.shape[0] // 4
    loads = []
    for part in range(4):
        rows = pl.ds(part * step, step)
        loads.append(pltpu.make_async_copy(cache_any.at[rows], cache.at[rows], sems.at[part]))
        loads[-1].start()
    lane = lax.broadcasted_iota(jnp.int32, (1, width), 1)
    base = jnp.where((lane >= per) & (lane < 2 * per), -1.0, 0.0)
    for o in range(owners):
        taken[o] = 0
        out_ref[o * per : o * per + per - 1, :] = jnp.zeros((per - 1, width), jnp.float32)
        out_ref[o * per + per - 1 : (o + 1) * per, :] = base

    def leave(i, _):
        owner = evict_ref[0, i]
        rank = taken[owner]
        taken[owner] = rank + 1
        place[i] = owner * per + rank
        spot = pl.ds(owner * per + per - 1, 1)
        meta = jnp.where(lane == rank, accum_ref[slot_ref[i]], out_ref[spot, :])
        row = evict_ref[1, i].astype(jnp.float32)
        out_ref[spot, :] = jnp.where(lane == per + rank, row, meta)
        return 0

    lax.fori_loop(0, listed, leave, 0, unroll=8)
    for o in range(owners):
        taken[o] = 0

    def ask(i, _):
        owner = miss_ref[0, i]
        rank = taken[owner]
        taken[owner] = rank + 1
        spot = pl.ds(owner * per + per - 1, 1)
        row = miss_ref[1, i].astype(jnp.float32)
        out_ref[spot, :] = jnp.where(lane == 2 * per + rank, row, out_ref[spot, :])
        return 0

    lax.fori_loop(0, listed, ask, 0, unroll=8)
    for load in loads:
        load.wait()

    def move(i, _):
        out_ref[pl.ds(place[i], 1), :] = cache[pl.ds(slot_ref[i], 1), :]
        return 0

    lax.fori_loop(0, listed, move, 0, unroll=8)


def payload(evict_slot, evict_dest, miss_dest, cache_accum, cache_rows, owners, per):
    smem = pl.BlockSpec(memory_space=pltpu.SMEM)
    return pl.pallas_call(
        payload_kernel,
        out_shape=jax.ShapeDtypeStruct((owners * per, cache_rows.shape[1]), jnp.float32),
        in_specs=[smem] * 4 + [pl.BlockSpec(memory_space=pl.ANY)],
        out_specs=pl.BlockSpec(memory_space=pltpu.VMEM),
        scratch_shapes=[
            pltpu.SMEM((owners,), jnp.int32),
            pltpu.SMEM(evict_slot.shape, jnp.int32),
            pltpu.VMEM(cache_rows.shape, jnp.float32),
            pltpu.SemaphoreType.DMA((4,)),
        ],
        compiler_params=pltpu.CompilerParams(vmem_limit_bytes=60 * 1024 * 1024),
        cost_estimate=pl.CostEstimate(flops=100_000, bytes_accessed=1_500_000, transcendentals=0),
        name="payload",
    )(evict_slot, evict_dest.T, miss_dest.T, cache_accum, cache_rows)


def add_kernel(keep_ref, came_ref, out_any, total, sems):
    chunks = sems.shape[0]
    size = keep_ref.shape[0] // chunks
    copies = []
    for c in range(chunks):
        part = pl.ds(c * size, size)
        total[part] = keep_ref[part] + came_ref[part]
        copies.append(pltpu.make_async_copy(total.at[part], out_any.at[part], sems.at[c]))
        copies[-1].start()
    for copy in copies:
        copy.wait()


def added(keep, came):
    vmem = pl.BlockSpec(memory_space=pltpu.VMEM)
    return pl.pallas_call(
        add_kernel,
        out_shape=jax.ShapeDtypeStruct(keep.shape, jnp.float32),
        in_specs=[vmem, vmem],
        out_specs=pl.BlockSpec(memory_space=pl.ANY),
        scratch_shapes=[pltpu.VMEM(keep.shape, jnp.float32), pltpu.SemaphoreType.DMA((8,))],
        compiler_params=pltpu.CompilerParams(vmem_limit_bytes=16 * 1024 * 1024),
        name="add_halves",
    )(keep, came)


def update_kernel(
    slots_ref,
    cache_ref,
    accum_ref,
    latent_ref,
    dlatent_ref,
    dlogit_ref,
    u_ref,
    v_ref,
    bias_ref,
    head_ref,
    rows_ref,
    accum_out,
):
    f32, bf16 = jnp.float32, jnp.bfloat16
    (cells, width), count = cache_ref.shape, latent_ref.shape[0]
    feats = u_ref.shape[0] // width
    looks = slots_ref.shape[0] // feats
    across = (((1,), (1,)), ((), ()))
    latent, dlatent = latent_ref[...], dlatent_ref[...]
    dlogit = jnp.transpose(dlogit_ref[...])
    cell = lax.broadcasted_iota(jnp.int32, (cells, count), 0)
    grad = jnp.zeros((cells, width), f32)
    for f in range(feats):
        counts = jnp.zeros((cells, count), f32)
        for look in range(looks):
            at = f * looks + look
            counts = counts + jnp.where(cell == slots_ref[at : at + 1, :], 1.0, 0.0)
        cut = slice(f * width, (f + 1) * width)
        moved = lax.dot_general(latent, u_ref[cut, :], across, preferred_element_type=f32)
        moved = moved + bias_ref[:, cut]
        through = lax.dot_general(dlatent, v_ref[cut, :], across, preferred_element_type=f32)
        dpooled = (dlogit * head_ref[:, cut] * (moved + 1.0) + through).astype(bf16)
        grad = grad + jnp.dot(counts.astype(bf16), dpooled, preferred_element_type=f32)
    mean = jnp.sum(grad * grad, axis=1, keepdims=True) / width
    accum = jnp.transpose(accum_ref[...]) + mean
    rows_ref[...] = cache_ref[...] - ETA * grad * lax.rsqrt(accum)
    accum_out[...] = jnp.transpose(accum)


def refill_kernel(evict_ref, place_ref, back_ref, old_ref, rows_ref):
    rows_ref[...] = old_ref[...]

    def refill(i, _):
        rows_ref[pl.ds(evict_ref[i], 1), :] = back_ref[pl.ds(place_ref[i], 1), :]
        return 0

    lax.fori_loop(0, evict_ref.shape[0], refill, 0, unroll=8)


def updated(slot_ids, cache_rows, cache_accum, saved, params):
    cells = cache_rows.shape[0]
    vmem = pl.BlockSpec(memory_space=pltpu.VMEM)
    return pl.pallas_call(
        update_kernel,
        out_shape=(
            jax.ShapeDtypeStruct(cache_rows.shape, jnp.float32),
            jax.ShapeDtypeStruct((1, cells), jnp.float32),
        ),
        in_specs=[vmem] * 10,
        out_specs=(vmem, vmem),
        compiler_params=pltpu.CompilerParams(vmem_limit_bytes=60 * 1024 * 1024),
        cost_estimate=pl.CostEstimate(
            flops=1_100_000_000, bytes_accessed=4_000_000, transcendentals=1000
        ),
        name="update",
    )(slot_ids.T, cache_rows, cache_accum[None, :], *saved, *params)


def refilled(evict_slot, place, back, rows):
    smem = pl.BlockSpec(memory_space=pltpu.SMEM)
    vmem = pl.BlockSpec(memory_space=pltpu.VMEM)
    return pl.pallas_call(
        refill_kernel,
        out_shape=jax.ShapeDtypeStruct(rows.shape, jnp.float32),
        in_specs=[smem, smem, vmem, vmem],
        out_specs=vmem,
        compiler_params=pltpu.CompilerParams(vmem_limit_bytes=60 * 1024 * 1024),
        cost_estimate=pl.CostEstimate(flops=100_000, bytes_accessed=2_000_000, transcendentals=0),
        name="refill",
    )(evict_slot, place, back, rows)


def reply_kernel(
    me_ref,
    ids_ref,
    sums_ref,
    got_ref,
    table_any,
    accum_any,
    reply_ref,
    table_out,
    accum_out,
    table,
    accum,
    sems,
):
    owners, per = sums_ref.shape
    cap = per - 2
    width = got_ref.shape[1]
    step = table.shape[0] // 4
    loads = [pltpu.make_async_copy(accum_any, accum, sems.at[4])]
    stores = [pltpu.make_async_copy(accum, accum_out, sems.at[4])]
    for part in range(4):
        rows = pl.ds(part * step, step)
        loads.append(pltpu.make_async_copy(table_any.at[rows], table.at[rows], sems.at[part]))
        stores.append(pltpu.make_async_copy(table.at[rows], table_out.at[rows], sems.at[part]))
    for load in loads:
        load.start()
    for load in loads:
        load.wait()

    def store(s, _):
        for r in range(cap):
            row = ids_ref[s, per + r]

            @pl.when(row >= 0)
            def _():
                table[pl.ds(row, 1), :] = got_ref[pl.ds(s * per + r, 1), :]
                accum[row] = sums_ref[s, r]

        return 0

    lax.fori_loop(0, owners, store, 0, unroll=2)
    for copy in stores:
        copy.start()
    lane = lax.broadcasted_iota(jnp.int32, (1, width), 1)

    def answer(s, _):
        block = (s ^ me_ref[0]) * per
        meta = jnp.zeros((1, width), jnp.float32)
        for r in range(cap):
            row = ids_ref[s, 2 * per + r]
            reply_ref[pl.ds(block + r, 1), :] = table[pl.ds(row, 1), :]
            meta = jnp.where(lane == r, accum[row], meta)
        reply_ref[pl.ds(block + cap, 1), :] = jnp.zeros((1, width), jnp.float32)
        reply_ref[pl.ds(block + per - 1, 1), :] = meta
        return 0

    lax.fori_loop(0, owners, answer, 0, unroll=4)
    for copy in stores:
        copy.wait()


def replied(me, got, table_rows, table_accum):
    owners, per, width = got.shape
    smem = pl.BlockSpec(memory_space=pltpu.SMEM)
    vmem = pl.BlockSpec(memory_space=pltpu.VMEM)
    anywhere = pl.BlockSpec(memory_space=pl.ANY)
    meta = got[:, per - 1, : 3 * per]
    return pl.pallas_call(
        reply_kernel,
        out_shape=(
            jax.ShapeDtypeStruct((owners * per, width), jnp.float32),
            jax.ShapeDtypeStruct(table_rows.shape, jnp.float32),
            jax.ShapeDtypeStruct(table_accum.shape, jnp.float32),
        ),
        in_specs=[smem, smem, smem, vmem, anywhere, anywhere],
        out_specs=(vmem, anywhere, anywhere),
        scratch_shapes=[
            pltpu.VMEM(table_rows.shape, jnp.float32),
            pltpu.SMEM(table_accum.shape, jnp.float32),
            pltpu.SemaphoreType.DMA((5,)),
        ],
        compiler_params=pltpu.CompilerParams(vmem_limit_bytes=60 * 1024 * 1024),
        cost_estimate=pl.CostEstimate(flops=100_000, bytes_accessed=3_000_000, transcendentals=0),
        name="reply",
    )(
        me[None],
        meta.astype(jnp.int32),
        meta[:, :per],
        got.reshape(owners * per, width),
        table_rows,
        table_accum,
    )


def scaled(index, half, proj_ref, stage, out_sems):
    chunks, width = stage.shape[0], stage.shape[2]
    edge, rows = width // 2, width // 4
    squares = jnp.zeros((edge, edge), jnp.float32)
    for c in range(chunks):
        for q in range(4):
            block = half[4 * c + q, :edge, :]
            squares = squares + block * block
    total = jnp.sum(jnp.sum(squares, axis=0, keepdims=True), axis=1, keepdims=True)
    scale = lax.rsqrt(total / (chunks * width * width) + EPS)
    copies = []
    for c in range(chunks):
        for q in range(4):
            at = slice(q * rows, (q + 1) * rows)
            stage[c, at, :edge] = half[4 * c + q, :rows, :] * scale
            stage[c, at, edge:] = half[4 * c + q, rows:edge, :] * scale
        copies.append(
            pltpu.make_async_copy(
                stage.at[c], proj_ref.at[index, pl.ds(c * width, width), :], out_sems.at[c]
            )
        )
        copies[-1].start()
    return copies


def own_kernel(core_ref, half, proj_ref, stage, out_sems):
    for copy in scaled(core_ref[0], half, proj_ref, stage, out_sems):
        copy.wait()


def other_kernel(
    core_ref,
    proj_in,
    own_ref,
    half,
    proj_ref,
    vec_ref,
    loss_ref,
    stage,
    out_sems,
):
    core = core_ref[0]
    copies = scaled(1 - core, half, proj_ref, stage, out_sems)
    edge = half.shape[2]
    tiles = vec_ref.shape[1] // edge
    mine = core == 0
    own = [own_ref[2 * t, 0:1, :] for t in range(tiles)]
    far = [half[2 * t, edge : edge + 1, :] for t in range(tiles)]
    for index in (0, 1):
        rows = [jnp.where(mine, *((a, b) if index == 0 else (b, a))) for a, b in zip(own, far)]
        squares = sum(row * row for row in rows)
        total = jnp.sum(squares, axis=1, keepdims=True)
        scale = lax.rsqrt(total / (tiles * edge) + EPS)
        for t in range(tiles):
            vec_ref[index : index + 1, t * edge : (t + 1) * edge] = rows[t] * scale
    loss_ref[...] = jnp.where(mine, half[0, edge + 1 : edge + 2, :], own_ref[0, 1:2, :])
    for copy in copies:
        copy.wait()


def normalized(core, own, other):
    blocks, depth, edge = own.shape
    chunks, width = blocks // 4, 2 * edge
    wide = chunks * width
    smem = pl.BlockSpec(memory_space=pltpu.SMEM)
    vmem = pl.BlockSpec(memory_space=pltpu.VMEM)
    anywhere = pl.BlockSpec(memory_space=pl.ANY)
    scratch = [
        pltpu.VMEM((chunks, width, width), jnp.float32),
        pltpu.SemaphoreType.DMA((chunks,)),
    ]
    proj = jax.ShapeDtypeStruct((2, wide, width), jnp.float32)
    limit = pltpu.CompilerParams(vmem_limit_bytes=16 * 1024 * 1024)
    half = pl.pallas_call(
        own_kernel,
        out_shape=proj,
        in_specs=[smem, vmem],
        out_specs=anywhere,
        scratch_shapes=scratch,
        compiler_params=limit,
        name="scale_own",
    )(core[None], own)
    return pl.pallas_call(
        other_kernel,
        out_shape=(
            proj,
            jax.ShapeDtypeStruct((2, wide), jnp.float32),
            jax.ShapeDtypeStruct((1, 128), jnp.float32),
        ),
        in_specs=[smem, anywhere, vmem, vmem],
        out_specs=(anywhere, vmem, vmem),
        scratch_shapes=scratch,
        input_output_aliases={1: 0},
        compiler_params=limit,
        name="scale_other",
    )(core[None], half, own[:, edge:, :], other)


def shards(
    slot_ids,
    labels,
    cache_rows,
    cache_accum,
    table_rows,
    table_accum,
    miss_dest,
    evict_slot,
    evict_dest,
    proj_u,
    proj_v,
    cross_bias,
    head,
):
    owners = 32
    per = 8
    width = cache_rows.shape[1]
    cells = cache_rows.shape[0]
    spots = owners * per
    core = lax.axis_index("table") % 2

    me = lax.axis_index("table")
    sent = payload(
        evict_slot, evict_dest, miss_dest, cache_accum, cache_rows, owners, per
    ).reshape(owners, per, width)
    sent, slots_late = lax.optimization_barrier((sent, slot_ids))
    got = lax.all_to_all(sent, "table", split_axis=0, concat_axis=0, tiled=True)

    count = slot_ids.shape[0]
    feats = proj_u.shape[0] // width
    send, left, latent, dlatent, dlogit, extra = dense(
        core, slots_late, labels, cache_rows, proj_u, proj_v, cross_bias, head
    )

    send, got = lax.optimization_barrier((send, got))
    held = added(kept(core, left, latent, dlatent, extra), swap_cores(send))
    held, got = lax.optimization_barrier((held, got))

    reply, table_new, accum_table = replied(me, got, table_rows, table_accum)
    back = reply.reshape(owners, per, width)

    held = exchange(held, plane_groups())
    back = cross(cross(back, 1), 8)
    rows_new, accum_new = updated(
        slot_ids,
        cache_rows,
        cache_accum,
        (latent, dlatent, dlogit),
        (proj_u, proj_v, cross_bias[None, :], head[None, :]),
    )
    held, back, rows_new, accum_new = lax.optimization_barrier(
        (held, back, rows_new, accum_new)
    )
    held = jnp.sum(held, axis=0)
    held = (held + shift_z(held, 4)) + (shift_z(held, 2) + shift_z(held, -2))
    back = cross(cross(back, 16), 4)
    held, back = lax.optimization_barrier((held, back))
    whole = jnp.broadcast_to(held[None], (4 * feats, *held.shape))
    whole = exchange(whole, plane_groups())
    back = cross(back, 2)
    in_place = (miss_dest[:, 0] ^ me) * per + ranks(miss_dest[:, 0])
    rows_new = refilled(evict_slot, in_place, back.reshape(spots, width), rows_new)
    fetched_accum = picked(back[:, per - 1, :per].reshape(-1), in_place)
    filled = evict_slot[:, None] == jnp.arange(cells, dtype=jnp.int32)[None, :]
    filled_sum = jnp.sum(jnp.where(filled, fetched_accum[:, None], 0.0), axis=0)
    accum_new = jnp.where(jnp.any(filled, axis=0), filled_sum, accum_new.reshape(cells))
    whole, rows_new, accum_new = lax.optimization_barrier((whole, rows_new, accum_new))
    clipped_proj, clipped_vecs, loss_row = normalized(core, whole, swap_cores(whole))
    loss = loss_row[0, 0] / (count * 256)
    return (rows_new, accum_new, table_new, accum_table, clipped_proj, clipped_vecs, loss)


def solution(mesh):
    split = P(AXES)
    rows = P(AXES, None)
    return jax.shard_map(
        shards,
        mesh=mesh,
        in_specs=(
            rows,
            split,
            rows,
            split,
            rows,
            split,
            rows,
            split,
            rows,
            P(),
            P(),
            P(),
            P(),
        ),
        out_specs=(rows, split, rows, split, P(), P(), P()),
        check_vma=False,
    )
```
